512 devices in a mesh: dp: 32 (over x, y), passage: 16 (over z, core).
Axes of the slice: x: 4, y: 8, z: 8, core: 2. Of those that a mesh axis runs over, the one named last changes fastest.
Arguments:
- hidden: bfloat16 [2048, 32, 768], P(('dp', 'passage')), may hold values from -6 to 6
- weight: bfloat16 [768, 128], P('passage'), may hold values from -0.21875 to 0.21875
- cache: bfloat16 [256, 180, 128], P('passage'), may hold values from -20 to 20
- lengths: int32 [256], P('passage'), may hold values from 8 to 180, as said below
- passage_ids: int32 [2048, 16], P(('dp', 'passage')), may hold values from 0 to 255, as said below
- owner_map: int32 [256], replicated, may hold values from 0 to 255, as said below
Outputs:
- hidden_grad: bfloat16 [2048, 32, 768], P(('dp', 'passage'))
- weight_grad: float32 [768, 128], P('passage')
- cache_grad: bfloat16 [256, 180, 128], P('passage')
The draws below stay inside these ranges and needn't reach their ends.
Inputs may be any that keep to these rules, and one draw needn't show every extreme that they name: `owner_map`: A permutation: each cache row belongs to exactly one passage id. Cache row r lies on index r // 16 of passage. `passage_ids`: among the 64 candidates of the queries of one device (aligned blocks of 4 queries), at most 12 have their cache row on any one index of passage; in every draw some index receives exactly 12 from each device of a group along passage. Ids may repeat within a query. `lengths`: cache row 0 has all 180 tokens live.
All inputs are finite; a program needn't handle non-finite values.
Results may differ from the reference program's by a relative error of at most 0.015.
The reference program's roundings to bfloat16 on the way count: a program that leaves them out, or rounds other values in their place, can miss the bound.
Values may be sent and summed in bfloat16 or wider, within the bound.
A program may use at most 64 MiB of HBM per device.

```python
import math
import jax
import jax.numpy as jnp
from jax import lax

D = 768
DIM = 128
QL = 32
PLEN = 180
CAND = 16
Q_DEV = 4
PASS_DEV = 16
CAP = 12
OWNERS = 16
QUERIES = 2048
PASSAGES = 256


def owner_table(key):
    return jax.random.permutation(key, PASSAGES).astype(jnp.int32)


def draw_owner_map(key, part):
    return owner_table(key)


def draw_passage_ids(key, part):
    table = owner_table(key)
    key = jax.random.fold_in(key, 2)
    inverse = jnp.argsort(table).astype(jnp.int32)
    blocks = QUERIES // Q_DEV
    pairs = Q_DEV * CAND
    group_key, block_key = jax.random.split(key)
    hot_owner = jax.random.randint(group_key, (blocks // OWNERS,), 0, OWNERS)
    hot_of_block = jnp.repeat(hot_owner, OWNERS)

    def one_block(bkey, hot_one):
        key_deck, key_order, key_first, key_second = jax.random.split(bkey, 4)
        others = (hot_one + 1 + jnp.arange(OWNERS - 1)) % OWNERS
        deck = jax.random.permutation(key_deck, jnp.repeat(others, CAP))[:pairs - CAP]
        owner_list = jnp.concatenate([jnp.full((CAP,), hot_one, jnp.int32), deck.astype(jnp.int32)])
        owner_list = jax.random.permutation(key_order, owner_list)
        first_slot = jax.random.randint(key_first, (pairs,), 0, PASS_DEV)
        second_slot = jax.random.randint(key_second, (pairs,), 0, PASS_DEV)
        return owner_list * PASS_DEV + jnp.minimum(first_slot, second_slot)
    rows = jax.vmap(one_block)(jax.random.split(block_key, blocks), hot_of_block)
    return inverse[rows.reshape(-1)].reshape(QUERIES, CAND).astype(jnp.int32)


def draw_lengths(key, part):
    key = jax.random.fold_in(key, 3)
    drawn = jax.random.randint(key, (PASSAGES,), 8, PLEN + 1).astype(jnp.int32)
    return drawn.at[0].set(PLEN)


def draw_cache(key, part):
    key = jax.random.fold_in(key, 4)
    key_base, key_scale = jax.random.split(key)
    base = jax.random.normal(key_base, (PASSAGES, PLEN, DIM), jnp.float32)
    row_scale = 0.3 * jax.random.uniform(key_scale, (PASSAGES, PLEN, 1), jnp.float32, 0.5, 1.5)
    return jnp.clip(base * row_scale, -20.0, 20.0).astype(jnp.bfloat16)


def shard_levels(stream_key, extent, pieces, least, high):
    loudness, own = 1.0, jax.random.fold_in(stream_key, 6)
    for axis_at, shards_of in pieces:
        draws = jnp.exp(jax.random.uniform(jax.random.fold_in(own, axis_at), (shards_of,), jnp.float32, least / len(pieces), high / len(pieces)))
        loudness = loudness * jnp.repeat(draws, extent[axis_at] // shards_of).reshape([-1 if axis == axis_at else 1 for axis in range(len(extent))])
    return loudness


def scatter_about(own_key, dims, spread, bound, shards=(), kind=jnp.bfloat16):
    level = shard_levels(own_key, dims, shards, -0.22, 0.18) if shards else 1.0
    values = jax.random.normal(own_key, dims, jnp.float32) * spread * level
    return jnp.minimum(jnp.maximum(values, -bound), bound).astype(kind)


def setup_inputs(seed: int = 0) -> dict:
    keys = jax.random.split(jax.random.key(seed), 7)
    hidden = scatter_about(keys[0], (QUERIES, QL, D), 1.0, 6.0, ((0, 512),))
    weight = scatter_about(keys[1], (D, DIM), D ** -0.5, 0.21875, ((0, 16),))
    cache = draw_cache(jax.random.fold_in(keys[6], 71), 0)
    lengths = draw_lengths(jax.random.fold_in(keys[6], 71), 0)
    passage_ids = draw_passage_ids(jax.random.fold_in(keys[6], 71), 0)
    owner_map = draw_owner_map(jax.random.fold_in(keys[6], 71), 0)
    return dict(hidden=hidden, weight=weight, cache=cache, lengths=lengths, passage_ids=passage_ids, owner_map=owner_map)


TAU = 0.1
EPS = 1e-06

def reference(hidden, weight, cache, lengths, passage_ids, owner_map):
    block = 64
    count = QUERIES // block
    similarity_scale = 1.0 / (TAU * math.sqrt(DIM))
    root_scale = 1.0 / math.sqrt(DIM)
    cache_rows = owner_map[passage_ids].astype(jnp.int32).reshape(count, block, CAND)
    hidden_blocks = hidden.reshape(count, block, QL, D)
    positions = jnp.arange(PLEN, dtype=jnp.int32)
    first_one = (jnp.arange(CAND) == 0).astype(jnp.float32)

    def step(carry, item):
        cache_acc, weight_acc = carry
        hidden_blk, rows_blk = item
        query_raw = jnp.dot(hidden_blk.reshape(block * QL, D), weight, preferred_element_type=jnp.float32).reshape(block, QL, DIM)
        inverse_rms = lax.rsqrt(lax.optimization_barrier(jnp.mean(query_raw * query_raw, axis=-1, keepdims=True)) + EPS)
        query_vectors = (query_raw * inverse_rms).astype(jnp.bfloat16)
        passage_tiles = cache[rows_blk]
        valid = positions[None, None, :] < lengths[rows_blk][:, :, None]
        similarity_values = jnp.einsum('hys,hfms->hfym', query_vectors.astype(jnp.float32), passage_tiles.astype(jnp.float32)) * similarity_scale
        masked = jnp.where(valid[:, :, None, :], similarity_values, -jnp.inf)
        row_top = lax.optimization_barrier(jnp.max(masked, axis=-1, keepdims=True))
        log_total = row_top[..., 0] + jnp.log(lax.optimization_barrier(jnp.sum(jnp.exp(masked - row_top), axis=-1)))
        scores = TAU * lax.optimization_barrier(jnp.sum(log_total, axis=-1))
        score_grad = jax.nn.softmax(scores, axis=-1) - first_one
        probs = jnp.exp(masked - log_total[..., None])
        weight_halfwidth = (score_grad[:, :, None, None] * probs * root_scale).astype(jnp.bfloat16)
        query_gradient = jnp.einsum('lhrt,lhtv->lrv', weight_halfwidth.astype(jnp.float32), passage_tiles.astype(jnp.float32))
        passage_tile_gradient = jnp.einsum('nukm,nkl->numl', weight_halfwidth.astype(jnp.float32), query_vectors.astype(jnp.float32))
        cache_acc = cache_acc.at[rows_blk.reshape(-1)].add(passage_tile_gradient.reshape(block * CAND, PLEN, DIM))
        mean_term = lax.optimization_barrier(jnp.mean(query_gradient * query_raw, axis=-1, keepdims=True))
        cube_rms = inverse_rms * inverse_rms * inverse_rms
        raw_grad = (inverse_rms * query_gradient - query_raw * cube_rms * mean_term).astype(jnp.bfloat16)
        hidden_grad = jnp.dot(raw_grad.reshape(block * QL, DIM), weight.T, preferred_element_type=jnp.float32).astype(jnp.bfloat16)
        weight_acc = weight_acc + jnp.dot(hidden_blk.reshape(block * QL, D).T, raw_grad.reshape(block * QL, DIM), preferred_element_type=jnp.float32)
        return ((cache_acc, weight_acc), hidden_grad.reshape(block, QL, D))
    init = (jnp.zeros((PASSAGES, PLEN, DIM), jnp.float32), jnp.zeros((D, DIM), jnp.float32))
    (cache_acc, weight_acc), hidden_grad = lax.scan(step, init, (hidden_blocks, cache_rows))
    return (hidden_grad.reshape(QUERIES, QL, D), weight_acc, cache_acc.astype(jnp.bfloat16))
```

```python
import functools
import math

import jax
import jax.numpy as jnp
from jax import lax
from jax.experimental import pallas as pl
from jax.experimental.pallas import tpu as pltpu
from jax.sharding import PartitionSpec as P

TAU = 0.1
EPS = 1e-06

NX, NY, NZ, NC = 4, 8, 8, 2
OWNERS = NZ * NC
Q_DEV, QL, CAND = 4, 32, 16
PASS_DEV, PLEN, ROWS = 16, 180, 192
DIM = 128
GROUPS = 60
SLOTS = 256
ENTRIES = 192
NEG = -1e30

F32, BF16, I32 = jnp.float32, jnp.bfloat16, jnp.int32


def dot(a, b):
    return jnp.dot(a, b, preferred_element_type=F32)


def dot_nt(a, b):
    return lax.dot_general(a, b, (((1,), (1,)), ((), ())), preferred_element_type=F32)


def dot_tn(a, b):
    return lax.dot_general(a, b, (((0,), (0,)), ((), ())), preferred_element_type=F32)


def iota(shape, axis):
    return lax.broadcasted_iota(I32, shape, axis)


def ind(cond, dtype=F32):
    return jnp.where(cond, 1.0, 0.0).astype(dtype)


def pieces(x):
    a = x.astype(BF16)
    rest = x - a.astype(F32)
    b = rest.astype(BF16)
    return (a, b, (rest - b.astype(F32)).astype(BF16))


class Place:
    def __init__(self):
        self.me = lax.axis_index("passage")
        self.z, self.c = self.me // NC, lax.rem(self.me, NC)
        self.sibling = self.z * NC + (1 - self.c)

    def ring(self, k):
        return lax.rem(self.z + k, NZ) * NC + self.c

    def ring_sibling(self, k):
        return lax.rem(self.z + k, NZ) * NC + (1 - self.c)


def remote(src, dst, send, recv, device):
    return pltpu.make_async_remote_copy(
        src_ref=src,
        dst_ref=dst,
        send_sem=send,
        recv_sem=recv,
        device_id=device,
        device_id_type=pl.DeviceIdType.MESH,
    )


def greet(devices):
    barrier = pltpu.get_barrier_semaphore()
    for device in devices:
        pl.semaphore_signal(
            barrier, inc=1, device_id=device, device_id_type=pl.DeviceIdType.MESH
        )
    pl.semaphore_wait(barrier, len(devices))


NEAR = (1, 7, 2, 6, 3, 5, 4)


class Gather:
    def __init__(self, place, buf, send, recv):
        self.place, self.buf, self.send, self.recv = place, buf, send, recv
        self.sent = []

    def copy(self, slot, n, peer):
        return remote(
            self.buf.at[slot], self.buf.at[slot], self.send.at[n], self.recv.at[slot],
            {"passage": peer},
        )

    def start(self):
        p = self.place
        for n, k in enumerate(NEAR):
            self.sent.append(self.copy(p.me, n, p.ring(k)))
            self.sent[-1].start()
        self.sent.append(self.copy(p.me, NZ - 1, p.sibling))
        self.sent[-1].start()

    def finish(self):
        p = self.place
        for n, k in enumerate(NEAR):
            forward = self.copy(p.ring(k), NZ + n, p.sibling)
            forward.wait_recv()
            forward.start()
            self.sent.append(forward)
        self.copy(p.sibling, 0, p.sibling).wait_recv()
        for k in NEAR:
            self.copy(p.ring_sibling(k), 0, p.sibling).wait_recv()
        for copy in self.sent:
            copy.wait_send()


def gather_sems():
    return [pltpu.SemaphoreType.DMA((2 * NZ - 1,)), pltpu.SemaphoreType.DMA((OWNERS,))]


def routing_tables(rows, me, tab_ref, hit_ref):
    rows_t = dot_nt(ind(iota((CAND, 128), 0) == iota((CAND, 128), 1), BF16), rows.astype(BF16))
    local = rows_t - (PASS_DEV * me).astype(F32)
    own = ind((local >= 0) & (local < PASS_DEV))
    hit = jnp.concatenate([ind(local == r) for r in range(PASS_DEV)], axis=0)
    lane_i, lane_j = iota((128, 128), 0), iota((128, 128), 1)
    upto = ind(lane_i <= lane_j, BF16)
    before = ind(lane_i < lane_j, BF16)
    ones = jnp.ones((128, 128), BF16)
    hit_bf = hit.astype(BF16)
    seen = dot(hit_bf, upto)
    total = dot(hit_bf, ones).astype(BF16)
    big_i, big_j = iota((256, 256), 0), iota((256, 256), 1)
    row_i, row_j = big_i // CAND, big_j // CAND
    ahead = dot(ind((row_i == row_j) & (big_j < big_i), BF16), total)
    number = dot(ind(row_i == row_j, BF16), total)
    groups = jnp.floor((number + 3.0) * 0.25)
    first = dot(
        ind((row_j < row_i) & (big_j == row_j * CAND), BF16), groups.astype(BF16)
    )
    rank = seen - 1.0 + ahead
    lap = jnp.floor(rank * 0.25)
    spot = 64.0 * (rank - 4.0 * lap) + first + lap
    place4 = 4.0 * (first + lap) + (rank - 4.0 * lap)

    def pick(values):
        out = jnp.zeros((CAND, 128), F32)
        for r in range(PASS_DEV):
            part = slice(r * CAND, (r + 1) * CAND)
            out = out + hit[part] * values[part]
        return out

    slot = jnp.where(own > 0, pick(spot), -1.0)
    place4 = pick(place4)
    cand = iota((CAND, 128), 0).astype(F32)
    code = CAND * cand + jnp.where(own > 0, local, 0.0)

    own_bf = own.astype(BF16)
    c_i, c_j = iota((CAND, CAND), 0), iota((CAND, CAND), 1)
    count = dot(jnp.ones((CAND, CAND), BF16), own_bf)
    earlier = dot(count.astype(BF16), before)
    entry = earlier + dot(ind(c_j < c_i, BF16), own_bf)
    entry = jnp.where(own > 0, entry, -1.0)
    last_entry = jnp.where(count > 0, earlier + count - 1.0, -1.0)

    lane = iota((8, 128), 1)
    query = ((lane // 8) * Q_DEV + lax.rem(lane, 8)).astype(F32).astype(BF16)
    one8 = jnp.ones((8, 128), BF16)
    qn, codes, valid, entry_place, entry_q = [], [], [], [], []
    for j in range(4):
        at = (iota((64, 128), 0) + 64 * j).astype(F32)
        acc = [jnp.zeros((64, 128), F32) for _ in range(4)]
        for c in range(CAND):
            one = ind(at == slot[c : c + 1])
            acc[0] = acc[0] + one
            acc[1] = acc[1] + one * code[c : c + 1]
            one = ind(at == entry[c : c + 1])
            acc[2] = acc[2] + one * place4[c : c + 1]
            acc[3] = acc[3] + one
        acc = [a.astype(BF16) for a in acc]
        hit_ref[64 * j : 64 * j + 64] = acc[0]
        qn.append(acc[0])
        codes.append(acc[1])
        entry_place.append(acc[2])
        entry_q.append(acc[3])
    at_slot = jnp.concatenate(qn, axis=0)
    qn = dot_nt(query, at_slot)
    valid = dot_nt(one8, at_slot)
    codes = dot_nt(one8, jnp.concatenate(codes, axis=0))
    entry_place = dot_nt(one8, jnp.concatenate(entry_place, axis=0))
    entry_q = dot_nt(query, jnp.concatenate(entry_q, axis=0))
    cands = jnp.floor(codes / CAND)
    row_of = codes - CAND * cands
    cands = jnp.where(valid > 0, cands, -1.0)

    last_group = jnp.where(number > 0, first + groups, 0.0)
    big = iota((256, 128), 0)
    diag = (big == iota((256, 128), 1) * CAND) & (iota((256, 128), 1) < PASS_DEV)
    last_row = dot(jnp.ones((8, 256), BF16), jnp.where(diag, last_group, 0.0).astype(BF16)) - 1.0
    pad = jnp.zeros((8, 128), F32)
    last_row = jnp.concatenate([last_row, pad], axis=1)
    last_entry = jnp.concatenate([last_entry[:8], pad], axis=1)

    sub = iota((8, SLOTS), 0)
    table = jnp.zeros((8, SLOTS), F32)
    rows_of_table = (qn, row_of, entry_place, entry_q, last_row, last_entry, cands)
    for n, values in enumerate(rows_of_table):
        table = jnp.where(sub == n, values, table)
    tab_ref[...] = table.astype(I32)


def gather_kernel(
    hidden_ref, weight_ref, ids_ref, map_ref,
    query_ref, full_ref, raw_ref, tab_ref, hit_ref,
    rows_buf, w_send, w_recv, r_send, r_recv, q_send, q_recv,
):
    place = Place()
    me = place.me
    full_ref[me] = weight_ref[...]
    near = [{"passage": place.ring(k)} for k in NEAR] + [{"passage": place.sibling}]
    greet(near)
    weights = Gather(place, full_ref, w_send, w_recv)
    weights.start()

    table = jnp.broadcast_to(map_ref[...].astype(F32), (8, 256)).astype(BF16)
    own = jnp.full((8, CAND), -1.0, F32)
    for q in range(Q_DEV):
        one = ind(iota((256, CAND), 0) == ids_ref[q : q + 1, :], BF16)
        own = jnp.where(iota((8, CAND), 0) == q, dot(table, one), own)
    rows_buf[me] = jnp.full((8, 128), -1.0, F32)
    rows_buf[me, :, 0:CAND] = own
    rows = Gather(place, rows_buf, r_send, r_recv)
    rows.start()

    weights.finish()
    raw = dot(hidden_ref[...], full_ref[...].reshape(-1, DIM))
    raw_ref[...] = raw
    inverse = lax.rsqrt(jnp.mean(raw * raw, axis=-1, keepdims=True) + EPS)
    query_ref[me] = (raw * inverse).astype(BF16)
    queries = Gather(place, query_ref, q_send, q_recv)
    queries.start()

    rows.finish()
    routing_tables(rows_buf[...].reshape(OWNERS * 8, 128), me, tab_ref, hit_ref)
    queries.finish()


def owner_kernel(
    cache_ref, len_ref, tab, tab_vec, hit_ref, query_ref,
    cg_ref, qg_ref,
    tiles, exps, logs, recips, scales, cg_run, qg_group, qg_run, score_buf, s_send, s_recv,
):
    place = Place()
    me = place.me
    others = [lax.rem(me + k, OWNERS) for k in range(1, OWNERS)]
    similarity_scale = 1.0 / (TAU * math.sqrt(DIM))
    root_scale = 1.0 / math.sqrt(DIM)

    for r in range(PASS_DEV):
        tiles[r, ROWS - 16 : ROWS] = jnp.zeros((16, DIM), BF16)
        tiles[r, 0:PLEN] = cache_ref[r]
    logs[...] = jnp.zeros_like(logs)
    recips[...] = jnp.zeros_like(recips)

    def load_queries(g):
        return jnp.concatenate([query_ref[tab[0, 64 * j + g]] for j in range(4)], axis=0)

    live = iota((ROWS, 128), 0)

    def forward(i, _):
        for u in range(4):
            g = 4 * i + u
            row = tab[1, g]
            sims = dot_nt(tiles[row], load_queries(g)) * similarity_scale
            sims = jnp.where(live < len_ref[row], sims, NEG)
            top = jnp.max(sims, axis=0, keepdims=True)
            e = jnp.exp(sims - top)
            total = jnp.sum(e, axis=0, keepdims=True)
            exps[g] = e
            logs[pl.ds(g, 1), :] = top + jnp.log(total)
            recips[pl.ds(g, 1), :] = 1.0 / total
        return 0

    lax.fori_loop(0, GROUPS // 4, forward, 0)

    of_place = iota((SLOTS, 128), 1) // QL == iota((SLOTS, 128), 0) // 64
    spread = jnp.where(of_place, jnp.concatenate([logs[...]] * 4, axis=0), 0.0)
    one8 = jnp.ones((8, 128), BF16)
    score_row = TAU * sum(dot_nt(one8, part) for part in pieces(spread))
    cands = tab_vec[6:7, :]
    is_cand = ind(iota((CAND, SLOTS), 0) == cands)
    hits = hit_ref[...]
    mine = sum(
        dot((is_cand * part[0:1].astype(F32)).astype(BF16), hits) for part in pieces(score_row)
    )
    score_buf[me] = mine[0:8] + pltpu.roll(mine[8:16], 4, 1)

    greet([{"passage": d} for d in others])
    copies = []
    for n, d in enumerate(others):
        copies.append(
            remote(score_buf.at[me], score_buf.at[me], s_send.at[n], s_recv.at[me], {"passage": d})
        )
        copies[-1].start()
    for d in others:
        remote(score_buf.at[d], score_buf.at[d], s_send.at[0], s_recv.at[d], {"passage": d}).wait_recv()
    for copy in copies:
        copy.wait_send()
    scores = score_buf[0]
    for d in range(1, OWNERS):
        scores = scores + score_buf[d]

    lane = iota((8, 128), 1)
    low = lax.rem(lane, 8) < Q_DEV

    def both(x, op):
        return op(x, jnp.where(low, pltpu.roll(x, 124, 1), pltpu.roll(x, 4, 1)))

    top = both(jnp.broadcast_to(jnp.max(scores, axis=0, keepdims=True), (8, 128)), jnp.maximum)
    e = jnp.exp(scores - top)
    total = both(jnp.broadcast_to(jnp.sum(e, axis=0, keepdims=True), (8, 128)), jnp.add)
    grad = e / total - ind((iota((8, 128), 0) == 0) & low)
    grad = jnp.concatenate(
        [jnp.where(low, grad, 0.0), jnp.where(low, pltpu.roll(grad, 124, 1), 0.0)], axis=0
    )
    at_slot = is_cand * sum(dot_nt(part, hits) for part in pieces(grad))
    at_slot = jnp.sum(at_slot, axis=0, keepdims=True)
    same_group = ind(lax.rem(iota((64, SLOTS), 1), 64) == iota((64, SLOTS), 0))
    to_lanes = ind(of_place, BF16)
    by_lane = sum(dot(part, to_lanes) for part in pieces(same_group * at_slot))
    scales[...] = by_lane * recips[...] * root_scale

    def backward(i, _):
        for u in range(4):
            g = 4 * i + u
            row = tab[1, g]
            w = (exps[g] * scales[pl.ds(g, 1), :]).astype(BF16)
            again = (row == tab[1, jnp.maximum(g - 1, 0)]) & (g > 0)
            cg_run[g + 1] = jnp.where(again, cg_run[g], 0.0) + dot(w, load_queries(g))
            qg_group[g] = dot_tn(w, tiles[row]).reshape(4, QL, DIM)
        return 0

    lax.fori_loop(0, GROUPS // 4, backward, 0)

    def finish_row(r, _):
        last = tab[4, r]
        cg_ref[r] = jnp.where(last >= 0, cg_run[jnp.maximum(last, 0) + 1], 0.0).astype(BF16)
        return 0

    lax.fori_loop(0, PASS_DEV, finish_row, 0)

    def entry_step(i, _):
        for u in range(4):
            e = 4 * i + u
            at = tab[2, e]
            again = (tab[3, e] == tab[3, jnp.maximum(e - 1, 0)]) & (e > 0)
            part = qg_group[at // 4, lax.rem(at, 4)]
            qg_run[e + 1] = jnp.where(again, qg_run[e], 0.0) + part
        return 0

    lax.fori_loop(0, ENTRIES // 4, entry_step, 0)

    def finish_query(q, _):
        last = tab[5, (q // Q_DEV) * 8 + lax.rem(q, Q_DEV)]
        qg_ref[q] = jnp.where(last >= 0, qg_run[jnp.maximum(last, 0) + 1], 0.0).astype(BF16)
        return 0

    lax.fori_loop(0, OWNERS * Q_DEV, finish_query, 0)


class Ring:
    def __init__(self, n, at, device, rows, cut, send, recv):
        self.n, self.at, self.device = n, at, device
        self.rows, self.cut, self.half = rows, cut, n // 2
        self.send, self.recv = send, recv

    def peer(self, k):
        return lax.rem(self.at + k + self.n, self.n)

    def span(self, base, t, part=None):
        lo, hi = 0, self.rows
        if part == 0:
            hi = self.cut
        if part == 1:
            lo = self.cut
        return pl.ds(pl.multiple_of(base + t * self.rows + lo, 16), hi - lo)

    def copy(self, src, dst, way, step):
        toward = self.device(self.peer(1 if way == 0 else -1))
        return remote(src, dst, self.send.at[way, step - 1], self.recv.at[way, step - 1], toward)


class Scatter(Ring):
    def bind(self, src, base, arrive):
        self.src, self.base, self.arrive = src, base, arrive
        return self

    def part(self, way):
        return slice(0, self.cut) if way == 0 else slice(self.cut, self.rows)

    def make(self, step, way):
        if step == 1:
            t = self.peer(self.half)
            src = self.src.at[self.span(self.base, t, way), :]
            dst = self.arrive.at[way, 0, self.part(way)]
        else:
            src = self.arrive.at[way, step - 2]
            dst = self.arrive.at[way, step - 1]
        return self.copy(src, dst, way, step)

    def start(self, step):
        for way in (0, 1):
            self.make(step, way).start()

    def finish(self, step):
        for way in (0, 1):
            self.make(step, way).wait_recv()
            if step == self.half:
                continue
            t = self.peer((self.half - step) * (1 if way == 0 else -1))
            own = self.src[self.span(self.base, t), :]
            if step == 1:
                part = self.part(way)
                for rows in (slice(0, self.cut), slice(self.cut, self.rows)):
                    mine = own[rows]
                    if rows == part:
                        mine = (mine.astype(F32) + self.arrive[way, 0, rows].astype(F32)).astype(BF16)
                    if step > 1 or rows != part:
                        self.arrive[way, 0, rows] = mine
                    else:
                        self.arrive[way, 0, rows] = mine
            else:
                both = own.astype(F32) + self.arrive[way, step - 1].astype(F32)
                self.arrive[way, step - 1] = both.astype(BF16)

    def result(self):
        own = self.src[self.span(self.base, self.at), :].astype(F32)
        return own + self.arrive[0, self.half - 1].astype(F32) + self.arrive[1, self.half - 1].astype(F32)

    def drain(self):
        for step in range(1, self.half + 1):
            for way in (0, 1):
                self.make(step, way).wait_send()


class Spread(Ring):
    def bind(self, buf, base):
        self.buf, self.base = buf, base
        return self

    def make(self, step, way, arriving=False):
        t = self.peer((step if arriving else step - 1) * (-1 if way == 0 else 1))
        span = self.span(self.base, t, way if step == self.half else None)
        return self.copy(self.buf.at[span, :], self.buf.at[span, :], way, step)

    def start(self, step):
        for way in (0, 1):
            self.make(step, way).start()

    def finish(self, step):
        for way in (0, 1):
            self.make(step, way, arriving=True).wait_recv()

    def drain(self):
        for step in range(1, self.half + 1):
            for way in (0, 1):
                self.make(step, way).wait_send()


class Swap:
    def __init__(self, n, at, device, send, recv):
        self.n, self.at, self.device, self.send, self.recv = n, at, device, send, recv

    def start(self, src_of, buf):
        self.buf, self.copies = buf, []
        for k in range(1, self.n):
            t = lax.rem(self.at + k, self.n)
            copy = remote(
                src_of(t), buf.at[self.at], self.send.at[k - 1], self.recv.at[self.at], self.device(t)
            )
            copy.start()
            self.copies.append(copy)

    def finish(self):
        for k in range(1, self.n):
            t = lax.rem(self.at + k, self.n)
            remote(
                self.buf.at[t], self.buf.at[t], self.send.at[0], self.recv.at[t], self.device(t)
            ).wait_recv()

    def drain(self):
        for copy in self.copies:
            copy.wait_send()


HALF_ROWS = PASS_DEV * ROWS // 2
AX, BY = HALF_ROWS // NX, HALF_ROWS // NY
SUB = HALF_ROWS // (NX * NY)


def sum_kernel(
    cg_ref, qg_ref, hidden_ref, full_ref, raw_ref,
    hid_ref, wg_ref, cache_ref,
    ax_buf, ay_buf, by_buf, bx_buf, mid_a, mid_b, fin, q_sib, q_out, q_in,
    w_own, w_sib, w_out, w_in, w_x, w_y,
    *sems,
):
    place = Place()
    me, z, c = place.me, place.z, place.c
    dp = lax.axis_index("dp")
    ix, iy = dp // NY, lax.rem(dp, NY)
    sems = list(sems)

    def take():
        return sems.pop(0), sems.pop(0)

    on_x = lambda t: {"dp": t * NY + iy}
    on_y = lambda t: {"dp": ix * NY + t}
    on_z = lambda t: {"passage": t * NC + c}
    sibling = {"passage": place.sibling}
    greet(
        [sibling]
        + [on_z(lax.rem(z + k, NZ)) for k in range(1, NZ)]
        + [on_x(lax.rem(ix + k, NX)) for k in range(1, NX)]
        + [on_y(lax.rem(iy + k, NY)) for k in range(1, NY)]
    )

    a1 = Scatter(NX, ix, on_x, AX, AX // 2, *take()).bind(cg_ref, 0, ax_buf)
    b1 = Scatter(NY, iy, on_y, BY, BY // 2, *take()).bind(cg_ref, HALF_ROWS, by_buf)
    a2 = Scatter(NY, iy, on_y, SUB, 32, *take()).bind(mid_a, 0, ay_buf)
    b2 = Scatter(NX, ix, on_x, SUB, 32, *take()).bind(mid_b, 0, bx_buf)
    a3 = Spread(NY, iy, on_y, SUB, 32, *take()).bind(fin, ix * AX)
    b3 = Spread(NX, ix, on_x, SUB, 32, *take()).bind(fin, HALF_ROWS + iy * BY)
    a4 = Spread(NX, ix, on_x, AX, AX // 2, *take()).bind(fin, 0)
    b4 = Spread(NY, iy, on_y, BY, BY // 2, *take()).bind(fin, HALF_ROWS)
    q_swap = Swap(NZ, z, on_z, *take())
    w_swap = Swap(NZ, z, on_z, *take())
    x_swap = Swap(NX, ix, on_x, *take())
    y_swap = Swap(NY, iy, on_y, *take())
    qs_send, qs_recv = take()
    ws_send, ws_recv = take()

    q_pair = remote(qg_ref.at[:, 1 - c], q_sib, qs_send, qs_recv, sibling)
    q_pair.start()
    a1.start(1)
    b1.start(1)
    q_pair.wait_recv()
    for t in range(NZ):
        q_out[t] = (qg_ref[t, c].astype(F32) + q_sib[t].astype(F32)).astype(BF16)
    q_swap.start(lambda t: q_out.at[t], q_in)

    a1.finish(1)
    a1.start(2)
    b1.finish(1)
    b1.start(2)
    b1.finish(2)
    b1.start(3)
    a1.finish(2)
    mid_a[...] = a1.result().astype(BF16)
    a2.start(1)
    b1.finish(3)
    b1.start(4)

    q_swap.finish()
    query_gradient = q_out[z].astype(F32)
    for k in range(1, NZ):
        query_gradient = query_gradient + q_in[lax.rem(z + k, NZ)].astype(F32)
    raw = raw_ref[...]
    inverse = lax.rsqrt(jnp.mean(raw * raw, axis=-1, keepdims=True) + EPS)
    mean_term = jnp.mean(query_gradient * raw, axis=-1, keepdims=True)
    raw_grad = (
        inverse * query_gradient - raw * (inverse * inverse * inverse) * mean_term
    ).astype(BF16)
    weight_part = dot_tn(hidden_ref[...], raw_grad)
    w_own[...] = weight_part.astype(BF16).reshape(w_own.shape)
    w_pair = remote(w_own.at[:, 1 - c], w_sib, ws_send, ws_recv, sibling)
    w_pair.start()

    a2.finish(1)
    a2.start(2)
    b1.finish(4)
    mid_b[...] = b1.result().astype(BF16)
    b2.start(1)
    hid_ref[...] = dot_nt(raw_grad, full_ref[...].reshape(-1, DIM)).astype(BF16)
    w_pair.wait_recv()
    for t in range(NZ):
        w_out[t] = (w_own[t, c].astype(F32) + w_sib[t].astype(F32)).astype(BF16)
    w_swap.start(lambda t: w_out.at[t], w_in)

    a2.finish(2)
    a2.start(3)
    b2.finish(1)
    b2.start(2)
    a2.finish(3)
    a2.start(4)
    b2.finish(2)
    fin[b3.span(b3.base, ix), :] = b2.result().astype(BF16)
    b3.start(1)
    a2.finish(4)
    fin[a3.span(a3.base, iy), :] = a2.result().astype(BF16)
    a3.start(1)

    w_swap.finish()
    total = w_out[z].astype(F32)
    for k in range(1, NZ):
        total = total + w_in[lax.rem(z + k, NZ)].astype(F32)
    w_x[ix] = total.astype(BF16)
    x_swap.start(lambda t: w_x.at[ix], w_x)

    b3.finish(1)
    b3.start(2)
    a3.finish(1)
    a3.start(2)
    b3.finish(2)
    b4.start(1)
    a3.finish(2)
    a3.start(3)
    b4.finish(1)
    b4.start(2)

    x_swap.finish()
    total = w_x[0].astype(F32)
    for t in range(1, NX):
        total = total + w_x[t].astype(F32)
    w_y[iy] = total.astype(BF16)
    y_swap.start(lambda t: w_y.at[iy], w_y)

    a3.finish(3)
    a3.start(4)
    b4.finish(2)
    b4.start(3)
    a3.finish(4)
    a4.start(1)
    b4.finish(3)
    b4.start(4)
    a4.finish(1)
    a4.start(2)

    y_swap.finish()
    total = w_y[0].astype(F32)
    for t in range(1, NY):
        total = total + w_y[t].astype(F32)
    wg_ref[...] = total

    b4.finish(4)
    for r in range(PASS_DEV // 2, PASS_DEV):
        cache_ref[r] = fin[r * ROWS : (r + 1) * ROWS, :][0:PLEN]
    a4.finish(2)
    for r in range(PASS_DEV // 2):
        cache_ref[r] = fin[r * ROWS : (r + 1) * ROWS, :][0:PLEN]

    q_pair.wait_send()
    w_pair.wait_send()
    for moved in (a1, b1, a2, b2, a3, b3, a4, b4, q_swap, w_swap, x_swap, y_swap):
        moved.drain()


def call(kernel, collective_id, out_shape, in_specs, scratch, args):
    return pl.pallas_call(
        kernel,
        out_shape=out_shape,
        in_specs=in_specs,
        out_specs=[VMEM] * len(out_shape),
        scratch_shapes=scratch,
        compiler_params=pltpu.CompilerParams(
            collective_id=collective_id, has_side_effects=True, vmem_limit_bytes=56 * 2**20
        ),
    )(*args)


VMEM = pl.BlockSpec(memory_space=pltpu.VMEM)
SMEM = pl.BlockSpec(memory_space=pltpu.SMEM)


def shards(hidden, weight, cache, lengths, passage_ids, owner_map):
    width = hidden.shape[-1]
    share = width // OWNERS
    tokens = Q_DEV * QL
    shape = jax.ShapeDtypeStruct
    dma = pltpu.SemaphoreType.DMA
    hidden = hidden.reshape(tokens, width)
    queries, full, raw, tab, hits = call(
        gather_kernel,
        0,
        [
            shape((OWNERS, tokens, DIM), BF16),
            shape((OWNERS, share, DIM), BF16),
            shape((tokens, DIM), F32),
            shape((8, SLOTS), I32),
            shape((SLOTS, 128), BF16),
        ],
        [VMEM] * 4,
        [pltpu.VMEM((OWNERS, 8, 128), F32)] + gather_sems() + gather_sems() + gather_sems(),
        (hidden, weight, passage_ids, owner_map.reshape(1, -1)),
    )
    cg, qg = call(
        owner_kernel,
        1,
        [
            shape((PASS_DEV, ROWS, DIM), BF16),
            shape((OWNERS * Q_DEV, QL, DIM), BF16),
        ],
        [VMEM, SMEM, SMEM, VMEM, VMEM, VMEM],
        [
            pltpu.VMEM((PASS_DEV, ROWS, DIM), BF16),
            pltpu.VMEM((GROUPS, ROWS, 128), F32),
            pltpu.VMEM((64, 128), F32),
            pltpu.VMEM((64, 128), F32),
            pltpu.VMEM((64, 128), F32),
            pltpu.VMEM((GROUPS + 1, ROWS, DIM), F32),
            pltpu.VMEM((GROUPS, 4, QL, DIM), F32),
            pltpu.VMEM((ENTRIES + 1, QL, DIM), F32),
            pltpu.VMEM((OWNERS, 8, 128), F32),
            dma((OWNERS - 1,)),
            dma((OWNERS,)),
        ],
        (cache, lengths, tab, tab, hits, queries.reshape(OWNERS * Q_DEV, QL, DIM)),
    )

    def ring(n):
        return [dma((2, n // 2)), dma((2, n // 2))]

    def swap(n):
        return [dma((n - 1,)), dma((n,))]

    sems = ring(NX) + ring(NY) + ring(NY) + ring(NX) + ring(NY) + ring(NX) + ring(NX) + ring(NY)
    sems += swap(NZ) + swap(NZ) + swap(NX) + swap(NY) + [dma, dma, dma, dma]
    hid, wg, cache_grad = call(
        sum_kernel,
        2,
        [
            shape((tokens, width), BF16),
            shape((share, DIM), F32),
            shape((PASS_DEV, PLEN, DIM), BF16),
        ],
        [VMEM] * 5,
        [
            pltpu.VMEM((2, NX // 2, AX, DIM), BF16),
            pltpu.VMEM((2, NY // 2, SUB, DIM), BF16),
            pltpu.VMEM((2, NY // 2, BY, DIM), BF16),
            pltpu.VMEM((2, NX // 2, SUB, DIM), BF16),
            pltpu.VMEM((AX, DIM), BF16),
            pltpu.VMEM((BY, DIM), BF16),
            pltpu.VMEM((PASS_DEV * ROWS, DIM), BF16),
            pltpu.VMEM((NZ, tokens, DIM), BF16),
            pltpu.VMEM((NZ, tokens, DIM), BF16),
            pltpu.VMEM((NZ, tokens, DIM), BF16),
            pltpu.VMEM((NZ, NC, share, DIM), BF16),
            pltpu.VMEM((NZ, share, DIM), BF16),
            pltpu.VMEM((NZ, share, DIM), BF16),
            pltpu.VMEM((NZ, share, DIM), BF16),
            pltpu.VMEM((NX, share, DIM), BF16),
            pltpu.VMEM((NY, share, DIM), BF16),
        ]
        + sems,
        (
            cg.reshape(PASS_DEV * ROWS, DIM),
            qg.reshape(NZ, NC, tokens, DIM),
            hidden,
            full,
            raw,
        ),
    )
    return hid.reshape(Q_DEV, QL, width), wg, cache_grad


def solution(mesh):
    in_specs = (
        P(("dp", "passage"), None, None),
        P("passage", None),
        P("passage", None, None),
        P("passage"),
        P(("dp", "passage"), None),
        P(),
    )
    out_specs = (P(("dp", "passage"), None, None), P("passage", None), P("passage", None, None))
    return jax.shard_map(shards, mesh=mesh, in_specs=in_specs, out_specs=out_specs, check_vma=False)
```

```python
import functools
import math

import jax
import jax.numpy as jnp
from jax import lax
from jax.experimental import pallas as pl
from jax.experimental.pallas import tpu as pltpu
from jax.sharding import PartitionSpec as P

TAU = 0.1
EPS = 1e-06

NX, NY, NZ, NC = 4, 8, 8, 2
OWNERS = NZ * NC
Q_DEV, QL, CAND = 4, 32, 16
PASS_DEV, PLEN, ROWS = 16, 180, 192
DIM = 128
GROUPS = 60
SLOTS = 256
ENTRIES = 192
NEG = -1e30

F32, BF16, I32 = jnp.float32, jnp.bfloat16, jnp.int32


def dot(a, b):
    return jnp.dot(a, b, preferred_element_type=F32)


def dot_nt(a, b):
    return lax.dot_general(a, b, (((1,), (1,)), ((), ())), preferred_element_type=F32)


def dot_tn(a, b):
    return lax.dot_general(a, b, (((0,), (0,)), ((), ())), preferred_element_type=F32)


def iota(shape, axis):
    return lax.broadcasted_iota(I32, shape, axis)


def ind(cond, dtype=F32):
    return jnp.where(cond, 1.0, 0.0).astype(dtype)


def pieces(x):
    a = x.astype(BF16)
    rest = x - a.astype(F32)
    b = rest.astype(BF16)
    return (a, b, (rest - b.astype(F32)).astype(BF16))


class Place:
    def __init__(self):
        self.me = lax.axis_index("passage")
        self.z, self.c = self.me // NC, lax.rem(self.me, NC)
        self.sibling = self.z * NC + (1 - self.c)

    def ring(self, k):
        return lax.rem(self.z + k, NZ) * NC + self.c

    def ring_sibling(self, k):
        return lax.rem(self.z + k, NZ) * NC + (1 - self.c)


def remote(src, dst, send, recv, device):
    return pltpu.make_async_remote_copy(
        src_ref=src,
        dst_ref=dst,
        send_sem=send,
        recv_sem=recv,
        device_id=device,
        device_id_type=pl.DeviceIdType.MESH,
    )


NEAR = (1, 7, 2, 6, 3, 5, 4)


class Gather:
    def __init__(self, place, buf, send, recv):
        self.place, self.buf, self.send, self.recv = place, buf, send, recv
        self.sent = []

    def copy(self, slot, n, peer):
        return remote(
            self.buf.at[slot], self.buf.at[slot], self.send.at[n], self.recv.at[slot],
            {"passage": peer},
        )

    def start(self):
        p = self.place
        for n, k in enumerate(NEAR):
            self.sent.append(self.copy(p.me, n, p.ring(k)))
            self.sent[-1].start()
        self.sent.append(self.copy(p.me, NZ - 1, p.sibling))
        self.sent[-1].start()

    def finish(self):
        p = self.place
        for n, k in enumerate(NEAR):
            forward = self.copy(p.ring(k), NZ + n, p.sibling)
            forward.wait_recv()
            forward.start()
            self.sent.append(forward)
        self.copy(p.sibling, 0, p.sibling).wait_recv()
        for k in NEAR:
            self.copy(p.ring_sibling(k), 0, p.sibling).wait_recv()
        for copy in self.sent:
            copy.wait_send()


def routing_tables(rows, me, tab_ref, hit_ref):
    rows_t = dot_nt(ind(iota((CAND, 128), 0) == iota((CAND, 128), 1), BF16), rows.astype(BF16))
    local = rows_t - (PASS_DEV * me).astype(F32)
    own = ind((local >= 0) & (local < PASS_DEV))
    hit = jnp.concatenate([ind(local == r) for r in range(PASS_DEV)], axis=0)
    lane_i, lane_j = iota((128, 128), 0), iota((128, 128), 1)
    upto = ind(lane_i <= lane_j, BF16)
    before = ind(lane_i < lane_j, BF16)
    ones = jnp.ones((128, 128), BF16)
    hit_bf = hit.astype(BF16)
    seen = dot(hit_bf, upto)
    total = dot(hit_bf, ones).astype(BF16)
    big_i, big_j = iota((256, 256), 0), iota((256, 256), 1)
    row_i, row_j = big_i // CAND, big_j // CAND
    ahead = dot(ind((row_i == row_j) & (big_j < big_i), BF16), total)
    number = dot(ind(row_i == row_j, BF16), total)
    groups = jnp.floor((number + 3.0) * 0.25)
    first = dot(
        ind((row_j < row_i) & (big_j == row_j * CAND), BF16), groups.astype(BF16)
    )
    rank = seen - 1.0 + ahead
    lap = jnp.floor(rank * 0.25)
    spot = 64.0 * (rank - 4.0 * lap) + first + lap
    place4 = 4.0 * (first + lap) + (rank - 4.0 * lap)

    def pick(values):
        out = jnp.zeros((CAND, 128), F32)
        for r in range(PASS_DEV):
            part = slice(r * CAND, (r + 1) * CAND)
            out = out + hit[part] * values[part]
        return out

    slot = jnp.where(own > 0, pick(spot), -1.0)
    place4 = pick(place4)
    cand = iota((CAND, 128), 0).astype(F32)
    code = CAND * cand + jnp.where(own > 0, local, 0.0)

    own_bf = own.astype(BF16)
    c_i, c_j = iota((CAND, CAND), 0), iota((CAND, CAND), 1)
    count = dot(jnp.ones((CAND, CAND), BF16), own_bf)
    earlier = dot(count.astype(BF16), before)
    entry = earlier + dot(ind(c_j < c_i, BF16), own_bf)
    entry = jnp.where(own > 0, entry, -1.0)
    last_entry = jnp.where(count > 0, earlier + count - 1.0, -1.0)

    lane = iota((8, 128), 1)
    query = ((lane // 8) * Q_DEV + lax.rem(lane, 8)).astype(F32).astype(BF16)
    one8 = jnp.ones((8, 128), BF16)
    qn, codes, valid, entry_place, entry_q = [], [], [], [], []
    for j in range(4):
        at = (iota((64, 128), 0) + 64 * j).astype(F32)
        acc = [jnp.zeros((64, 128), F32) for _ in range(4)]
        for c in range(CAND):
            one = ind(at == slot[c : c + 1])
            acc[0] = acc[0] + one
            acc[1] = acc[1] + one * code[c : c + 1]
            one = ind(at == entry[c : c + 1])
            acc[2] = acc[2] + one * place4[c : c + 1]
            acc[3] = acc[3] + one
        acc = [a.astype(BF16) for a in acc]
        hit_ref[64 * j : 64 * j + 64] = acc[0]
        qn.append(acc[0])
        codes.append(acc[1])
        entry_place.append(acc[2])
        entry_q.append(acc[3])
    at_slot = jnp.concatenate(qn, axis=0)
    qn = dot_nt(query, at_slot)
    valid = dot_nt(one8, at_slot)
    codes = dot_nt(one8, jnp.concatenate(codes, axis=0))
    entry_place = dot_nt(one8, jnp.concatenate(entry_place, axis=0))
    entry_q = dot_nt(query, jnp.concatenate(entry_q, axis=0))
    cands = jnp.floor(codes / CAND)
    row_of = codes - CAND * cands
    cands = jnp.where(valid > 0, cands, -1.0)

    last_group = jnp.where(number > 0, first + groups, 0.0)
    big = iota((256, 128), 0)
    diag = (big == iota((256, 128), 1) * CAND) & (iota((256, 128), 1) < PASS_DEV)
    last_row = dot(jnp.ones((8, 256), BF16), jnp.where(diag, last_group, 0.0).astype(BF16)) - 1.0
    pad = jnp.zeros((8, 128), F32)
    last_row = jnp.concatenate([last_row, pad], axis=1)
    last_entry = jnp.concatenate([last_entry[:8], pad], axis=1)

    sub = iota((8, SLOTS), 0)
    table = jnp.zeros((8, SLOTS), F32)
    rows_of_table = (qn, row_of, entry_place, entry_q, last_row, last_entry, cands)
    most = (OWNERS * Q_DEV - 1, PASS_DEV - 1, 4 * GROUPS - 1, OWNERS * Q_DEV - 1, GROUPS - 1, ENTRIES - 1, CAND - 1)
    for n, values in enumerate(rows_of_table):
        table = jnp.where(sub == n, jnp.clip(values, -1.0, most[n]), table)
    tab_ref[...] = jnp.clip(table.astype(I32), -1, SLOTS - 1)


FAR = (4, 3, 5, 2, 6, 1, 7)
A_ROWS, B_ROWS = 64, 32
A_PIECE, B_PIECE = NY * A_ROWS, NX * B_ROWS
B_AT = NX * A_PIECE
FLAT = PASS_DEV * ROWS


def rows_at(start, count):
    return pl.ds(pl.multiple_of(start, 16), count)


class Swap:
    def __init__(self, n, at, device, send, recv):
        self.n, self.at, self.device, self.send, self.recv = n, at, device, send, recv

    def start(self, src_of, buf):
        self.buf, self.copies = buf, []
        far = sorted(range(1, self.n), key=lambda k: -min(k, self.n - k))
        for k in far:
            t = lax.rem(self.at + k, self.n)
            copy = remote(
                src_of(t), buf.at[self.at], self.send.at[k - 1], self.recv.at[self.at], self.device(t)
            )
            copy.start()
            self.copies.append(copy)

    def finish(self):
        for k in range(1, self.n):
            t = lax.rem(self.at + k, self.n)
            remote(
                self.buf.at[t], self.buf.at[t], self.send.at[0], self.recv.at[t], self.device(t)
            ).wait_recv()

    def drain(self):
        for copy in self.copies:
            copy.wait_send()


def gather_kernel(
    hidden_ref, weight_ref, cache_ref, ids_ref, map_ref,
    query_ref, full_ref, raw_ref, tab_ref, hit_ref, tiles,
    rows_buf, cache_f, w_send, w_recv, r_send, r_recv, q_send, q_recv,
):
    place = Place()
    me = place.me
    barrier = pltpu.get_barrier_semaphore()
    peers = [{"passage": place.ring(k)} for k in NEAR] + [{"passage": place.sibling}]
    for device in peers:
        pl.semaphore_signal(barrier, inc=1, device_id=device, device_id_type=pl.DeviceIdType.MESH)

    full_ref[me] = weight_ref[...]
    table = jnp.broadcast_to(map_ref[...].astype(F32), (8, 256)).astype(BF16)
    own = jnp.full((8, CAND), -1.0, F32)
    for q in range(Q_DEV):
        one = ind(iota((256, CAND), 0) == ids_ref[q : q + 1, :], BF16)
        own = jnp.where(iota((8, CAND), 0) == q, dot(table, one), own)
    rows_buf[me] = jnp.full((8, 128), -1.0, F32)
    rows_buf[me, :, 0:CAND] = own
    pl.semaphore_wait(barrier, len(peers))

    weights = Gather(place, full_ref, w_send, w_recv)
    weights.start()
    rows = Gather(place, rows_buf, r_send, r_recv)
    rows.start()

    cache_f[...] = cache_ref[...].reshape(PLEN * PASS_DEV, DIM).astype(F32)
    for r in range(PASS_DEV):
        tiles[r, ROWS - 16 : ROWS] = jnp.zeros((16, DIM), BF16)
        tiles[r, 0:PLEN] = cache_f[pl.ds(r, PLEN, stride=PASS_DEV), :].astype(BF16)

    weights.finish()
    raw = dot(hidden_ref[...], full_ref[...].reshape(-1, DIM))
    raw_ref[...] = raw
    inverse = lax.rsqrt(jnp.mean(raw * raw, axis=-1, keepdims=True) + EPS)
    query_ref[me] = (raw * inverse).astype(BF16)
    queries = Gather(place, query_ref, q_send, q_recv)
    queries.start()

    rows.finish()
    routing_tables(rows_buf[...].reshape(OWNERS * 8, 128), me, tab_ref, hit_ref)
    queries.finish()


def pair_kernel(
    hidden_ref, full_ref, raw_ref, tiles, len_ref, tab, tab_vec, hit_ref, query_ref,
    hid_ref, wg_ref, cache_out,
    cache_f, exps, logs, recips, scales,
    score_buf, grad_vec, grad_tab, cg_run, qg_group, qg_run, qg_ref, cg_ref,
    ax_buf, ay_buf, by_buf, bx_buf, mid_a, mid_b, fin, q_sib, q_out, q_in, w_own, w_sib, w_out, w_in, w_x, w_y,
    grad_sem, out_sem,
    s_send, s_recv,
    qs_send, qs_recv, qz_send, qz_recv, ws_send, ws_recv, wz_send, wz_recv, wx_send, wx_recv, wy_send, wy_recv,
    a1_send, a1_recv, a2_send, a2_recv, a3_send, a3_recv, a4_send, a4_recv,
    b1_send, b1_recv, b2_send, b2_recv, b3_send, b3_recv, b4_send, b4_recv,
):
    place = Place()
    me, z, c = place.me, place.z, place.c
    dp = lax.axis_index("dp")
    ix, iy = dp // NY, lax.rem(dp, NY)
    others = [lax.rem(me + k, OWNERS) for k in range(1, OWNERS)]
    to_x = lambda k: {"dp": lax.rem(ix + k, NX) * NY + iy}
    to_y = lambda k: {"dp": ix * NY + lax.rem(iy + k, NY)}
    sibling = {"passage": place.sibling}
    similarity_scale = 1.0 / (TAU * math.sqrt(DIM))
    root_scale = 1.0 / math.sqrt(DIM)

    barrier = pltpu.get_barrier_semaphore()
    peers = [{"passage": d} for d in others]
    peers += [to_x(k) for k in range(1, NX)] + [to_y(k) for k in range(1, NY)]
    for device in peers:
        pl.semaphore_signal(barrier, inc=1, device_id=device, device_id_type=pl.DeviceIdType.MESH)
    logs[...] = jnp.zeros_like(logs)
    recips[...] = jnp.zeros_like(recips)

    def bounded(value, most):
        return jnp.minimum(jnp.maximum(value, 0), most)

    def row_of(g):
        return bounded(tab[1, g], PASS_DEV - 1)

    def load_queries(g):
        parts = []
        for j in range(4):
            n = bounded(tab[0, 64 * j + g], OWNERS * Q_DEV - 1)
            parts.append(query_ref[n])
        return jnp.concatenate(parts, axis=0)

    live = iota((ROWS, 128), 0)

    def forward(i, _):
        for u in range(4):
            g = 4 * i + u
            row = row_of(g)
            sims = dot_nt(tiles[row], load_queries(g)) * similarity_scale
            sims = jnp.where(live < len_ref[row], sims, NEG)
            top = jnp.max(sims, axis=0, keepdims=True)
            e = jnp.exp(sims - top)
            total = jnp.sum(e, axis=0, keepdims=True)
            exps[g] = e
            logs[pl.ds(g, 1), :] = top + jnp.log(total)
            recips[pl.ds(g, 1), :] = 1.0 / total
        return 0

    lax.fori_loop(0, GROUPS // 4, forward, 0)

    of_place = iota((SLOTS, 128), 1) // QL == iota((SLOTS, 128), 0) // 64
    spread = jnp.where(of_place, jnp.concatenate([logs[...]] * 4, axis=0), 0.0)
    one8 = jnp.ones((8, 128), BF16)
    score_row = TAU * sum(dot_nt(one8, part) for part in pieces(spread))
    cands = tab_vec[6:7, :]
    is_cand = ind(iota((CAND, SLOTS), 0) == cands)
    hits = hit_ref[...]
    mine = sum(
        dot((is_cand * part[0:1].astype(F32)).astype(BF16), hits) for part in pieces(score_row)
    )
    score_buf[me] = mine[0:8] + pltpu.roll(mine[8:16], 4, 1)
    pl.semaphore_wait(barrier, len(peers))
    score_swap = Swap(OWNERS, me, lambda t: {"passage": t}, s_send, s_recv)
    score_swap.start(lambda t: score_buf.at[me], score_buf)

    def products(i, _):
        for u in range(4):
            g = 4 * i + u
            w = (exps[g] * recips[pl.ds(g, 1), :]).astype(BF16)
            qg_group[g] = dot_tn(w, tiles[row_of(g)]).reshape(4, QL, DIM)
        return 0

    lax.fori_loop(0, GROUPS // 4, products, 0)

    score_swap.finish()
    scores = score_buf[0]
    for d in range(1, OWNERS):
        scores = scores + score_buf[d]
    lane = iota((8, 128), 1)
    low = lax.rem(lane, 8) < Q_DEV

    def both(x, op):
        return op(x, jnp.where(low, pltpu.roll(x, 124, 1), pltpu.roll(x, 4, 1)))

    top = both(jnp.broadcast_to(jnp.max(scores, axis=0, keepdims=True), (8, 128)), jnp.maximum)
    e = jnp.exp(scores - top)
    total = both(jnp.broadcast_to(jnp.sum(e, axis=0, keepdims=True), (8, 128)), jnp.add)
    grad = e / total - ind((iota((8, 128), 0) == 0) & low)
    grad = jnp.concatenate(
        [jnp.where(low, grad, 0.0), jnp.where(low, pltpu.roll(grad, 124, 1), 0.0)], axis=0
    )
    at_slot = is_cand * sum(dot_nt(part, hits) for part in pieces(grad))
    at_slot = jnp.sum(at_slot, axis=0, keepdims=True)
    grad_vec[...] = jnp.broadcast_to(at_slot * root_scale, (8, SLOTS))
    grad_copy = pltpu.make_async_copy(grad_vec, grad_tab, grad_sem)
    grad_copy.start()
    same_group = ind(lax.rem(iota((64, SLOTS), 1), 64) == iota((64, SLOTS), 0))
    to_lanes = ind(of_place, BF16)
    by_lane = sum(dot(part, to_lanes) for part in pieces(same_group * at_slot))
    scales[...] = by_lane * recips[...] * root_scale
    grad_copy.wait()

    def entry_step(i, run):
        for u in range(4):
            e = 4 * i + u
            at = bounded(tab[2, e], 4 * GROUPS - 1)
            group, spot = at // 4, lax.rem(at, 4)
            again = (tab[3, e] == tab[3, jnp.maximum(e - 1, 0)]) & (e > 0)
            run = jnp.where(again, run, 0.0) + qg_group[group, spot] * grad_tab[0, 64 * spot + group]
            qg_run[e] = run
        return run

    lax.fori_loop(0, ENTRIES // 4, entry_step, jnp.zeros((QL, DIM), F32))

    def finish_query(d, _):
        for q in range(Q_DEV):
            last = tab[5, 8 * d + q]
            value = jnp.where(last >= 0, qg_run[bounded(last, ENTRIES - 1)], 0.0)
            qg_ref[d // NC, lax.rem(d, NC), q * QL : (q + 1) * QL, :] = value.astype(BF16)
        return 0

    lax.fori_loop(0, OWNERS, finish_query, 0)
    q_pair = remote(qg_ref.at[:, 1 - c], q_sib, qs_send, qs_recv, sibling)
    q_pair.start()

    def cache_step(i, run):
        for u in range(4):
            g = 4 * i + u
            row = tab[1, g]
            w = (exps[g] * scales[pl.ds(g, 1), :]).astype(BF16)
            again = (row == tab[1, jnp.maximum(g - 1, 0)]) & (g > 0)
            cg_run[g + 1] = jnp.where(again, cg_run[g], 0.0) + dot(w, load_queries(g))
        return run

    lax.fori_loop(0, 4, cache_step, 0)
    q_pair.wait_recv()
    for t in range(NZ):
        q_out[t] = (qg_ref[t, c].astype(F32) + q_sib[t].astype(F32)).astype(BF16)
    on_z = lambda t: {"passage": t * NC + c}
    q_swap = Swap(NZ, z, on_z, qz_send, qz_recv)
    q_swap.start(lambda t: q_out.at[t], q_in)
    lax.fori_loop(4, GROUPS // 4, cache_step, 0)

    for r in range(PASS_DEV):
        last = tab[4, r]
        value = jnp.where(last >= 0, cg_run[bounded(last, GROUPS - 1) + 1], 0.0)
        cache_f[pl.ds(r, ROWS, stride=PASS_DEV), :] = value
    cg_ref[...] = cache_f[...].astype(BF16)

    sent = []

    def push(src, dst, send, recv, device):
        copy = remote(src, dst, send, recv, device)
        copy.start()
        sent.append(copy)

    def await_recv(dst, send, recv):
        remote(dst, dst, send, recv, sibling).wait_recv()

    def y_at(k):
        return lax.rem(iy + k + NY, NY)

    def x_at(k):
        return lax.rem(ix + k + NX, NX)

    for k in FAR:
        src = cg_ref.at[rows_at(B_AT + y_at(k) * B_PIECE, B_PIECE), :]
        push(src, by_buf.at[k - 1], b1_send.at[k - 1], b1_recv.at[k - 1], to_y(k))
    for d in FAR + (0,):
        for k in (2, 1, 3):
            src = cg_ref.at[rows_at(x_at(k) * A_PIECE + y_at(d) * A_ROWS, A_ROWS), :]
            push(src, ax_buf.at[k - 1, d], a1_send.at[k - 1, d], a1_recv.at[k - 1, d], to_x(k))

    q_swap.finish()
    query_gradient = q_out[z].astype(F32)
    for k in range(1, NZ):
        query_gradient = query_gradient + q_in[lax.rem(z + k, NZ)].astype(F32)
    raw = raw_ref[...]
    inverse = lax.rsqrt(jnp.mean(raw * raw, axis=-1, keepdims=True) + EPS)
    mean_term = jnp.mean(query_gradient * raw, axis=-1, keepdims=True)
    raw_grad = (
        inverse * query_gradient - raw * (inverse * inverse * inverse) * mean_term
    ).astype(BF16)
    weight_part = dot_tn(hidden_ref[...], raw_grad)
    w_own[...] = weight_part.astype(BF16).reshape(w_own.shape)
    w_pair = remote(w_own.at[:, 1 - c], w_sib, ws_send, ws_recv, sibling)
    w_pair.start()

    def a_first(d):
        total = cg_ref[rows_at(ix * A_PIECE + y_at(d) * A_ROWS, A_ROWS), :].astype(F32)
        for k in range(1, NX):
            await_recv(ax_buf.at[k - 1, d], a1_send.at[k - 1, d], a1_recv.at[k - 1, d])
            total = total + ax_buf[k - 1, d].astype(F32)
        mid_a[d] = total.astype(BF16)
        if d:
            push(mid_a.at[d], ay_buf.at[d - 1], a2_send.at[d - 1], a2_recv.at[d - 1], to_y(d))

    for d in FAR[:4]:
        a_first(d)
    w_pair.wait_recv()
    for t in range(NZ):
        w_out[t] = (w_own[t, c].astype(F32) + w_sib[t].astype(F32)).astype(BF16)
    w_swap = Swap(NZ, z, on_z, wz_send, wz_recv)
    w_swap.start(lambda t: w_out.at[t], w_in)
    for d in FAR[4:] + (0,):
        a_first(d)
    hid_ref[...] = dot_nt(raw_grad, full_ref[...].reshape(-1, DIM)).astype(BF16)

    total = cg_ref[rows_at(B_AT + iy * B_PIECE, B_PIECE), :].astype(F32)
    for k in range(1, NY):
        await_recv(by_buf.at[k - 1], b1_send.at[k - 1], b1_recv.at[k - 1])
        total = total + by_buf[k - 1].astype(F32)
    mid_b[...] = total.astype(BF16)
    for k in (2, 1, 3):
        src = mid_b.at[rows_at(x_at(k) * B_ROWS, B_ROWS), :]
        push(src, bx_buf.at[k - 1], b2_send.at[k - 1], b2_recv.at[k - 1], to_x(k))
    total = mid_b[rows_at(ix * B_ROWS, B_ROWS), :].astype(F32)
    for k in range(1, NX):
        await_recv(bx_buf.at[k - 1], b2_send.at[k - 1], b2_recv.at[k - 1])
        total = total + bx_buf[k - 1].astype(F32)
    b_span = lambda kx, ky: fin.at[rows_at(B_AT + y_at(ky) * B_PIECE + x_at(kx) * B_ROWS, B_ROWS), :]
    fin[rows_at(B_AT + iy * B_PIECE + ix * B_ROWS, B_ROWS), :] = total.astype(BF16)
    for k in (2, 1, 3):
        push(b_span(0, 0), b_span(0, 0), b3_send.at[k - 1], b3_recv.at[k - 1], to_x(k))

    total = mid_a[0].astype(F32)
    for d in range(1, NY):
        await_recv(ay_buf.at[d - 1], a2_send.at[d - 1], a2_recv.at[d - 1])
        total = total + ay_buf[d - 1].astype(F32)
    a_span = lambda kx, ky: fin.at[rows_at(x_at(kx) * A_PIECE + y_at(ky) * A_ROWS, A_ROWS), :]
    fin[rows_at(ix * A_PIECE + iy * A_ROWS, A_ROWS), :] = total.astype(BF16)
    for d in FAR:
        push(a_span(0, 0), a_span(0, 0), a3_send.at[d - 1], a3_recv.at[d - 1], to_y(d))
    for k in (2, 1, 3):
        push(a_span(0, 0), a_span(0, 0), a4_send.at[k - 1, 0], a4_recv.at[k - 1, 0], to_x(k))

    w_swap.finish()
    total = w_out[z].astype(F32)
    for k in range(1, NZ):
        total = total + w_in[lax.rem(z + k, NZ)].astype(F32)
    w_x[ix] = total.astype(BF16)
    x_swap = Swap(NX, ix, lambda t: {"dp": t * NY + iy}, wx_send, wx_recv)
    x_swap.start(lambda t: w_x.at[ix], w_x)

    for k in range(1, NX):
        await_recv(b_span(-k, 0), b3_send.at[k - 1], b3_recv.at[k - 1])
    b_line = lambda k: fin.at[rows_at(B_AT + y_at(k) * B_PIECE, B_PIECE), :]
    for d in FAR:
        push(b_line(0), b_line(0), b4_send.at[d - 1], b4_recv.at[d - 1], to_y(d))

    def a_forward(d):
        await_recv(a_span(0, -d), a3_send.at[d - 1], a3_recv.at[d - 1])
        for k in (2, 1, 3):
            push(a_span(0, -d), a_span(0, -d), a4_send.at[k - 1, d], a4_recv.at[k - 1, d], to_x(k))

    for d in NEAR[:4]:
        a_forward(d)
    x_swap.finish()
    total = w_x[0].astype(F32)
    for t in range(1, NX):
        total = total + w_x[t].astype(F32)
    w_y[iy] = total.astype(BF16)
    y_swap = Swap(NY, iy, lambda t: {"dp": ix * NY + t}, wy_send, wy_recv)
    y_swap.start(lambda t: w_y.at[iy], w_y)
    for d in NEAR[4:]:
        a_forward(d)

    for d in range(1, NY):
        await_recv(b_line(-d), b4_send.at[d - 1], b4_recv.at[d - 1])
    b_live = PLEN * PASS_DEV - B_AT
    b_out = pltpu.make_async_copy(
        fin.at[pl.ds(B_AT, b_live), :], cache_out.at[pl.ds(B_AT, b_live), :], out_sem.at[0]
    )
    b_out.start()
    for d in range(NY):
        for k in range(1, NX):
            await_recv(a_span(-k, -d), a4_send.at[k - 1, d], a4_recv.at[k - 1, d])
    a_out = pltpu.make_async_copy(
        fin.at[pl.ds(0, B_AT), :], cache_out.at[pl.ds(0, B_AT), :], out_sem.at[1]
    )
    a_out.start()
    y_swap.finish()
    total = w_y[0].astype(F32)
    for t in range(1, NY):
        total = total + w_y[t].astype(F32)
    wg_ref[...] = total

    q_pair.wait_send()
    w_pair.wait_send()
    for moved in (score_swap, q_swap, w_swap, x_swap, y_swap):
        moved.drain()
    for copy in sent:
        copy.wait_send()
    b_out.wait()
    a_out.wait()


VMEM = pl.BlockSpec(memory_space=pltpu.VMEM)
SMEM = pl.BlockSpec(memory_space=pltpu.SMEM)
ANY = pl.BlockSpec(memory_space=pl.ANY)


def call(kernel, collective_id, out_shape, in_specs, out_specs, scratch, args):
    return pl.pallas_call(
        kernel,
        out_shape=out_shape,
        in_specs=in_specs,
        out_specs=out_specs,
        scratch_shapes=scratch,
        compiler_params=pltpu.CompilerParams(
            collective_id=collective_id, has_side_effects=True, vmem_limit_bytes=56 * 2**20
        ),
    )(*args)


def shards(hidden, weight, cache, lengths, passage_ids, owner_map):
    width = hidden.shape[-1]
    share = width // OWNERS
    tokens = Q_DEV * QL
    shape = jax.ShapeDtypeStruct
    dma = pltpu.SemaphoreType.DMA
    vmem = pltpu.VMEM

    def pair(*sizes):
        return [dma(sizes), dma(sizes)]

    gather = [dma((2 * NZ - 1,)), dma((OWNERS,))]
    hidden = hidden.reshape(tokens, width)
    queries, full, raw, tab, hits, tiles = call(
        gather_kernel,
        0,
        [
            shape((OWNERS, tokens, DIM), BF16),
            shape((OWNERS, share, DIM), BF16),
            shape((tokens, DIM), F32),
            shape((8, SLOTS), I32),
            shape((SLOTS, 128), BF16),
            shape((PASS_DEV, ROWS, DIM), BF16),
        ],
        [VMEM] * 5,
        [VMEM] * 6,
        [vmem((OWNERS, 8, 128), F32), vmem((PLEN * PASS_DEV, DIM), F32)] + gather + gather + gather,
        (hidden, weight, jnp.transpose(cache, (1, 0, 2)), passage_ids, owner_map.reshape(1, -1)),
    )
    scratch = [
        vmem((FLAT, DIM), F32),
        vmem((GROUPS, ROWS, 128), F32),
        vmem((64, 128), F32),
        vmem((64, 128), F32),
        vmem((64, 128), F32),
        vmem((OWNERS, 8, 128), F32),
        vmem((8, SLOTS), F32),
        pltpu.SMEM((8, SLOTS), F32),
        vmem((GROUPS + 1, ROWS, DIM), F32),
        vmem((GROUPS, 4, QL, DIM), F32),
        vmem((ENTRIES, QL, DIM), F32),
        vmem((NZ, NC, tokens, DIM), BF16),
        vmem((FLAT, DIM), BF16),
        vmem((NX - 1, NY, A_ROWS, DIM), BF16),
        vmem((NY - 1, A_ROWS, DIM), BF16),
        vmem((NY - 1, B_PIECE, DIM), BF16),
        vmem((NX - 1, B_ROWS, DIM), BF16),
        vmem((NY, A_ROWS, DIM), BF16),
        vmem((B_PIECE, DIM), BF16),
        vmem((FLAT, DIM), BF16),
        vmem((NZ, tokens, DIM), BF16),
        vmem((NZ, tokens, DIM), BF16),
        vmem((NZ, tokens, DIM), BF16),
        vmem((NZ, NC, share, DIM), BF16),
        vmem((NZ, share, DIM), BF16),
        vmem((NZ, share, DIM), BF16),
        vmem((NZ, share, DIM), BF16),
        vmem((NX, share, DIM), BF16),
        vmem((NY, share, DIM), BF16),
        dma,
        dma((2,)),
    ]
    swap = lambda n: [dma((n - 1,)), dma((n,))]
    scratch += swap(OWNERS)
    scratch += [dma, dma] + swap(NZ) + [dma, dma] + swap(NZ) + swap(NX) + swap(NY)
    scratch += pair(NX - 1, NY) + pair(NY - 1) + pair(NY - 1) + pair(NX - 1, NY)
    scratch += pair(NY - 1) + pair(NX - 1) + pair(NX - 1) + pair(NY - 1)

    hid, wg, cache_grad = call(
        pair_kernel,
        1,
        [
            shape((tokens, width), BF16),
            shape((share, DIM), F32),
            shape((PLEN * PASS_DEV, DIM), BF16),
        ],
        [VMEM, VMEM, VMEM, VMEM, SMEM, SMEM, VMEM, VMEM, VMEM],
        [VMEM, VMEM, ANY],
        scratch,
        (hidden, full, raw, tiles, lengths, tab, tab, hits, queries.reshape(OWNERS * Q_DEV, QL, DIM)),
    )
    cache_grad = jnp.transpose(cache_grad.reshape(PLEN, PASS_DEV, DIM), (1, 0, 2))
    return hid.reshape(Q_DEV, QL, width), wg, cache_grad


def solution(mesh):
    in_specs = (
        P(("dp", "passage"), None, None),
        P("passage", None),
        P("passage", None, None),
        P("passage"),
        P(("dp", "passage"), None),
        P(),
    )
    out_specs = (P(("dp", "passage"), None, None), P("passage", None), P("passage", None, None))
    return jax.shard_map(shards, mesh=mesh, in_specs=in_specs, out_specs=out_specs, check_vma=False)
```

```python
import functools
import math

import jax
import jax.numpy as jnp
from jax import lax
from jax.experimental import pallas as pl
from jax.experimental.pallas import tpu as pltpu
from jax.sharding import PartitionSpec as P

TAU = 0.1
EPS = 1e-06

NX, NY, NZ, NC = 4, 8, 8, 2
OWNERS = NZ * NC
Q_DEV, QL, CAND = 4, 32, 16
PASS_DEV, PLEN, ROWS = 16, 180, 192
DIM = 128
GROUPS = 60
SLOTS = 256
ENTRIES = 192
NEG = -1e30

F32, BF16, I32 = jnp.float32, jnp.bfloat16, jnp.int32


def dot(a, b):
    return jnp.dot(a, b, preferred_element_type=F32)


def dot_nt(a, b):
    return lax.dot_general(a, b, (((1,), (1,)), ((), ())), preferred_element_type=F32)


def dot_tn(a, b):
    return lax.dot_general(a, b, (((0,), (0,)), ((), ())), preferred_element_type=F32)


def iota(shape, axis):
    return lax.broadcasted_iota(I32, shape, axis)


def ind(cond, dtype=F32):
    return jnp.where(cond, 1.0, 0.0).astype(dtype)


def pieces(x):
    a = x.astype(BF16)
    rest = x - a.astype(F32)
    b = rest.astype(BF16)
    return (a, b, (rest - b.astype(F32)).astype(BF16))


class Place:
    def __init__(self):
        self.me = lax.axis_index("passage")
        self.z, self.c = self.me // NC, lax.rem(self.me, NC)
        self.sibling = self.z * NC + (1 - self.c)

    def ring(self, k):
        return lax.rem(self.z + k, NZ) * NC + self.c

    def ring_sibling(self, k):
        return lax.rem(self.z + k, NZ) * NC + (1 - self.c)


def remote(src, dst, send, recv, device):
    return pltpu.make_async_remote_copy(
        src_ref=src,
        dst_ref=dst,
        send_sem=send,
        recv_sem=recv,
        device_id=device,
        device_id_type=pl.DeviceIdType.MESH,
    )


NEAR = (1, 7, 2, 6, 3, 5, 4)


class Gather:
    def __init__(self, place, buf, send, recv):
        self.place, self.buf, self.send, self.recv = place, buf, send, recv
        self.sent = []

    def copy(self, slot, n, peer):
        return remote(
            self.buf.at[slot], self.buf.at[slot], self.send.at[n], self.recv.at[slot],
            {"passage": peer},
        )

    def start(self):
        p = self.place
        for n, k in enumerate(NEAR):
            self.sent.append(self.copy(p.me, n, p.ring(k)))
            self.sent[-1].start()
        self.sent.append(self.copy(p.me, NZ - 1, p.sibling))
        self.sent[-1].start()

    def finish(self, landed=lambda slot: None):
        p = self.place
        for n, k in enumerate(NEAR):
            forward = self.copy(p.ring(k), NZ + n, p.sibling)
            forward.wait_recv()
            forward.start()
            self.sent.append(forward)
            landed(p.ring(k))
        self.copy(p.sibling, 0, p.sibling).wait_recv()
        landed(p.sibling)
        for k in NEAR:
            self.copy(p.ring_sibling(k), 0, p.sibling).wait_recv()
            landed(p.ring_sibling(k))
        for copy in self.sent:
            copy.wait_send()


def routing_tables(rows, me, tab_ref, hit_ref):
    rows_t = dot_nt(ind(iota((CAND, 128), 0) == iota((CAND, 128), 1), BF16), rows.astype(BF16))
    local = rows_t - (PASS_DEV * me).astype(F32)
    own = ind((local >= 0) & (local < PASS_DEV))
    hit = jnp.concatenate([ind(local == r) for r in range(PASS_DEV)], axis=0)
    lane_i, lane_j = iota((128, 128), 0), iota((128, 128), 1)
    upto = ind(lane_i <= lane_j, BF16)
    before = ind(lane_i < lane_j, BF16)
    ones = jnp.ones((128, 128), BF16)
    hit_bf = hit.astype(BF16)
    seen = dot(hit_bf, upto)
    total = dot(hit_bf, ones).astype(BF16)
    big_i, big_j = iota((256, 256), 0), iota((256, 256), 1)
    row_i, row_j = big_i // CAND, big_j // CAND
    ahead = dot(ind((row_i == row_j) & (big_j < big_i), BF16), total)
    number = dot(ind(row_i == row_j, BF16), total)
    groups = jnp.floor((number + 3.0) * 0.25)
    first = dot(
        ind((row_j < row_i) & (big_j == row_j * CAND), BF16), groups.astype(BF16)
    )
    rank = seen - 1.0 + ahead
    lap = jnp.floor(rank * 0.25)
    spot = 64.0 * (rank - 4.0 * lap) + first + lap
    place4 = 4.0 * (first + lap) + (rank - 4.0 * lap)

    def pick(values):
        out = jnp.zeros((CAND, 128), F32)
        for r in range(PASS_DEV):
            part = slice(r * CAND, (r + 1) * CAND)
            out = out + hit[part] * values[part]
        return out

    slot = jnp.where(own > 0, pick(spot), -1.0)
    place4 = pick(place4)
    cand = iota((CAND, 128), 0).astype(F32)
    code = CAND * cand + jnp.where(own > 0, local, 0.0)

    own_bf = own.astype(BF16)
    c_i, c_j = iota((CAND, CAND), 0), iota((CAND, CAND), 1)
    count = dot(jnp.ones((CAND, CAND), BF16), own_bf)
    earlier = dot(count.astype(BF16), before)
    entry = earlier + dot(ind(c_j < c_i, BF16), own_bf)
    entry = jnp.where(own > 0, entry, -1.0)
    last_entry = jnp.where(count > 0, earlier + count - 1.0, -1.0)

    lane = iota((8, 128), 1)
    query = ((lane // 8) * Q_DEV + lax.rem(lane, 8)).astype(F32).astype(BF16)
    one8 = jnp.ones((8, 128), BF16)
    qn, codes, valid, entry_place, entry_q = [], [], [], [], []
    for j in range(4):
        at = (iota((64, 128), 0) + 64 * j).astype(F32)
        acc = [jnp.zeros((64, 128), F32) for _ in range(4)]
        for c in range(CAND):
            one = ind(at == slot[c : c + 1])
            acc[0] = acc[0] + one
            acc[1] = acc[1] + one * code[c : c + 1]
            one = ind(at == entry[c : c + 1])
            acc[2] = acc[2] + one * place4[c : c + 1]
            acc[3] = acc[3] + one
        acc = [a.astype(BF16) for a in acc]
        hit_ref[64 * j : 64 * j + 64] = acc[0]
        qn.append(acc[0])
        codes.append(acc[1])
        entry_place.append(acc[2])
        entry_q.append(acc[3])
    at_slot = jnp.concatenate(qn, axis=0)
    qn = dot_nt(query, at_slot)
    valid = dot_nt(one8, at_slot)
    codes = dot_nt(one8, jnp.concatenate(codes, axis=0))
    entry_place = dot_nt(one8, jnp.concatenate(entry_place, axis=0))
    entry_q = dot_nt(query, jnp.concatenate(entry_q, axis=0))
    cands = jnp.floor(codes / CAND)
    row_of = codes - CAND * cands
    cands = jnp.where(valid > 0, cands, -1.0)

    last_group = jnp.where(number > 0, first + groups, 0.0)
    big = iota((256, 128), 0)
    diag = (big == iota((256, 128), 1) * CAND) & (iota((256, 128), 1) < PASS_DEV)
    last_row = dot(jnp.ones((8, 256), BF16), jnp.where(diag, last_group, 0.0).astype(BF16)) - 1.0
    pad = jnp.zeros((8, 128), F32)
    last_row = jnp.concatenate([last_row, pad], axis=1)
    last_entry = jnp.concatenate([last_entry[:8], pad], axis=1)

    sub = iota((8, SLOTS), 0)
    table = jnp.zeros((8, SLOTS), F32)
    rows_of_table = (qn, row_of, entry_place, entry_q, last_row, last_entry, cands)
    most = (OWNERS * Q_DEV - 1, PASS_DEV - 1, 4 * GROUPS - 1, OWNERS * Q_DEV - 1, GROUPS - 1, ENTRIES - 1, CAND - 1)
    for n, values in enumerate(rows_of_table):
        table = jnp.where(sub == n, jnp.clip(values, -1.0, most[n]), table)
    tab_ref[...] = jnp.clip(table.astype(I32), -1, SLOTS - 1)


FAR = (4, 3, 5, 2, 6, 1, 7)
A_ROWS, B_ROWS = 64, 32
A_PIECE, B_PIECE = NY * A_ROWS, NX * B_ROWS
B_AT = NX * A_PIECE
FLAT = PASS_DEV * ROWS


def rows_at(start, count):
    return pl.ds(pl.multiple_of(start, 16), count)


class Swap:
    def __init__(self, n, at, device, send, recv):
        self.n, self.at, self.device, self.send, self.recv = n, at, device, send, recv

    def start(self, src_of, buf):
        self.buf, self.copies = buf, []
        far = sorted(range(1, self.n), key=lambda k: -min(k, self.n - k))
        for k in far:
            t = lax.rem(self.at + k, self.n)
            copy = remote(
                src_of(t), buf.at[self.at], self.send.at[k - 1], self.recv.at[self.at], self.device(t)
            )
            copy.start()
            self.copies.append(copy)

    def finish(self):
        for k in range(1, self.n):
            t = lax.rem(self.at + k, self.n)
            remote(
                self.buf.at[t], self.buf.at[t], self.send.at[0], self.recv.at[t], self.device(t)
            ).wait_recv()

    def drain(self):
        for copy in self.copies:
            copy.wait_send()


def gather_kernel(
    hidden_hbm, weight_ref, cache_hbm, ids_ref, map_ref,
    query_out, full_out, raw_ref, tab_ref, hit_ref, tiles_out,
    hidden_ref, cache_ref, query_ref, full_ref, tiles,
    rows_buf, cache_f, in_sem, tiles_sem, full_sem, query_sem, w_send, w_recv, r_send, r_recv, q_send, q_recv,
):
    place = Place()
    me = place.me
    barrier = pltpu.get_barrier_semaphore()
    peers = [{"passage": place.ring(k)} for k in NEAR] + [{"passage": place.sibling}]
    for device in peers:
        pl.semaphore_signal(barrier, inc=1, device_id=device, device_id_type=pl.DeviceIdType.MESH)

    hidden_in = pltpu.make_async_copy(hidden_hbm, hidden_ref, in_sem.at[0])
    cache_in = pltpu.make_async_copy(cache_hbm, cache_ref, in_sem.at[1])
    hidden_in.start()
    cache_in.start()
    full_ref[me] = weight_ref[...]
    table = jnp.broadcast_to(map_ref[...].astype(F32), (8, 256)).astype(BF16)
    own = jnp.full((8, CAND), -1.0, F32)
    for q in range(Q_DEV):
        one = ind(iota((256, CAND), 0) == ids_ref[q : q + 1, :], BF16)
        own = jnp.where(iota((8, CAND), 0) == q, dot(table, one), own)
    rows_buf[me] = jnp.full((8, 128), -1.0, F32)
    rows_buf[me, :, 0:CAND] = own
    pl.semaphore_wait(barrier, len(peers))

    weights = Gather(place, full_ref, w_send, w_recv)
    weights.start()
    rows = Gather(place, rows_buf, r_send, r_recv)
    rows.start()

    cache_in.wait()
    cache_f[...] = cache_ref[...].reshape(PLEN * PASS_DEV, DIM).astype(F32)
    for r in range(PASS_DEV):
        tiles[r, ROWS - 16 : ROWS] = jnp.zeros((16, DIM), BF16)
        tiles[r, 0:PLEN] = cache_f[pl.ds(r, PLEN, stride=PASS_DEV), :].astype(BF16)

    tiles_copy = pltpu.make_async_copy(tiles, tiles_out, tiles_sem)
    tiles_copy.start()
    hidden_in.wait()
    weights.finish()
    full_copy = pltpu.make_async_copy(full_ref, full_out, full_sem)
    full_copy.start()
    raw = dot(hidden_ref[...], full_ref[...].reshape(-1, DIM))
    raw_ref[...] = raw
    inverse = lax.rsqrt(jnp.mean(raw * raw, axis=-1, keepdims=True) + EPS)
    query_ref[me] = (raw * inverse).astype(BF16)
    queries = Gather(place, query_ref, q_send, q_recv)
    queries.start()

    rows.finish()
    routing_tables(rows_buf[...].reshape(OWNERS * 8, 128), me, tab_ref, hit_ref)
    kept = []

    def keep(slot):
        copy = pltpu.make_async_copy(query_ref.at[slot], query_out.at[slot], query_sem.at[slot])
        copy.start()
        kept.append(copy)

    keep(me)
    queries.finish(keep)
    for copy in kept + [tiles_copy, full_copy]:
        copy.wait()


def pair_kernel(
    hidden_hbm, full_hbm, raw_hbm, tiles_hbm, len_ref, tab, tab_hbm, hit_hbm, query_hbm,
    hid_ref, wg_ref, cache_out,
    hidden_ref, full_ref, raw_ref, tiles, tab_vec, hit_ref, query_ref, in_sem,
    cache_f, exps, logs, recips, scales,
    score_buf, grad_vec, grad_tab, cg_run, qg_group, qg_run, qg_ref, cg_ref,
    ax_buf, ay_buf, by_buf, bx_buf, mid_a, mid_b, fin, q_sib, q_out, q_in, w_own, w_sib, w_out, w_in, w_x, w_y,
    grad_sem, out_sem,
    s_send, s_recv,
    qs_send, qs_recv, qz_send, qz_recv, ws_send, ws_recv, wz_send, wz_recv, wx_send, wx_recv, wy_send, wy_recv,
    a1_send, a1_recv, a2_send, a2_recv, a3_send, a3_recv, a4_send, a4_recv,
    b1_send, b1_recv, b2_send, b2_recv, b3_send, b3_recv, b4_send, b4_recv,
):
    place = Place()
    me, z, c = place.me, place.z, place.c
    dp = lax.axis_index("dp")
    ix, iy = dp // NY, lax.rem(dp, NY)
    others = [lax.rem(me + k, OWNERS) for k in range(1, OWNERS)]
    to_x = lambda k: {"dp": lax.rem(ix + k, NX) * NY + iy}
    to_y = lambda k: {"dp": ix * NY + lax.rem(iy + k, NY)}
    sibling = {"passage": place.sibling}
    similarity_scale = 1.0 / (TAU * math.sqrt(DIM))
    root_scale = 1.0 / math.sqrt(DIM)

    barrier = pltpu.get_barrier_semaphore()
    peers = [{"passage": d} for d in others]
    peers += [to_x(k) for k in range(1, NX)] + [to_y(k) for k in range(1, NY)]
    for device in peers:
        pl.semaphore_signal(barrier, inc=1, device_id=device, device_id_type=pl.DeviceIdType.MESH)
    moves = [
        pltpu.make_async_copy(src, dst, in_sem.at[n])
        for n, (src, dst) in enumerate(
            [
                (tiles_hbm, tiles),
                (query_hbm, query_ref),
                (tab_hbm, tab_vec),
                (hit_hbm, hit_ref),
                (hidden_hbm, hidden_ref),
                (full_hbm, full_ref),
                (raw_hbm, raw_ref),
            ]
        )
    ]
    for move in moves:
        move.start()
    logs[...] = jnp.zeros_like(logs)
    recips[...] = jnp.zeros_like(recips)
    for move in moves[:2]:
        move.wait()

    def bounded(value, most):
        return jnp.minimum(jnp.maximum(value, 0), most)

    def row_of(g):
        return bounded(tab[1, g], PASS_DEV - 1)

    def load_queries(g):
        parts = []
        for j in range(4):
            n = bounded(tab[0, 64 * j + g], OWNERS * Q_DEV - 1)
            parts.append(query_ref[n])
        return jnp.concatenate(parts, axis=0)

    live = iota((ROWS, 128), 0)

    def forward(i, _):
        for u in range(4):
            g = 4 * i + u
            row = row_of(g)
            sims = dot_nt(tiles[row], load_queries(g)) * similarity_scale
            sims = jnp.where(live < len_ref[row], sims, NEG)
            top = jnp.max(sims, axis=0, keepdims=True)
            e = jnp.exp(sims - top)
            total = jnp.sum(e, axis=0, keepdims=True)
            exps[g] = e
            logs[pl.ds(g, 1), :] = top + jnp.log(total)
            recips[pl.ds(g, 1), :] = 1.0 / total
        return 0

    lax.fori_loop(0, GROUPS // 4, forward, 0)

    for move in moves[2:]:
        move.wait()

    of_place = iota((SLOTS, 128), 1) // QL == iota((SLOTS, 128), 0) // 64
    spread = jnp.where(of_place, jnp.concatenate([logs[...]] * 4, axis=0), 0.0)
    one8 = jnp.ones((8, 128), BF16)
    score_row = TAU * sum(dot_nt(one8, part) for part in pieces(spread))
    cands = tab_vec[6:7, :]
    is_cand = ind(iota((CAND, SLOTS), 0) == cands)
    hits = hit_ref[...]
    mine = sum(
        dot((is_cand * part[0:1].astype(F32)).astype(BF16), hits) for part in pieces(score_row)
    )
    score_buf[me] = mine[0:8] + pltpu.roll(mine[8:16], 4, 1)
    pl.semaphore_wait(barrier, len(peers))
    score_swap = Swap(OWNERS, me, lambda t: {"passage": t}, s_send, s_recv)
    score_swap.start(lambda t: score_buf.at[me], score_buf)

    def products(i, _):
        for u in range(4):
            g = 4 * i + u
            w = (exps[g] * recips[pl.ds(g, 1), :]).astype(BF16)
            qg_group[g] = dot_tn(w, tiles[row_of(g)]).reshape(4, QL, DIM)
        return 0

    lax.fori_loop(0, GROUPS // 4, products, 0)

    score_swap.finish()
    scores = score_buf[0]
    for d in range(1, OWNERS):
        scores = scores + score_buf[d]
    lane = iota((8, 128), 1)
    low = lax.rem(lane, 8) < Q_DEV

    def both(x, op):
        return op(x, jnp.where(low, pltpu.roll(x, 124, 1), pltpu.roll(x, 4, 1)))

    top = both(jnp.broadcast_to(jnp.max(scores, axis=0, keepdims=True), (8, 128)), jnp.maximum)
    e = jnp.exp(scores - top)
    total = both(jnp.broadcast_to(jnp.sum(e, axis=0, keepdims=True), (8, 128)), jnp.add)
    grad = e / total - ind((iota((8, 128), 0) == 0) & low)
    grad = jnp.concatenate(
        [jnp.where(low, grad, 0.0), jnp.where(low, pltpu.roll(grad, 124, 1), 0.0)], axis=0
    )
    at_slot = is_cand * sum(dot_nt(part, hits) for part in pieces(grad))
    at_slot = jnp.sum(at_slot, axis=0, keepdims=True)
    grad_vec[...] = jnp.broadcast_to(at_slot * root_scale, (8, SLOTS))
    grad_copy = pltpu.make_async_copy(grad_vec, grad_tab, grad_sem)
    grad_copy.start()
    same_group = ind(lax.rem(iota((64, SLOTS), 1), 64) == iota((64, SLOTS), 0))
    to_lanes = ind(of_place, BF16)
    by_lane = sum(dot(part, to_lanes) for part in pieces(same_group * at_slot))
    scales[...] = by_lane * recips[...] * root_scale
    grad_copy.wait()

    def entry_step(i, run):
        for u in range(4):
            e = 4 * i + u
            at = bounded(tab[2, e], 4 * GROUPS - 1)
            group, spot = at // 4, lax.rem(at, 4)
            again = (tab[3, e] == tab[3, jnp.maximum(e - 1, 0)]) & (e > 0)
            run = jnp.where(again, run, 0.0) + qg_group[group, spot] * grad_tab[0, 64 * spot + group]
            qg_run[e] = run
        return run

    lax.fori_loop(0, ENTRIES // 4, entry_step, jnp.zeros((QL, DIM), F32))

    def finish_query(d, _):
        for q in range(Q_DEV):
            last = tab[5, 8 * d + q]
            value = jnp.where(last >= 0, qg_run[bounded(last, ENTRIES - 1)], 0.0)
            qg_ref[d // NC, lax.rem(d, NC), q * QL : (q + 1) * QL, :] = value.astype(BF16)
        return 0

    lax.fori_loop(0, OWNERS, finish_query, 0)
    q_pair = remote(qg_ref.at[:, 1 - c], q_sib, qs_send, qs_recv, sibling)
    q_pair.start()

    def cache_step(i, run):
        for u in range(4):
            g = 4 * i + u
            row = tab[1, g]
            w = (exps[g] * scales[pl.ds(g, 1), :]).astype(BF16)
            again = (row == tab[1, jnp.maximum(g - 1, 0)]) & (g > 0)
            cg_run[g + 1] = jnp.where(again, cg_run[g], 0.0) + dot(w, load_queries(g))
        return run

    lax.fori_loop(0, 4, cache_step, 0)
    q_pair.wait_recv()
    for t in range(NZ):
        q_out[t] = (qg_ref[t, c].astype(F32) + q_sib[t].astype(F32)).astype(BF16)
    on_z = lambda t: {"passage": t * NC + c}
    q_swap = Swap(NZ, z, on_z, qz_send, qz_recv)
    q_swap.start(lambda t: q_out.at[t], q_in)
    lax.fori_loop(4, GROUPS // 4, cache_step, 0)

    for r in range(PASS_DEV):
        last = tab[4, r]
        value = jnp.where(last >= 0, cg_run[bounded(last, GROUPS - 1) + 1], 0.0)
        cache_f[pl.ds(r, ROWS, stride=PASS_DEV), :] = value
    cg_ref[...] = cache_f[...].astype(BF16)

    sent = []

    def push(src, dst, send, recv, device):
        copy = remote(src, dst, send, recv, device)
        copy.start()
        sent.append(copy)

    def await_recv(dst, send, recv):
        remote(dst, dst, send, recv, sibling).wait_recv()

    def y_at(k):
        return lax.rem(iy + k + NY, NY)

    def x_at(k):
        return lax.rem(ix + k + NX, NX)

    for k in FAR:
        src = cg_ref.at[rows_at(B_AT + y_at(k) * B_PIECE, B_PIECE), :]
        push(src, by_buf.at[k - 1], b1_send.at[k - 1], b1_recv.at[k - 1], to_y(k))
    for d in FAR + (0,):
        for k in (2, 1, 3):
            src = cg_ref.at[rows_at(x_at(k) * A_PIECE + y_at(d) * A_ROWS, A_ROWS), :]
            push(src, ax_buf.at[k - 1, d], a1_send.at[k - 1, d], a1_recv.at[k - 1, d], to_x(k))

    q_swap.finish()
    query_gradient = q_out[z].astype(F32)
    for k in range(1, NZ):
        query_gradient = query_gradient + q_in[lax.rem(z + k, NZ)].astype(F32)
    raw = raw_ref[...]
    inverse = lax.rsqrt(jnp.mean(raw * raw, axis=-1, keepdims=True) + EPS)
    mean_term = jnp.mean(query_gradient * raw, axis=-1, keepdims=True)
    raw_grad = (
        inverse * query_gradient - raw * (inverse * inverse * inverse) * mean_term
    ).astype(BF16)
    weight_part = dot_tn(hidden_ref[...], raw_grad)
    w_own[...] = weight_part.astype(BF16).reshape(w_own.shape)
    w_pair = remote(w_own.at[:, 1 - c], w_sib, ws_send, ws_recv, sibling)
    w_pair.start()

    def a_first(d):
        total = cg_ref[rows_at(ix * A_PIECE + y_at(d) * A_ROWS, A_ROWS), :].astype(F32)
        for k in range(1, NX):
            await_recv(ax_buf.at[k - 1, d], a1_send.at[k - 1, d], a1_recv.at[k - 1, d])
            total = total + ax_buf[k - 1, d].astype(F32)
        mid_a[d] = total.astype(BF16)
        if d:
            push(mid_a.at[d], ay_buf.at[d - 1], a2_send.at[d - 1], a2_recv.at[d - 1], to_y(d))

    for d in FAR[:4]:
        a_first(d)
    w_pair.wait_recv()
    for t in range(NZ):
        w_out[t] = (w_own[t, c].astype(F32) + w_sib[t].astype(F32)).astype(BF16)
    w_swap = Swap(NZ, z, on_z, wz_send, wz_recv)
    w_swap.start(lambda t: w_out.at[t], w_in)
    for d in FAR[4:] + (0,):
        a_first(d)
    hid_ref[...] = dot_nt(raw_grad, full_ref[...].reshape(-1, DIM)).astype(BF16)

    total = cg_ref[rows_at(B_AT + iy * B_PIECE, B_PIECE), :].astype(F32)
    for k in range(1, NY):
        await_recv(by_buf.at[k - 1], b1_send.at[k - 1], b1_recv.at[k - 1])
        total = total + by_buf[k - 1].astype(F32)
    mid_b[...] = total.astype(BF16)
    for k in (2, 1, 3):
        src = mid_b.at[rows_at(x_at(k) * B_ROWS, B_ROWS), :]
        push(src, bx_buf.at[k - 1], b2_send.at[k - 1], b2_recv.at[k - 1], to_x(k))
    total = mid_b[rows_at(ix * B_ROWS, B_ROWS), :].astype(F32)
    for k in range(1, NX):
        await_recv(bx_buf.at[k - 1], b2_send.at[k - 1], b2_recv.at[k - 1])
        total = total + bx_buf[k - 1].astype(F32)
    b_span = lambda kx, ky: fin.at[rows_at(B_AT + y_at(ky) * B_PIECE + x_at(kx) * B_ROWS, B_ROWS), :]
    fin[rows_at(B_AT + iy * B_PIECE + ix * B_ROWS, B_ROWS), :] = total.astype(BF16)
    for k in (2, 1, 3):
        push(b_span(0, 0), b_span(0, 0), b3_send.at[k - 1], b3_recv.at[k - 1], to_x(k))

    total = mid_a[0].astype(F32)
    for d in range(1, NY):
        await_recv(ay_buf.at[d - 1], a2_send.at[d - 1], a2_recv.at[d - 1])
        total = total + ay_buf[d - 1].astype(F32)
    a_span = lambda kx, ky: fin.at[rows_at(x_at(kx) * A_PIECE + y_at(ky) * A_ROWS, A_ROWS), :]
    fin[rows_at(ix * A_PIECE + iy * A_ROWS, A_ROWS), :] = total.astype(BF16)
    for d in FAR:
        push(a_span(0, 0), a_span(0, 0), a3_send.at[d - 1], a3_recv.at[d - 1], to_y(d))
    for k in (2, 1, 3):
        push(a_span(0, 0), a_span(0, 0), a4_send.at[k - 1, 0], a4_recv.at[k - 1, 0], to_x(k))

    w_swap.finish()
    total = w_out[z].astype(F32)
    for k in range(1, NZ):
        total = total + w_in[lax.rem(z + k, NZ)].astype(F32)
    w_x[ix] = total.astype(BF16)
    x_swap = Swap(NX, ix, lambda t: {"dp": t * NY + iy}, wx_send, wx_recv)
    x_swap.start(lambda t: w_x.at[ix], w_x)

    for k in range(1, NX):
        await_recv(b_span(-k, 0), b3_send.at[k - 1], b3_recv.at[k - 1])
    b_line = lambda k: fin.at[rows_at(B_AT + y_at(k) * B_PIECE, B_PIECE), :]
    for d in FAR:
        push(b_line(0), b_line(0), b4_send.at[d - 1], b4_recv.at[d - 1], to_y(d))

    def a_forward(d):
        await_recv(a_span(0, -d), a3_send.at[d - 1], a3_recv.at[d - 1])
        for k in (2, 1, 3):
            push(a_span(0, -d), a_span(0, -d), a4_send.at[k - 1, d], a4_recv.at[k - 1, d], to_x(k))

    for d in NEAR[:4]:
        a_forward(d)
    x_swap.finish()
    total = w_x[0].astype(F32)
    for t in range(1, NX):
        total = total + w_x[t].astype(F32)
    w_y[iy] = total.astype(BF16)
    y_swap = Swap(NY, iy, lambda t: {"dp": ix * NY + t}, wy_send, wy_recv)
    y_swap.start(lambda t: w_y.at[iy], w_y)
    for d in NEAR[4:]:
        a_forward(d)

    for d in range(1, NY):
        await_recv(b_line(-d), b4_send.at[d - 1], b4_recv.at[d - 1])
    b_live = PLEN * PASS_DEV - B_AT
    b_out = pltpu.make_async_copy(
        fin.at[pl.ds(B_AT, b_live), :], cache_out.at[pl.ds(B_AT, b_live), :], out_sem.at[0]
    )
    b_out.start()
    for d in range(NY):
        for k in range(1, NX):
            await_recv(a_span(-k, -d), a4_send.at[k - 1, d], a4_recv.at[k - 1, d])
    a_out = pltpu.make_async_copy(
        fin.at[pl.ds(0, B_AT), :], cache_out.at[pl.ds(0, B_AT), :], out_sem.at[1]
    )
    a_out.start()
    y_swap.finish()
    total = w_y[0].astype(F32)
    for t in range(1, NY):
        total = total + w_y[t].astype(F32)
    wg_ref[...] = total

    q_pair.wait_send()
    w_pair.wait_send()
    for moved in (score_swap, q_swap, w_swap, x_swap, y_swap):
        moved.drain()
    for copy in sent:
        copy.wait_send()
    b_out.wait()
    a_out.wait()


def result_kernel(hid, wg, cache, hid_out, wg_out, cache_out, hid_buf, wg_buf, cache_buf, sems):
    part = PLEN * PASS_DEV // 4
    moves = []
    for n in range(4):
        span = pl.ds(n * part, part)
        moves.append((cache.at[span, :], cache_buf.at[span, :], cache_out.at[span, :]))
    moves += [(hid, hid_buf, hid_out), (wg, wg_buf, wg_out)]
    reads, writes = [], []
    for n, (src, mid, _) in enumerate(moves):
        reads.append(pltpu.make_async_copy(src, mid, sems.at[0, n]))
        reads[-1].start()
    for n, (_, mid, dst) in enumerate(moves):
        reads[n].wait()
        writes.append(pltpu.make_async_copy(mid, dst, sems.at[1, n]))
        writes[-1].start()
    for copy in writes:
        copy.wait()


VMEM = pl.BlockSpec(memory_space=pltpu.VMEM)
SMEM = pl.BlockSpec(memory_space=pltpu.SMEM)
ANY = pl.BlockSpec(memory_space=pl.ANY)


def call(kernel, collective_id, out_shape, in_specs, out_specs, scratch, args):
    return pl.pallas_call(
        kernel,
        out_shape=out_shape,
        in_specs=in_specs,
        out_specs=out_specs,
        scratch_shapes=scratch,
        compiler_params=pltpu.CompilerParams(
            collective_id=collective_id, has_side_effects=True, vmem_limit_bytes=56 * 2**20
        ),
    )(*args)


def shards(hidden, weight, cache, lengths, passage_ids, owner_map):
    width = hidden.shape[-1]
    share = width // OWNERS
    tokens = Q_DEV * QL
    shape = jax.ShapeDtypeStruct
    dma = pltpu.SemaphoreType.DMA
    vmem = pltpu.VMEM

    def pair(*sizes):
        return [dma(sizes), dma(sizes)]

    gather = [dma((2 * NZ - 1,)), dma((OWNERS,))]
    hidden = hidden.reshape(tokens, width)
    queries, full, raw, tab, hits, tiles = call(
        gather_kernel,
        0,
        [
            shape((OWNERS, tokens, DIM), BF16),
            shape((OWNERS, share, DIM), BF16),
            shape((tokens, DIM), F32),
            shape((8, SLOTS), I32),
            shape((SLOTS, 128), BF16),
            shape((PASS_DEV, ROWS, DIM), BF16),
        ],
        [ANY, VMEM, ANY, VMEM, VMEM],
        [ANY, ANY, VMEM, VMEM, VMEM, ANY],
        [
            vmem((tokens, width), BF16),
            vmem((PLEN, PASS_DEV, DIM), BF16),
            vmem((OWNERS, tokens, DIM), BF16),
            vmem((OWNERS, share, DIM), BF16),
            vmem((PASS_DEV, ROWS, DIM), BF16),
            vmem((OWNERS, 8, 128), F32),
            vmem((PLEN * PASS_DEV, DIM), F32),
            dma((2,)),
            dma,
            dma,
            dma((OWNERS,)),
        ]
        + gather
        + gather
        + gather,
        (hidden, weight, jnp.transpose(cache, (1, 0, 2)), passage_ids, owner_map.reshape(1, -1)),
    )
    scratch = [
        vmem((tokens, width), BF16),
        vmem((OWNERS, share, DIM), BF16),
        vmem((tokens, DIM), F32),
        vmem((PASS_DEV, ROWS, DIM), BF16),
        vmem((8, SLOTS), I32),
        vmem((SLOTS, 128), BF16),
        vmem((OWNERS * Q_DEV, QL, DIM), BF16),
        dma((7,)),
        vmem((FLAT, DIM), F32),
        vmem((GROUPS, ROWS, 128), F32),
        vmem((64, 128), F32),
        vmem((64, 128), F32),
        vmem((64, 128), F32),
        vmem((OWNERS, 8, 128), F32),
        vmem((8, SLOTS), F32),
        pltpu.SMEM((8, SLOTS), F32),
        vmem((GROUPS + 1, ROWS, DIM), F32),
        vmem((GROUPS, 4, QL, DIM), F32),
        vmem((ENTRIES, QL, DIM), F32),
        vmem((NZ, NC, tokens, DIM), BF16),
        vmem((FLAT, DIM), BF16),
        vmem((NX - 1, NY, A_ROWS, DIM), BF16),
        vmem((NY - 1, A_ROWS, DIM), BF16),
        vmem((NY - 1, B_PIECE, DIM), BF16),
        vmem((NX - 1, B_ROWS, DIM), BF16),
        vmem((NY, A_ROWS, DIM), BF16),
        vmem((B_PIECE, DIM), BF16),
        vmem((FLAT, DIM), BF16),
        vmem((NZ, tokens, DIM), BF16),
        vmem((NZ, tokens, DIM), BF16),
        vmem((NZ, tokens, DIM), BF16),
        vmem((NZ, NC, share, DIM), BF16),
        vmem((NZ, share, DIM), BF16),
        vmem((NZ, share, DIM), BF16),
        vmem((NZ, share, DIM), BF16),
        vmem((NX, share, DIM), BF16),
        vmem((NY, share, DIM), BF16),
        dma,
        dma((2,)),
    ]
    swap = lambda n: [dma((n - 1,)), dma((n,))]
    scratch += swap(OWNERS)
    scratch += [dma, dma] + swap(NZ) + [dma, dma] + swap(NZ) + swap(NX) + swap(NY)
    scratch += pair(NX - 1, NY) + pair(NY - 1) + pair(NY - 1) + pair(NX - 1, NY)
    scratch += pair(NY - 1) + pair(NX - 1) + pair(NX - 1) + pair(NY - 1)

    hid, wg, cache_grad = call(
        pair_kernel,
        1,
        [
            shape((tokens, width), BF16),
            shape((share, DIM), F32),
            shape((PLEN * PASS_DEV, DIM), BF16),
        ],
        [ANY, ANY, ANY, ANY, SMEM, SMEM, ANY, ANY, ANY],
        [VMEM, VMEM, ANY],
        scratch,
        (hidden, full, raw, tiles, lengths, tab, tab, hits, queries.reshape(OWNERS * Q_DEV, QL, DIM)),
    )
    hid, wg, cache_grad = pl.pallas_call(
        result_kernel,
        out_shape=[shape(x.shape, x.dtype) for x in (hid, wg, cache_grad)],
        in_specs=[ANY] * 3,
        out_specs=[ANY] * 3,
        scratch_shapes=[vmem(x.shape, x.dtype) for x in (hid, wg, cache_grad)] + [dma((2, 6))],
    )(hid, wg, cache_grad)
    cache_grad = jnp.transpose(cache_grad.reshape(PLEN, PASS_DEV, DIM), (1, 0, 2))
    return hid.reshape(Q_DEV, QL, width), wg, cache_grad


def solution(mesh):
    in_specs = (
        P(("dp", "passage"), None, None),
        P("passage", None),
        P("passage", None, None),
        P("passage"),
        P(("dp", "passage"), None),
        P(),
    )
    out_specs = (P(("dp", "passage"), None, None), P("passage", None), P("passage", None, None))
    return jax.shard_map(shards, mesh=mesh, in_specs=in_specs, out_specs=out_specs, check_vma=False)
```

```python
import functools
import math

import jax
import jax.numpy as jnp
from jax import lax
from jax.experimental import pallas as pl
from jax.experimental.pallas import tpu as pltpu
from jax.sharding import PartitionSpec as P

TAU = 0.1
EPS = 1e-06

NX, NY, NZ, NC = 4, 8, 8, 2
OWNERS = NZ * NC
Q_DEV, QL, CAND = 4, 32, 16
PASS_DEV, PLEN, ROWS = 16, 180, 192
DIM = 128
GROUPS = 60
SLOTS = 256
CAP = 12
PAIRS = Q_DEV * CAND
NEG = -1e30

F32, BF16, I32 = jnp.float32, jnp.bfloat16, jnp.int32


def dot(a, b):
    return jnp.dot(a, b, preferred_element_type=F32)


def dot_nt(a, b):
    return lax.dot_general(a, b, (((1,), (1,)), ((), ())), preferred_element_type=F32)


def dot_tn(a, b):
    return lax.dot_general(a, b, (((0,), (0,)), ((), ())), preferred_element_type=F32)


def iota(shape, axis):
    return lax.broadcasted_iota(I32, shape, axis)


def ind(cond, dtype=F32):
    return jnp.where(cond, 1.0, 0.0).astype(dtype)


def pieces(x):
    a = x.astype(BF16)
    rest = x - a.astype(F32)
    b = rest.astype(BF16)
    return (a, b, (rest - b.astype(F32)).astype(BF16))


class Place:
    def __init__(self):
        self.me = lax.axis_index("passage")
        self.z, self.c = self.me // NC, lax.rem(self.me, NC)
        self.sibling = self.z * NC + (1 - self.c)

    def ring(self, k):
        return lax.rem(self.z + k, NZ) * NC + self.c

    def ring_sibling(self, k):
        return lax.rem(self.z + k, NZ) * NC + (1 - self.c)


def remote(src, dst, send, recv, device):
    return pltpu.make_async_remote_copy(
        src_ref=src,
        dst_ref=dst,
        send_sem=send,
        recv_sem=recv,
        device_id=device,
        device_id_type=pl.DeviceIdType.MESH,
    )


NEAR = (1, 7, 2, 6, 3, 5, 4)


class Gather:
    def __init__(self, place, buf, send, recv):
        self.place, self.buf, self.send, self.recv = place, buf, send, recv
        self.sent, self.relayed = [], 0

    def copy(self, slot, n, peer):
        return remote(
            self.buf.at[slot], self.buf.at[slot], self.send.at[n], self.recv.at[slot],
            {"passage": peer},
        )

    def start(self):
        p = self.place
        for n, k in list(enumerate(NEAR))[::-1]:
            self.sent.append(self.copy(p.me, n, p.ring(k)))
            self.sent[-1].start()
        self.sent.append(self.copy(p.me, NZ - 1, p.sibling))
        self.sent[-1].start()

    def relay(self, upto):
        p = self.place
        for n in range(self.relayed, upto):
            forward = self.copy(p.ring(NEAR[n]), NZ + n, p.sibling)
            forward.wait_recv()
            forward.start()
            self.sent.append(forward)
        self.relayed = upto

    def finish(self):
        p = self.place
        self.relay(NZ - 1)
        self.copy(p.sibling, 0, p.sibling).wait_recv()
        for k in NEAR:
            self.copy(p.ring_sibling(k), 0, p.sibling).wait_recv()

    def drain(self):
        for copy in self.sent:
            copy.wait_send()


FAR = (4, 3, 5, 2, 6, 1, 7)
A_ROWS, B_ROWS = 64, 32
A_PIECE, B_PIECE = NY * A_ROWS, NX * B_ROWS
B_AT = NX * A_PIECE
FLAT = PASS_DEV * ROWS


def rows_at(start, count):
    return pl.ds(pl.multiple_of(start, 16), count)


class Swap:
    def __init__(self, n, at, device, send, recv):
        self.n, self.at, self.device, self.send, self.recv = n, at, device, send, recv

    def start(self, src_of, buf):
        self.buf, self.copies = buf, []
        far = sorted(range(1, self.n), key=lambda k: -min(k, self.n - k))
        for k in far:
            t = lax.rem(self.at + k, self.n)
            copy = remote(
                src_of(t), buf.at[self.at], self.send.at[k - 1], self.recv.at[self.at], self.device(t)
            )
            copy.start()
            self.copies.append(copy)

    def finish(self):
        for k in range(1, self.n):
            t = lax.rem(self.at + k, self.n)
            remote(
                self.buf.at[t], self.buf.at[t], self.send.at[0], self.recv.at[t], self.device(t)
            ).wait_recv()

    def drain(self):
        for copy in self.copies:
            copy.wait_send()


def pair_kernel(
    hidden_hbm, weight_ref, cache_hbm, len_ref, ids, owner_of,
    hid_ref, wg_ref, cache_out,
    hidden_ref, cache_ref, query_ref, full_ref, tiles, rows_buf, rows_vec, rows_tab, count_vec, count_tab,
    tab_vec, tab, last_tab,
    cache_f, exps, logs, recips, scales,
    score_buf, grad_vec, grad_tab, cg_run, qg_group, qg_ref, cg_ref,
    ax_buf, ay_buf, by_buf, bx_buf, mid_a, mid_b, fin, q_sib, q_out, q_in, w_own, w_sib, w_out, w_in, w_x, w_y,
    in_sem, tab_sem, grad_sem, out_sem,
    w_send, w_recv, r_send, r_recv, q_send, q_recv, s_send, s_recv,
    qs_send, qs_recv, qz_send, qz_recv, ws_send, ws_recv, wz_send, wz_recv, wx_send, wx_recv, wy_send, wy_recv,
    a1_send, a1_recv, a2_send, a2_recv, a3_send, a3_recv, a4_send, a4_recv,
    b1_send, b1_recv, b2_send, b2_recv, b3_send, b3_recv, b4_send, b4_recv,
):
    place = Place()
    me, z, c = place.me, place.z, place.c
    dp = lax.axis_index("dp")
    ix, iy = dp // NY, lax.rem(dp, NY)
    others = [lax.rem(me + k, OWNERS) for k in range(1, OWNERS)]
    to_x = lambda k: {"dp": lax.rem(ix + k, NX) * NY + iy}
    to_y = lambda k: {"dp": ix * NY + lax.rem(iy + k, NY)}
    sibling = {"passage": place.sibling}
    similarity_scale = 1.0 / (TAU * math.sqrt(DIM))
    root_scale = 1.0 / math.sqrt(DIM)

    barrier = pltpu.get_barrier_semaphore()
    peers = [{"passage": d} for d in others]
    peers += [to_x(k) for k in range(1, NX)] + [to_y(k) for k in range(1, NY)]
    for device in peers:
        pl.semaphore_signal(barrier, inc=1, device_id=device, device_id_type=pl.DeviceIdType.MESH)
    hidden_in = pltpu.make_async_copy(hidden_hbm, hidden_ref, in_sem.at[0])
    cache_in = pltpu.make_async_copy(cache_hbm, cache_ref, in_sem.at[1])
    hidden_in.start()
    cache_in.start()

    def bounded(value, most):
        return jnp.minimum(jnp.maximum(value, 0), most)

    full_ref[me] = weight_ref[...]
    lane = iota((8, 128), 1)
    mine = jnp.full((8, 128), -1, I32)
    for q in range(Q_DEV):
        for n in range(CAND):
            row = owner_of[bounded(ids[q, n], OWNERS * PASS_DEV - 1)]
            mine = jnp.where(lane == CAND * q + n, row, mine)
    rows_buf[me] = mine
    pl.semaphore_wait(barrier, len(peers))
    weights = Gather(place, full_ref, w_send, w_recv)
    weights.start()
    rows = Gather(place, rows_buf, r_send, r_recv)
    rows.start()

    cache_in.wait()
    cache_f[0 : PLEN * PASS_DEV, :] = cache_ref[...].reshape(PLEN * PASS_DEV, DIM).astype(F32)
    for r in range(PASS_DEV):
        tiles[r, ROWS - 16 : ROWS] = jnp.zeros((16, DIM), BF16)
        tiles[r, 0:PLEN] = cache_f[pl.ds(r, PLEN, stride=PASS_DEV), :].astype(BF16)
    logs[...] = jnp.zeros_like(logs)
    recips[...] = jnp.zeros_like(recips)

    hidden_in.wait()
    weights.finish()
    raw = dot(hidden_ref[...], full_ref[...].reshape(-1, DIM))
    inverse = lax.rsqrt(jnp.mean(raw * raw, axis=-1, keepdims=True) + EPS)
    vectors = (raw * inverse).astype(BF16)
    query_ref[me] = vectors.reshape(Q_DEV, QL, DIM)
    queries = Gather(place, query_ref, q_send, q_recv)
    queries.start()

    rows.finish()
    for d in range(OWNERS):
        rows_vec[d : d + 1, :] = rows_buf[d, 0:1, :]
    to_rows = pltpu.make_async_copy(rows_vec, rows_tab, tab_sem.at[0])
    to_rows.start()
    to_rows.wait()
    first_row = PASS_DEV * me

    def count_pairs(d, counts):
        for n in range(PAIRS):
            counts = counts + jnp.where(lane == rows_tab[d, n] - first_row, 1, 0)
        return counts

    count_vec[...] = lax.fori_loop(0, OWNERS, count_pairs, jnp.zeros((8, 128), I32))
    to_count = pltpu.make_async_copy(count_vec, count_tab, tab_sem.at[1])
    to_count.start()
    queries.relay(2)
    to_count.wait()
    starts = [0]
    for r in range(PASS_DEV):
        number = count_tab[0, r]
        starts.append(starts[-1] + ((number + 3) >> 2))
        last_tab[r] = jnp.where(number > 0, starts[-1] - 1, -1)
    slot = iota((8, 128), 0) * 128 + lane
    group = slot & 63
    slot_row = jnp.zeros((8, 128), I32)
    for r in range(1, PASS_DEV):
        slot_row = slot_row + jnp.where(group >= starts[r], 1, 0)
    slot_start = jnp.zeros((8, 128), I32)
    for r in range(1, PASS_DEV):
        slot_start = jnp.where(slot_row == r, starts[r], slot_start)
    slot_rank = 4 * (group - slot_start) + (slot >> 6)

    def place_pairs(d, carry):
        seen, at_slot, at_entry = carry
        entry = CAND * d
        for n in range(PAIRS):
            row = rows_tab[d, n] - first_row
            pair = PAIRS * d + n
            same = slot_row == row
            at_slot = jnp.where(same & (slot_rank == seen), pair, at_slot)
            seen = seen + jnp.where(same, 1, 0)
            own = (row >= 0) & (row < PASS_DEV)
            at_entry = jnp.where(slot == jnp.where(own, entry, -1), pair, at_entry)
            entry = entry + jnp.where(own, 1, 0)
        return seen, at_slot, at_entry

    none = jnp.full((8, 128), -1, I32)
    _, at_slot, at_entry = lax.fori_loop(
        0, OWNERS, place_pairs, (jnp.zeros((8, 128), I32), none, none - 1)
    )
    tab_vec[0] = at_slot
    tab_vec[1] = slot_row
    tab_vec[2] = at_entry
    to_tab = pltpu.make_async_copy(tab_vec.at[pl.ds(0, 3)], tab.at[pl.ds(0, 3)], tab_sem.at[2])
    to_tab.start()
    queries.relay(6)
    to_tab.wait()

    def place_entries(i, spots):
        for u in range(16):
            s = 16 * i + u
            pair = tab[0, s // 128, lax.rem(s, 128)]
            spots = jnp.where(at_entry == pair, 4 * lax.rem(s, 64) + s // 64, spots)
        return spots

    tab_vec[3] = lax.fori_loop(0, SLOTS // 16, place_entries, jnp.zeros((8, 128), I32))
    to_spots = pltpu.make_async_copy(tab_vec.at[3], tab.at[3], tab_sem.at[3])
    to_spots.start()
    queries.finish()
    to_spots.wait()

    def row_of(g):
        return bounded(tab[1, 0, g], PASS_DEV - 1)

    def load_queries(g):
        parts = []
        for j in range(4):
            pair = tab[0, j // 2, 64 * (j % 2) + g]
            query = bounded(pair >> 4, OWNERS * Q_DEV - 1)
            parts.append(query_ref[query >> 2, query & (Q_DEV - 1)])
        return jnp.concatenate(parts, axis=0)

    live = iota((ROWS, 128), 0)

    def forward(i, _):
        for u in range(4):
            g = 4 * i + u
            row = row_of(g)
            sims = dot_nt(tiles[row], load_queries(g)) * similarity_scale
            sims = jnp.where(live < len_ref[row], sims, NEG)
            top = jnp.max(sims, axis=0, keepdims=True)
            e = jnp.exp(sims - top)
            total = jnp.sum(e, axis=0, keepdims=True)
            exps[g] = e
            logs[pl.ds(g, 1), :] = top + jnp.log(total)
            recips[pl.ds(g, 1), :] = 1.0 / total
        return 0

    lax.fori_loop(0, GROUPS // 4, forward, 0)

    of_place = iota((SLOTS, 128), 1) // QL == iota((SLOTS, 128), 0) // 64
    spread = jnp.where(of_place, jnp.concatenate([logs[...]] * 4, axis=0), 0.0)
    one8 = jnp.ones((8, 128), BF16)
    score_row = TAU * sum(dot_nt(one8, part) for part in pieces(spread))
    pair = jnp.concatenate([at_slot[0:1], at_slot[1:2]], axis=1)
    is_cand = ind((iota((CAND, SLOTS), 0) == (pair & (CAND - 1))) & (pair >= 0))
    lane_of = ((pair >> 6) << 3) + ((pair >> 4) & (Q_DEV - 1))
    hits = ind((iota((128, SLOTS), 0) == lane_of) & (pair >= 0), BF16)
    mine = sum(
        dot_nt((is_cand * part[0:1].astype(F32)).astype(BF16), hits) for part in pieces(score_row)
    )
    score_buf[me] = mine[0:8] + pltpu.roll(mine[8:16], 4, 1)
    score_swap = Swap(OWNERS, me, lambda t: {"passage": t}, s_send, s_recv)
    score_swap.start(lambda t: score_buf.at[me], score_buf)

    def products(i, _):
        for u in range(4):
            g = 4 * i + u
            w = (exps[g] * recips[pl.ds(g, 1), :]).astype(BF16)
            qg_group[g] = dot_tn(w, tiles[row_of(g)]).reshape(4, QL, DIM)
        return 0

    lax.fori_loop(0, GROUPS // 4, products, 0)

    score_swap.finish()
    scores = score_buf[0]
    for d in range(1, OWNERS):
        scores = scores + score_buf[d]
    low = lax.rem(lane, 8) < Q_DEV

    def both(x, op):
        return op(x, jnp.where(low, pltpu.roll(x, 124, 1), pltpu.roll(x, 4, 1)))

    top = both(jnp.broadcast_to(jnp.max(scores, axis=0, keepdims=True), (8, 128)), jnp.maximum)
    e = jnp.exp(scores - top)
    total = both(jnp.broadcast_to(jnp.sum(e, axis=0, keepdims=True), (8, 128)), jnp.add)
    grad = e / total - ind((iota((8, 128), 0) == 0) & low)
    grad = jnp.concatenate(
        [jnp.where(low, grad, 0.0), jnp.where(low, pltpu.roll(grad, 124, 1), 0.0)], axis=0
    )
    grad_row = is_cand * sum(dot(part, hits) for part in pieces(grad))
    grad_row = jnp.sum(grad_row, axis=0, keepdims=True)
    grad_vec[...] = jnp.broadcast_to(grad_row * root_scale, (8, SLOTS))
    grad_copy = pltpu.make_async_copy(grad_vec, grad_tab, grad_sem)
    grad_copy.start()
    same_group = ind(lax.rem(iota((64, SLOTS), 1), 64) == iota((64, SLOTS), 0))
    to_lanes = ind(of_place, BF16)
    by_lane = sum(dot(part, to_lanes) for part in pieces(same_group * grad_row))
    scales[...] = by_lane * recips[...] * root_scale
    grad_copy.wait()

    def sum_device(d, _):
        sums = [jnp.zeros((QL, DIM), F32) for _ in range(Q_DEV)]
        for n in range(CAP):
            sub, spot_lane = d // 8, CAND * lax.rem(d, 8) + n
            pair = tab[2, sub, spot_lane]
            at = bounded(tab[3, sub, spot_lane], 4 * GROUPS - 1)
            part = qg_group[at >> 2, at & 3]
            grad = grad_tab[0, 64 * (at & 3) + (at >> 2)]
            for q in range(Q_DEV):
                one = jnp.where((pair >= 0) & (((pair >> 4) & (Q_DEV - 1)) == q), grad, 0.0)
                sums[q] = sums[q] + part * one
        for q in range(Q_DEV):
            qg_ref[d // NC, lax.rem(d, NC), q * QL : (q + 1) * QL, :] = sums[q].astype(BF16)
        return 0

    lax.fori_loop(0, OWNERS, sum_device, 0)
    q_pair = remote(qg_ref.at[:, 1 - c], q_sib, qs_send, qs_recv, sibling)
    q_pair.start()

    def cache_step(i, run):
        for u in range(4):
            g = 4 * i + u
            row = row_of(g)
            w = (exps[g] * scales[pl.ds(g, 1), :]).astype(BF16)
            again = (row == row_of(jnp.maximum(g - 1, 0))) & (g > 0)
            cg_run[g + 1] = jnp.where(again, cg_run[g], 0.0) + dot(w, load_queries(g))
        return run

    lax.fori_loop(0, 4, cache_step, 0)
    q_pair.wait_recv()
    for t in range(NZ):
        q_out[t] = (qg_ref[t, c].astype(F32) + q_sib[t].astype(F32)).astype(BF16)
    on_z = lambda t: {"passage": t * NC + c}
    q_swap = Swap(NZ, z, on_z, qz_send, qz_recv)
    q_swap.start(lambda t: q_out.at[t], q_in)
    lax.fori_loop(4, GROUPS // 4, cache_step, 0)

    for r in range(PASS_DEV):
        last = last_tab[r]
        value = jnp.where(last >= 0, cg_run[bounded(last, GROUPS - 1) + 1], 0.0)
        cache_f[pl.ds(r, ROWS, stride=PASS_DEV), :] = value
    cg_ref[...] = cache_f[...].astype(BF16)

    sent = []

    def push(src, dst, send, recv, device):
        copy = remote(src, dst, send, recv, device)
        copy.start()
        sent.append(copy)

    def await_recv(dst, send, recv):
        remote(dst, dst, send, recv, sibling).wait_recv()

    def y_at(k):
        return lax.rem(iy + k + NY, NY)

    def x_at(k):
        return lax.rem(ix + k + NX, NX)

    for k in FAR:
        src = cg_ref.at[rows_at(B_AT + y_at(k) * B_PIECE, B_PIECE), :]
        push(src, by_buf.at[k - 1], b1_send.at[k - 1], b1_recv.at[k - 1], to_y(k))
    for d in FAR + (0,):
        for k in (2, 1, 3):
            src = cg_ref.at[rows_at(x_at(k) * A_PIECE + y_at(d) * A_ROWS, A_ROWS), :]
            push(src, ax_buf.at[k - 1, d], a1_send.at[k - 1, d], a1_recv.at[k - 1, d], to_x(k))

    q_swap.finish()
    query_gradient = q_out[z].astype(F32)
    for k in range(1, NZ):
        query_gradient = query_gradient + q_in[lax.rem(z + k, NZ)].astype(F32)
    inverse = lax.rsqrt(jnp.mean(raw * raw, axis=-1, keepdims=True) + EPS)
    mean_term = jnp.mean(query_gradient * raw, axis=-1, keepdims=True)
    raw_grad = (
        inverse * query_gradient - raw * (inverse * inverse * inverse) * mean_term
    ).astype(BF16)
    weight_part = dot_tn(hidden_ref[...], raw_grad)
    w_own[...] = weight_part.astype(BF16).reshape(w_own.shape)
    w_pair = remote(w_own.at[:, 1 - c], w_sib, ws_send, ws_recv, sibling)
    w_pair.start()

    def a_first(d):
        total = cg_ref[rows_at(ix * A_PIECE + y_at(d) * A_ROWS, A_ROWS), :].astype(F32)
        for k in range(1, NX):
            await_recv(ax_buf.at[k - 1, d], a1_send.at[k - 1, d], a1_recv.at[k - 1, d])
            total = total + ax_buf[k - 1, d].astype(F32)
        mid_a[d] = total.astype(BF16)
        if d:
            push(mid_a.at[d], ay_buf.at[d - 1], a2_send.at[d - 1], a2_recv.at[d - 1], to_y(d))

    for d in FAR[:4]:
        a_first(d)
    w_pair.wait_recv()
    for t in range(NZ):
        w_out[t] = (w_own[t, c].astype(F32) + w_sib[t].astype(F32)).astype(BF16)
    w_swap = Swap(NZ, z, on_z, wz_send, wz_recv)
    w_swap.start(lambda t: w_out.at[t], w_in)
    for d in FAR[4:] + (0,):
        a_first(d)
    hid_ref[...] = dot_nt(raw_grad, full_ref[...].reshape(-1, DIM)).astype(BF16)

    total = cg_ref[rows_at(B_AT + iy * B_PIECE, B_PIECE), :].astype(F32)
    for k in range(1, NY):
        await_recv(by_buf.at[k - 1], b1_send.at[k - 1], b1_recv.at[k - 1])
        total = total + by_buf[k - 1].astype(F32)
    mid_b[...] = total.astype(BF16)
    for k in (2, 1, 3):
        src = mid_b.at[rows_at(x_at(k) * B_ROWS, B_ROWS), :]
        push(src, bx_buf.at[k - 1], b2_send.at[k - 1], b2_recv.at[k - 1], to_x(k))
    total = mid_b[rows_at(ix * B_ROWS, B_ROWS), :].astype(F32)
    for k in range(1, NX):
        await_recv(bx_buf.at[k - 1], b2_send.at[k - 1], b2_recv.at[k - 1])
        total = total + bx_buf[k - 1].astype(F32)
    b_span = lambda kx, ky: fin.at[rows_at(B_AT + y_at(ky) * B_PIECE + x_at(kx) * B_ROWS, B_ROWS), :]
    fin[rows_at(B_AT + iy * B_PIECE + ix * B_ROWS, B_ROWS), :] = total.astype(BF16)
    for k in (2, 1, 3):
        push(b_span(0, 0), b_span(0, 0), b3_send.at[k - 1], b3_recv.at[k - 1], to_x(k))

    total = mid_a[0].astype(F32)
    for d in range(1, NY):
        await_recv(ay_buf.at[d - 1], a2_send.at[d - 1], a2_recv.at[d - 1])
        total = total + ay_buf[d - 1].astype(F32)
    a_span = lambda kx, ky: fin.at[rows_at(x_at(kx) * A_PIECE + y_at(ky) * A_ROWS, A_ROWS), :]
    fin[rows_at(ix * A_PIECE + iy * A_ROWS, A_ROWS), :] = total.astype(BF16)
    for d in FAR:
        push(a_span(0, 0), a_span(0, 0), a3_send.at[d - 1], a3_recv.at[d - 1], to_y(d))
    for k in (2, 1, 3):
        push(a_span(0, 0), a_span(0, 0), a4_send.at[k - 1, 0], a4_recv.at[k - 1, 0], to_x(k))

    w_swap.finish()
    total = w_out[z].astype(F32)
    for k in range(1, NZ):
        total = total + w_in[lax.rem(z + k, NZ)].astype(F32)
    w_x[ix] = total.astype(BF16)
    x_swap = Swap(NX, ix, lambda t: {"dp": t * NY + iy}, wx_send, wx_recv)
    x_swap.start(lambda t: w_x.at[ix], w_x)

    for k in range(1, NX):
        await_recv(b_span(-k, 0), b3_send.at[k - 1], b3_recv.at[k - 1])
    b_line = lambda k: fin.at[rows_at(B_AT + y_at(k) * B_PIECE, B_PIECE), :]
    for d in FAR:
        push(b_line(0), b_line(0), b4_send.at[d - 1], b4_recv.at[d - 1], to_y(d))

    def a_forward(d):
        await_recv(a_span(0, -d), a3_send.at[d - 1], a3_recv.at[d - 1])
        for k in (2, 1, 3):
            push(a_span(0, -d), a_span(0, -d), a4_send.at[k - 1, d], a4_recv.at[k - 1, d], to_x(k))

    for d in NEAR[:4]:
        a_forward(d)
    x_swap.finish()
    total = w_x[0].astype(F32)
    for t in range(1, NX):
        total = total + w_x[t].astype(F32)
    w_y[iy] = total.astype(BF16)
    y_swap = Swap(NY, iy, lambda t: {"dp": ix * NY + t}, wy_send, wy_recv)
    y_swap.start(lambda t: w_y.at[iy], w_y)
    for d in NEAR[4:]:
        a_forward(d)

    for d in range(1, NY):
        await_recv(b_line(-d), b4_send.at[d - 1], b4_recv.at[d - 1])
    b_live = PLEN * PASS_DEV - B_AT
    b_out = pltpu.make_async_copy(
        fin.at[pl.ds(B_AT, b_live), :], cache_out.at[pl.ds(B_AT, b_live), :], out_sem.at[0]
    )
    b_out.start()
    for d in range(NY):
        for k in range(1, NX):
            await_recv(a_span(-k, -d), a4_send.at[k - 1, d], a4_recv.at[k - 1, d])
    a_out = pltpu.make_async_copy(
        fin.at[pl.ds(0, B_AT), :], cache_out.at[pl.ds(0, B_AT), :], out_sem.at[1]
    )
    a_out.start()
    y_swap.finish()
    total = w_y[0].astype(F32)
    for t in range(1, NY):
        total = total + w_y[t].astype(F32)
    wg_ref[...] = total

    q_pair.wait_send()
    w_pair.wait_send()
    for moved in (weights, rows, queries, score_swap, q_swap, w_swap, x_swap, y_swap):
        moved.drain()
    for copy in sent:
        copy.wait_send()
    b_out.wait()
    a_out.wait()


def result_kernel(hid, wg, cache, hid_out, wg_out, cache_out, hid_buf, wg_buf, cache_buf, sems):
    part = PLEN * PASS_DEV // 4
    moves = []
    for n in range(4):
        span = pl.ds(n * part, part)
        moves.append((cache.at[span, :], cache_buf.at[span, :], cache_out.at[span, :]))
    moves += [(hid, hid_buf, hid_out), (wg, wg_buf, wg_out)]
    reads, writes = [], []
    for n, (src, mid, _) in enumerate(moves):
        reads.append(pltpu.make_async_copy(src, mid, sems.at[0, n]))
        reads[-1].start()
    for n, (_, mid, dst) in enumerate(moves):
        reads[n].wait()
        writes.append(pltpu.make_async_copy(mid, dst, sems.at[1, n]))
        writes[-1].start()
    for copy in writes:
        copy.wait()


VMEM = pl.BlockSpec(memory_space=pltpu.VMEM)
SMEM = pl.BlockSpec(memory_space=pltpu.SMEM)
ANY = pl.BlockSpec(memory_space=pl.ANY)


def call(kernel, collective_id, out_shape, in_specs, out_specs, scratch, args):
    return pl.pallas_call(
        kernel,
        out_shape=out_shape,
        in_specs=in_specs,
        out_specs=out_specs,
        scratch_shapes=scratch,
        compiler_params=pltpu.CompilerParams(
            collective_id=collective_id, has_side_effects=True, vmem_limit_bytes=56 * 2**20
        ),
    )(*args)


def shards(hidden, weight, cache, lengths, passage_ids, owner_map):
    width = hidden.shape[-1]
    share = width // OWNERS
    tokens = Q_DEV * QL
    shape = jax.ShapeDtypeStruct
    dma = pltpu.SemaphoreType.DMA
    vmem = pltpu.VMEM

    def pair(*sizes):
        return [dma(sizes), dma(sizes)]

    scratch = [
        vmem((tokens, width), BF16),
        vmem((PLEN, PASS_DEV, DIM), BF16),
        vmem((OWNERS, Q_DEV, QL, DIM), BF16),
        vmem((OWNERS, share, DIM), BF16),
        vmem((PASS_DEV, ROWS, DIM), BF16),
        vmem((OWNERS, 8, 128), I32),
        vmem((OWNERS, 128), I32),
        pltpu.SMEM((OWNERS, 128), I32),
        vmem((8, 128), I32),
        pltpu.SMEM((8, 128), I32),
        vmem((4, 8, 128), I32),
        pltpu.SMEM((4, 8, 128), I32),
        pltpu.SMEM((PASS_DEV,), I32),
        vmem((FLAT, DIM), F32),
        vmem((GROUPS, ROWS, 128), F32),
        vmem((64, 128), F32),
        vmem((64, 128), F32),
        vmem((64, 128), F32),
        vmem((OWNERS, 8, 128), F32),
        vmem((8, SLOTS), F32),
        pltpu.SMEM((8, SLOTS), F32),
        vmem((GROUPS + 1, ROWS, DIM), F32),
        vmem((GROUPS, 4, QL, DIM), F32),
        vmem((NZ, NC, tokens, DIM), BF16),
        vmem((FLAT, DIM), BF16),
        vmem((NX - 1, NY, A_ROWS, DIM), BF16),
        vmem((NY - 1, A_ROWS, DIM), BF16),
        vmem((NY - 1, B_PIECE, DIM), BF16),
        vmem((NX - 1, B_ROWS, DIM), BF16),
        vmem((NY, A_ROWS, DIM), BF16),
        vmem((B_PIECE, DIM), BF16),
        vmem((FLAT, DIM), BF16),
        vmem((NZ, tokens, DIM), BF16),
        vmem((NZ, tokens, DIM), BF16),
        vmem((NZ, tokens, DIM), BF16),
        vmem((NZ, NC, share, DIM), BF16),
        vmem((NZ, share, DIM), BF16),
        vmem((NZ, share, DIM), BF16),
        vmem((NZ, share, DIM), BF16),
        vmem((NX, share, DIM), BF16),
        vmem((NY, share, DIM), BF16),
        dma((2,)),
        dma((4,)),
        dma,
        dma((2,)),
    ]
    gather = [dma((2 * NZ - 1,)), dma((OWNERS,))]
    swap = lambda n: [dma((n - 1,)), dma((n,))]
    scratch += gather + gather + gather + swap(OWNERS)
    scratch += [dma, dma] + swap(NZ) + [dma, dma] + swap(NZ) + swap(NX) + swap(NY)
    scratch += pair(NX - 1, NY) + pair(NY - 1) + pair(NY - 1) + pair(NX - 1, NY)
    scratch += pair(NY - 1) + pair(NX - 1) + pair(NX - 1) + pair(NY - 1)

    hid, wg, cache_grad = call(
        pair_kernel,
        0,
        [
            shape((tokens, width), BF16),
            shape((share, DIM), F32),
            shape((PLEN * PASS_DEV, DIM), BF16),
        ],
        [ANY, VMEM, ANY, SMEM, SMEM, SMEM],
        [VMEM, VMEM, ANY],
        scratch,
        (
            hidden.reshape(tokens, width),
            weight,
            jnp.transpose(cache, (1, 0, 2)),
            lengths,
            passage_ids,
            owner_map,
        ),
    )
    hid, wg, cache_grad = pl.pallas_call(
        result_kernel,
        out_shape=[shape(x.shape, x.dtype) for x in (hid, wg, cache_grad)],
        in_specs=[ANY] * 3,
        out_specs=[ANY] * 3,
        scratch_shapes=[vmem(x.shape, x.dtype) for x in (hid, wg, cache_grad)] + [dma((2, 6))],
    )(hid, wg, cache_grad)
    cache_grad = jnp.transpose(cache_grad.reshape(PLEN, PASS_DEV, DIM), (1, 0, 2))
    return hid.reshape(Q_DEV, QL, width), wg, cache_grad


def solution(mesh):
    in_specs = (
        P(("dp", "passage"), None, None),
        P("passage", None),
        P("passage", None, None),
        P("passage"),
        P(("dp", "passage"), None),
        P(),
    )
    out_specs = (P(("dp", "passage"), None, None), P("passage", None), P("passage", None, None))
    return jax.shard_map(shards, mesh=mesh, in_specs=in_specs, out_specs=out_specs, check_vma=False)
```

```python
import functools
import math

import jax
import jax.numpy as jnp
from jax import lax
from jax.experimental import pallas as pl
from jax.experimental.pallas import tpu as pltpu
from jax.sharding import PartitionSpec as P

TAU = 0.1
EPS = 1e-06

NX, NY, NZ, NC = 4, 8, 8, 2
OWNERS = NZ * NC
Q_DEV, QL, CAND = 4, 32, 16
PASS_DEV, PLEN, ROWS = 16, 180, 192
DIM = 128
GROUPS = 60
SLOTS = 256
CAP = 12
PAIRS = Q_DEV * CAND
NEG = -1e30

F32, BF16, I32 = jnp.float32, jnp.bfloat16, jnp.int32


def dot(a, b):
    return jnp.dot(a, b, preferred_element_type=F32)


def dot_nt(a, b):
    return lax.dot_general(a, b, (((1,), (1,)), ((), ())), preferred_element_type=F32)


def dot_tn(a, b):
    return lax.dot_general(a, b, (((0,), (0,)), ((), ())), preferred_element_type=F32)


def iota(shape, axis):
    return lax.broadcasted_iota(I32, shape, axis)


def ind(cond, dtype=F32):
    return jnp.where(cond, 1.0, 0.0).astype(dtype)


def pieces(x):
    a = x.astype(BF16)
    rest = x - a.astype(F32)
    b = rest.astype(BF16)
    return (a, b, (rest - b.astype(F32)).astype(BF16))


class Place:
    def __init__(self):
        self.me = lax.axis_index("passage")
        self.z, self.c = self.me >> 1, self.me & (NC - 1)
        self.sibling = self.z * NC + (1 - self.c)

    def ring(self, k):
        return ((self.z + k) & (NZ - 1)) * NC + self.c

    def ring_sibling(self, k):
        return ((self.z + k) & (NZ - 1)) * NC + (1 - self.c)


def remote(src, dst, send, recv, device):
    return pltpu.make_async_remote_copy(
        src_ref=src,
        dst_ref=dst,
        send_sem=send,
        recv_sem=recv,
        device_id=device,
        device_id_type=pl.DeviceIdType.MESH,
    )


NEAR = (1, 7, 2, 6, 3, 5, 4)


class Gather:
    def __init__(self, place, buf, send, recv):
        self.place, self.buf, self.send, self.recv = place, buf, send, recv
        self.sent, self.relayed = [], 0

    def copy(self, slot, n, peer):
        return remote(
            self.buf.at[slot], self.buf.at[slot], self.send.at[n], self.recv.at[slot],
            {"passage": peer},
        )

    def start(self):
        p = self.place
        for n, k in list(enumerate(NEAR))[::-1]:
            self.sent.append(self.copy(p.me, n, p.ring(k)))
            self.sent[-1].start()
        self.sent.append(self.copy(p.me, NZ - 1, p.sibling))
        self.sent[-1].start()

    def relay(self, upto):
        p = self.place
        for n in range(self.relayed, upto):
            forward = self.copy(p.ring(NEAR[n]), NZ + n, p.sibling)
            forward.wait_recv()
            forward.start()
            self.sent.append(forward)
        self.relayed = upto

    def finish(self):
        p = self.place
        self.relay(NZ - 1)
        self.copy(p.sibling, 0, p.sibling).wait_recv()
        for k in NEAR:
            self.copy(p.ring_sibling(k), 0, p.sibling).wait_recv()

    def drain(self):
        for copy in self.sent:
            copy.wait_send()


FAR = (4, 3, 5, 2, 6, 1, 7)
A_ROWS, B_ROWS = 64, 32
A_PIECE, B_PIECE = NY * A_ROWS, NX * B_ROWS
B_AT = NX * A_PIECE
FLAT = PASS_DEV * ROWS


def rows_at(start, count):
    return pl.ds(pl.multiple_of(start, 16), count)


class Swap:
    def __init__(self, n, at, device, send, recv):
        self.n, self.at, self.device, self.send, self.recv = n, at, device, send, recv

    def start(self, src_of, buf):
        self.buf, self.copies = buf, []
        far = sorted(range(1, self.n), key=lambda k: -min(k, self.n - k))
        for k in far:
            t = (self.at + k) & (self.n - 1)
            copy = remote(
                src_of(t), buf.at[self.at], self.send.at[k - 1], self.recv.at[self.at], self.device(t)
            )
            copy.start()
            self.copies.append(copy)

    def finish(self):
        for k in range(1, self.n):
            t = (self.at + k) & (self.n - 1)
            remote(
                self.buf.at[t], self.buf.at[t], self.send.at[0], self.recv.at[t], self.device(t)
            ).wait_recv()

    def drain(self):
        for copy in self.copies:
            copy.wait_send()


def pair_kernel(
    hidden_hbm, weight_ref, cache_hbm, len_ref, ids, owner_of,
    hid_ref, wg_ref, cache_out,
    hidden_ref, cache_ref, query_ref, full_ref, tiles, rows_buf, rows_vec, rows_tab,
    tab_vec, tab,
    cache_f, exps, logs, recips, scales,
    score_buf, grad_vec, grad_tab, cg_run, qg_group, qg_ref, cg_ref,
    ax_buf, ay_buf, by_buf, bx_buf, mid_a, mid_b, fin, q_sib, q_out, q_in, w_own, w_sib, w_out, w_in, w_x, w_y,
    in_sem, tab_sem, grad_sem, out_sem,
    w_send, w_recv, r_send, r_recv, q_send, q_recv, s_send, s_recv,
    qs_send, qs_recv, qz_send, qz_recv, ws_send, ws_recv, wz_send, wz_recv, wx_send, wx_recv, wy_send, wy_recv,
    a1_send, a1_recv, a2_send, a2_recv, a3_send, a3_recv, a4_send, a4_recv,
    b1_send, b1_recv, b2_send, b2_recv, b3_send, b3_recv, b4_send, b4_recv,
):
    place = Place()
    me, z, c = place.me, place.z, place.c
    dp = lax.axis_index("dp")
    ix, iy = dp >> 3, dp & (NY - 1)
    others = [(me + k) & (OWNERS - 1) for k in range(1, OWNERS)]
    to_x = lambda k: {"dp": ((ix + k) & (NX - 1)) * NY + iy}
    to_y = lambda k: {"dp": ix * NY + ((iy + k) & (NY - 1))}
    sibling = {"passage": place.sibling}
    similarity_scale = 1.0 / (TAU * math.sqrt(DIM))
    root_scale = 1.0 / math.sqrt(DIM)

    barrier = pltpu.get_barrier_semaphore()
    peers = [{"passage": d} for d in others]
    peers += [to_x(k) for k in range(1, NX)] + [to_y(k) for k in range(1, NY)]
    for device in peers:
        pl.semaphore_signal(barrier, inc=1, device_id=device, device_id_type=pl.DeviceIdType.MESH)
    hidden_in = pltpu.make_async_copy(hidden_hbm, hidden_ref, in_sem.at[0])
    cache_in = pltpu.make_async_copy(cache_hbm, cache_ref, in_sem.at[1])
    hidden_in.start()
    cache_in.start()

    def bounded(value, most):
        return jnp.minimum(jnp.maximum(value, 0), most)

    full_ref[me] = weight_ref[...]
    lane = iota((8, 128), 1)
    slot = iota((8, 128), 0) * 128 + lane
    mine = jnp.full((8, 128), -1, I32)
    listed = jnp.zeros((8, 128), I32)
    for n in range(PAIRS):
        row = owner_of[bounded(ids[n // CAND, n % CAND], OWNERS * PASS_DEV - 1)]
        same = (slot >> 4) == (row >> 4)
        mine = jnp.where(same & ((slot & 15) == listed), 256 * n + row, mine)
        listed = listed + jnp.where(same, 1, 0)
    rows_buf[me] = mine
    pl.semaphore_wait(barrier, len(peers))
    weights = Gather(place, full_ref, w_send, w_recv)
    weights.start()
    rows = Gather(place, rows_buf, r_send, r_recv)
    rows.start()

    cache_in.wait()
    cache_f[0 : PLEN * PASS_DEV, :] = cache_ref[...].reshape(PLEN * PASS_DEV, DIM).astype(F32)
    for r in range(PASS_DEV):
        tiles[r, ROWS - 16 : ROWS] = jnp.zeros((16, DIM), BF16)
        tiles[r, 0:PLEN] = cache_f[pl.ds(r, PLEN, stride=PASS_DEV), :].astype(BF16)
    logs[...] = jnp.zeros_like(logs)
    recips[...] = jnp.zeros_like(recips)

    weights.relay(NZ - 1)
    rows.finish()
    for d in range(OWNERS):
        rows_vec[d : d + 1, :] = rows_buf[d, pl.ds(me >> 3, 1), :]
    to_rows = pltpu.make_async_copy(rows_vec, rows_tab, tab_sem.at[0])
    to_rows.start()
    hidden_in.wait()
    weights.finish()
    raw = dot(hidden_ref[...], full_ref[...].reshape(-1, DIM))
    inverse = lax.rsqrt(jnp.mean(raw * raw, axis=-1, keepdims=True) + EPS)
    vectors = (raw * inverse).astype(BF16)
    query_ref[me] = vectors.reshape(Q_DEV, QL, DIM)
    queries = Gather(place, query_ref, q_send, q_recv)
    queries.start()

    to_rows.wait()
    first_row = PASS_DEV * me

    my_lane = 16 * (me & 7)

    def listed_pair(d, n):
        value = rows_tab[d, my_lane + n]
        row = jnp.where(value >= 0, (value & 255) - first_row, -1)
        return jnp.where(value >= 0, PAIRS * d + (value >> 8), -1), row

    deep = iota((PASS_DEV, 128), 0)

    def count_pairs(d, counts):
        for n in range(CAP):
            counts = counts + jnp.where(deep == listed_pair(d, n)[1], 1, 0)
        return counts

    counts = lax.fori_loop(0, OWNERS, count_pairs, jnp.zeros((PASS_DEV, 128), I32))
    group = slot & 63
    start = jnp.zeros((8, 128), I32)
    slot_row, slot_start, last = start, start, start - 1
    for r in range(PASS_DEV):
        number = jnp.broadcast_to(counts[r : r + 1, :], (8, 128))
        if r:
            slot_row = slot_row + jnp.where(group >= start, 1, 0)
            slot_start = jnp.where(group >= start, start, slot_start)
        start = start + ((number + 3) >> 2)
        last = jnp.where((lane == r) & (number > 0), start - 1, last)
    slot_rank = 4 * (group - slot_start) + (slot >> 6)

    def place_pairs(d, carry):
        seen, at_slot, at_entry = carry
        for n in range(CAP):
            pair, row = listed_pair(d, n)
            same = slot_row == row
            at_slot = jnp.where(same & (slot_rank == seen), pair, at_slot)
            seen = seen + jnp.where(same, 1, 0)
            at_entry = jnp.where((slot == 16 * d + n) & (pair >= 0), pair, at_entry)
        return seen, at_slot, at_entry

    none = jnp.full((8, 128), -1, I32)
    _, at_slot, at_entry = lax.fori_loop(
        0, OWNERS, place_pairs, (jnp.zeros((8, 128), I32), none, none - 1)
    )
    tab_vec[0] = at_slot
    tab_vec[1] = slot_row
    tab_vec[2] = at_entry
    tab_vec[3] = last
    to_tab = pltpu.make_async_copy(tab_vec.at[pl.ds(0, 4)], tab.at[pl.ds(0, 4)], tab_sem.at[1])
    to_tab.start()
    queries.finish()
    to_tab.wait()

    def row_of(g):
        return bounded(tab[1, 0, g], PASS_DEV - 1)

    def load_queries(g):
        parts = []
        for j in range(4):
            pair = tab[0, j // 2, 64 * (j % 2) + g]
            query = bounded(pair >> 4, OWNERS * Q_DEV - 1)
            parts.append(query_ref[query >> 2, query & (Q_DEV - 1)])
        return jnp.concatenate(parts, axis=0)

    live = iota((ROWS, 128), 0)

    def forward(i, _):
        for u in range(4):
            g = 4 * i + u
            row = row_of(g)
            sims = dot_nt(tiles[row], load_queries(g)) * similarity_scale
            sims = jnp.where(live < len_ref[row], sims, NEG)
            top = jnp.max(sims, axis=0, keepdims=True)
            e = jnp.exp(sims - top)
            total = jnp.sum(e, axis=0, keepdims=True)
            exps[g] = e
            logs[pl.ds(g, 1), :] = top + jnp.log(total)
            recips[pl.ds(g, 1), :] = 1.0 / total
        return 0

    lax.fori_loop(0, GROUPS // 4, forward, 0)

    of_place = iota((SLOTS, 128), 1) // QL == iota((SLOTS, 128), 0) // 64
    spread = jnp.where(of_place, jnp.concatenate([logs[...]] * 4, axis=0), 0.0)
    one8 = jnp.ones((8, 128), BF16)
    score_row = TAU * sum(dot_nt(one8, part) for part in pieces(spread))
    pair = jnp.concatenate([at_slot[0:1], at_slot[1:2]], axis=1)
    is_cand = ind((iota((CAND, SLOTS), 0) == (pair & (CAND - 1))) & (pair >= 0))
    lane_of = ((pair >> 6) << 3) + ((pair >> 4) & (Q_DEV - 1))
    hits = ind((iota((128, SLOTS), 0) == lane_of) & (pair >= 0), BF16)
    mine = sum(
        dot_nt((is_cand * part[0:1].astype(F32)).astype(BF16), hits) for part in pieces(score_row)
    )
    score_buf[me] = mine[0:8] + pltpu.roll(mine[8:16], 4, 1)
    score_swap = Swap(OWNERS, me, lambda t: {"passage": t}, s_send, s_recv)
    score_swap.start(lambda t: score_buf.at[me], score_buf)

    def place_entries(i, spots):
        for u in range(16):
            pair = tab[0, i >> 3, 16 * (i & 7) + u]
            spots = jnp.where(at_entry == pair, 64 * (i & 3) + (i >> 2) + 4 * u, spots)
        return spots

    tab_vec[4] = lax.fori_loop(0, SLOTS // 16, place_entries, jnp.zeros((8, 128), I32))
    to_spots = pltpu.make_async_copy(tab_vec.at[4], tab.at[4], tab_sem.at[2])
    to_spots.start()

    def products(i, _):
        for u in range(4):
            g = 4 * i + u
            w = (exps[g] * recips[pl.ds(g, 1), :]).astype(BF16)
            qg_group[g] = dot_tn(w, tiles[row_of(g)]).reshape(4, QL, DIM)
        return 0

    lax.fori_loop(0, GROUPS // 4, products, 0)

    score_swap.finish()
    scores = score_buf[0]
    for d in range(1, OWNERS):
        scores = scores + score_buf[d]
    low = lax.rem(lane, 8) < Q_DEV

    def both(x, op):
        return op(x, jnp.where(low, pltpu.roll(x, 124, 1), pltpu.roll(x, 4, 1)))

    top = both(jnp.broadcast_to(jnp.max(scores, axis=0, keepdims=True), (8, 128)), jnp.maximum)
    e = jnp.exp(scores - top)
    total = both(jnp.broadcast_to(jnp.sum(e, axis=0, keepdims=True), (8, 128)), jnp.add)
    grad = e / total - ind((iota((8, 128), 0) == 0) & low)
    grad = jnp.concatenate(
        [jnp.where(low, grad, 0.0), jnp.where(low, pltpu.roll(grad, 124, 1), 0.0)], axis=0
    )
    grad_row = is_cand * sum(dot(part, hits) for part in pieces(grad))
    grad_row = jnp.sum(grad_row, axis=0, keepdims=True)
    grad_vec[...] = jnp.broadcast_to(grad_row * root_scale, (8, SLOTS))
    grad_copy = pltpu.make_async_copy(grad_vec, grad_tab, grad_sem)
    grad_copy.start()
    same_group = ind(lax.rem(iota((64, SLOTS), 1), 64) == iota((64, SLOTS), 0))
    to_lanes = ind(of_place, BF16)
    by_lane = sum(dot(part, to_lanes) for part in pieces(same_group * grad_row))
    scales[...] = by_lane * recips[...] * root_scale
    to_spots.wait()
    grad_copy.wait()

    def sum_device(d, _):
        sums = [jnp.zeros((QL, DIM), F32) for _ in range(Q_DEV)]
        for n in range(CAP):
            sub, spot_lane = d >> 3, 16 * (d & 7) + n
            pair = tab[2, sub, spot_lane]
            at = bounded(tab[4, sub, spot_lane], 4 * GROUPS - 1)
            part = qg_group[at >> 2, at & 3]
            grad = grad_tab[0, 64 * (at & 3) + (at >> 2)]
            for q in range(Q_DEV):
                one = jnp.where((pair >= 0) & (((pair >> 4) & (Q_DEV - 1)) == q), grad, 0.0)
                sums[q] = sums[q] + part * one
        for q in range(Q_DEV):
            qg_ref[d >> 1, d & 1, q * QL : (q + 1) * QL, :] = sums[q].astype(BF16)
        return 0

    lax.fori_loop(0, OWNERS, sum_device, 0)
    q_pair = remote(qg_ref.at[:, 1 - c], q_sib, qs_send, qs_recv, sibling)
    q_pair.start()

    def cache_step(i, run):
        for u in range(4):
            g = 4 * i + u
            row = row_of(g)
            w = (exps[g] * scales[pl.ds(g, 1), :]).astype(BF16)
            again = (row == row_of(jnp.maximum(g - 1, 0))) & (g > 0)
            cg_run[g + 1] = jnp.where(again, cg_run[g], 0.0) + dot(w, load_queries(g))
        return run

    lax.fori_loop(0, 4, cache_step, 0)
    q_pair.wait_recv()
    for t in range(NZ):
        q_out[t] = (qg_ref[t, c].astype(F32) + q_sib[t].astype(F32)).astype(BF16)
    on_z = lambda t: {"passage": t * NC + c}
    q_swap = Swap(NZ, z, on_z, qz_send, qz_recv)
    q_swap.start(lambda t: q_out.at[t], q_in)
    lax.fori_loop(4, GROUPS // 4, cache_step, 0)

    for r in range(PASS_DEV):
        last = tab[3, 0, r]
        value = jnp.where(last >= 0, cg_run[bounded(last, GROUPS - 1) + 1], 0.0)
        cache_f[pl.ds(r, ROWS, stride=PASS_DEV), :] = value
    cg_ref[...] = cache_f[...].astype(BF16)

    sent = []

    def push(src, dst, send, recv, device):
        copy = remote(src, dst, send, recv, device)
        copy.start()
        sent.append(copy)

    def await_recv(dst, send, recv):
        remote(dst, dst, send, recv, sibling).wait_recv()

    def y_at(k):
        return (iy + k) & (NY - 1)

    def x_at(k):
        return (ix + k) & (NX - 1)

    for k in FAR:
        src = cg_ref.at[rows_at(B_AT + y_at(k) * B_PIECE, B_PIECE), :]
        push(src, by_buf.at[k - 1], b1_send.at[k - 1], b1_recv.at[k - 1], to_y(k))
    for d in FAR + (0,):
        for k in (2, 1, 3):
            src = cg_ref.at[rows_at(x_at(k) * A_PIECE + y_at(d) * A_ROWS, A_ROWS), :]
            push(src, ax_buf.at[k - 1, d], a1_send.at[k - 1, d], a1_recv.at[k - 1, d], to_x(k))

    q_swap.finish()
    query_gradient = q_out[z].astype(F32)
    for k in range(1, NZ):
        query_gradient = query_gradient + q_in[(z + k) & (NZ - 1)].astype(F32)
    inverse = lax.rsqrt(jnp.mean(raw * raw, axis=-1, keepdims=True) + EPS)
    mean_term = jnp.mean(query_gradient * raw, axis=-1, keepdims=True)
    raw_grad = (
        inverse * query_gradient - raw * (inverse * inverse * inverse) * mean_term
    ).astype(BF16)
    weight_part = dot_tn(hidden_ref[...], raw_grad)
    w_own[...] = weight_part.astype(BF16).reshape(w_own.shape)
    w_pair = remote(w_own.at[:, 1 - c], w_sib, ws_send, ws_recv, sibling)
    w_pair.start()

    def a_first(d):
        total = cg_ref[rows_at(ix * A_PIECE + y_at(d) * A_ROWS, A_ROWS), :].astype(F32)
        for k in range(1, NX):
            await_recv(ax_buf.at[k - 1, d], a1_send.at[k - 1, d], a1_recv.at[k - 1, d])
            total = total + ax_buf[k - 1, d].astype(F32)
        mid_a[d] = total.astype(BF16)
        if d:
            push(mid_a.at[d], ay_buf.at[d - 1], a2_send.at[d - 1], a2_recv.at[d - 1], to_y(d))

    for d in FAR[:4]:
        a_first(d)
    w_pair.wait_recv()
    for t in range(NZ):
        w_out[t] = (w_own[t, c].astype(F32) + w_sib[t].astype(F32)).astype(BF16)
    w_swap = Swap(NZ, z, on_z, wz_send, wz_recv)
    w_swap.start(lambda t: w_out.at[t], w_in)
    for d in FAR[4:] + (0,):
        a_first(d)
    hid_ref[...] = dot_nt(raw_grad, full_ref[...].reshape(-1, DIM)).astype(BF16)

    total = cg_ref[rows_at(B_AT + iy * B_PIECE, B_PIECE), :].astype(F32)
    for k in range(1, NY):
        await_recv(by_buf.at[k - 1], b1_send.at[k - 1], b1_recv.at[k - 1])
        total = total + by_buf[k - 1].astype(F32)
    mid_b[...] = total.astype(BF16)
    for k in (2, 1, 3):
        src = mid_b.at[rows_at(x_at(k) * B_ROWS, B_ROWS), :]
        push(src, bx_buf.at[k - 1], b2_send.at[k - 1], b2_recv.at[k - 1], to_x(k))
    total = mid_b[rows_at(ix * B_ROWS, B_ROWS), :].astype(F32)
    for k in range(1, NX):
        await_recv(bx_buf.at[k - 1], b2_send.at[k - 1], b2_recv.at[k - 1])
        total = total + bx_buf[k - 1].astype(F32)
    b_span = lambda kx, ky: fin.at[rows_at(B_AT + y_at(ky) * B_PIECE + x_at(kx) * B_ROWS, B_ROWS), :]
    fin[rows_at(B_AT + iy * B_PIECE + ix * B_ROWS, B_ROWS), :] = total.astype(BF16)
    for k in (2, 1, 3):
        push(b_span(0, 0), b_span(0, 0), b3_send.at[k - 1], b3_recv.at[k - 1], to_x(k))

    total = mid_a[0].astype(F32)
    for d in range(1, NY):
        await_recv(ay_buf.at[d - 1], a2_send.at[d - 1], a2_recv.at[d - 1])
        total = total + ay_buf[d - 1].astype(F32)
    a_span = lambda kx, ky: fin.at[rows_at(x_at(kx) * A_PIECE + y_at(ky) * A_ROWS, A_ROWS), :]
    fin[rows_at(ix * A_PIECE + iy * A_ROWS, A_ROWS), :] = total.astype(BF16)
    for d in FAR:
        push(a_span(0, 0), a_span(0, 0), a3_send.at[d - 1], a3_recv.at[d - 1], to_y(d))
    for k in (2, 1, 3):
        push(a_span(0, 0), a_span(0, 0), a4_send.at[k - 1, 0], a4_recv.at[k - 1, 0], to_x(k))

    w_swap.finish()
    total = w_out[z].astype(F32)
    for k in range(1, NZ):
        total = total + w_in[(z + k) & (NZ - 1)].astype(F32)
    w_x[ix] = total.astype(BF16)
    x_swap = Swap(NX, ix, lambda t: {"dp": t * NY + iy}, wx_send, wx_recv)
    x_swap.start(lambda t: w_x.at[ix], w_x)

    for k in range(1, NX):
        await_recv(b_span(-k, 0), b3_send.at[k - 1], b3_recv.at[k - 1])
    b_line = lambda k: fin.at[rows_at(B_AT + y_at(k) * B_PIECE, B_PIECE), :]
    for d in FAR:
        push(b_line(0), b_line(0), b4_send.at[d - 1], b4_recv.at[d - 1], to_y(d))

    def a_forward(d):
        await_recv(a_span(0, -d), a3_send.at[d - 1], a3_recv.at[d - 1])
        for k in (2, 1, 3):
            push(a_span(0, -d), a_span(0, -d), a4_send.at[k - 1, d], a4_recv.at[k - 1, d], to_x(k))

    for d in NEAR[:4]:
        a_forward(d)
    x_swap.finish()
    total = w_x[0].astype(F32)
    for t in range(1, NX):
        total = total + w_x[t].astype(F32)
    w_y[iy] = total.astype(BF16)
    y_swap = Swap(NY, iy, lambda t: {"dp": ix * NY + t}, wy_send, wy_recv)
    y_swap.start(lambda t: w_y.at[iy], w_y)
    for d in NEAR[4:]:
        a_forward(d)

    for d in range(1, NY):
        await_recv(b_line(-d), b4_send.at[d - 1], b4_recv.at[d - 1])
    b_live = PLEN * PASS_DEV - B_AT
    b_out = pltpu.make_async_copy(
        fin.at[pl.ds(B_AT, b_live), :], cache_out.at[pl.ds(B_AT, b_live), :], out_sem.at[0]
    )
    b_out.start()
    for d in range(NY):
        for k in range(1, NX):
            await_recv(a_span(-k, -d), a4_send.at[k - 1, d], a4_recv.at[k - 1, d])
    a_out = pltpu.make_async_copy(
        fin.at[pl.ds(0, B_AT), :], cache_out.at[pl.ds(0, B_AT), :], out_sem.at[1]
    )
    a_out.start()
    y_swap.finish()
    total = w_y[0].astype(F32)
    for t in range(1, NY):
        total = total + w_y[t].astype(F32)
    wg_ref[...] = total

    q_pair.wait_send()
    w_pair.wait_send()
    for moved in (weights, rows, queries, score_swap, q_swap, w_swap, x_swap, y_swap):
        moved.drain()
    for copy in sent:
        copy.wait_send()
    b_out.wait()
    a_out.wait()


def result_kernel(hid, wg, cache, hid_out, wg_out, cache_out, hid_buf, wg_buf, cache_buf, sems):
    part = PLEN * PASS_DEV // 4
    moves = []
    for n in range(4):
        span = pl.ds(n * part, part)
        moves.append((cache.at[span, :], cache_buf.at[span, :], cache_out.at[span, :]))
    moves += [(hid, hid_buf, hid_out), (wg, wg_buf, wg_out)]
    reads, writes = [], []
    for n, (src, mid, _) in enumerate(moves):
        reads.append(pltpu.make_async_copy(src, mid, sems.at[0, n]))
        reads[-1].start()
    for n, (_, mid, dst) in enumerate(moves):
        reads[n].wait()
        writes.append(pltpu.make_async_copy(mid, dst, sems.at[1, n]))
        writes[-1].start()
    for copy in writes:
        copy.wait()


VMEM = pl.BlockSpec(memory_space=pltpu.VMEM)
SMEM = pl.BlockSpec(memory_space=pltpu.SMEM)
ANY = pl.BlockSpec(memory_space=pl.ANY)


def call(kernel, collective_id, out_shape, in_specs, out_specs, scratch, args):
    return pl.pallas_call(
        kernel,
        out_shape=out_shape,
        in_specs=in_specs,
        out_specs=out_specs,
        scratch_shapes=scratch,
        compiler_params=pltpu.CompilerParams(
            collective_id=collective_id, has_side_effects=True, vmem_limit_bytes=56 * 2**20
        ),
    )(*args)


def shards(hidden, weight, cache, lengths, passage_ids, owner_map):
    width = hidden.shape[-1]
    share = width // OWNERS
    tokens = Q_DEV * QL
    shape = jax.ShapeDtypeStruct
    dma = pltpu.SemaphoreType.DMA
    vmem = pltpu.VMEM

    def pair(*sizes):
        return [dma(sizes), dma(sizes)]

    scratch = [
        vmem((tokens, width), BF16),
        vmem((PLEN, PASS_DEV, DIM), BF16),
        vmem((OWNERS, Q_DEV, QL, DIM), BF16),
        vmem((OWNERS, share, DIM), BF16),
        vmem((PASS_DEV, ROWS, DIM), BF16),
        vmem((OWNERS, 8, 128), I32),
        vmem((OWNERS, 128), I32),
        pltpu.SMEM((OWNERS, 128), I32),
        vmem((5, 8, 128), I32),
        pltpu.SMEM((5, 8, 128), I32),
        vmem((FLAT, DIM), F32),
        vmem((GROUPS, ROWS, 128), F32),
        vmem((64, 128), F32),
        vmem((64, 128), F32),
        vmem((64, 128), F32),
        vmem((OWNERS, 8, 128), F32),
        vmem((8, SLOTS), F32),
        pltpu.SMEM((8, SLOTS), F32),
        vmem((GROUPS + 1, ROWS, DIM), F32),
        vmem((GROUPS, 4, QL, DIM), F32),
        vmem((NZ, NC, tokens, DIM), BF16),
        vmem((FLAT, DIM), BF16),
        vmem((NX - 1, NY, A_ROWS, DIM), BF16),
        vmem((NY - 1, A_ROWS, DIM), BF16),
        vmem((NY - 1, B_PIECE, DIM), BF16),
        vmem((NX - 1, B_ROWS, DIM), BF16),
        vmem((NY, A_ROWS, DIM), BF16),
        vmem((B_PIECE, DIM), BF16),
        vmem((FLAT, DIM), BF16),
        vmem((NZ, tokens, DIM), BF16),
        vmem((NZ, tokens, DIM), BF16),
        vmem((NZ, tokens, DIM), BF16),
        vmem((NZ, NC, share, DIM), BF16),
        vmem((NZ, share, DIM), BF16),
        vmem((NZ, share, DIM), BF16),
        vmem((NZ, share, DIM), BF16),
        vmem((NX, share, DIM), BF16),
        vmem((NY, share, DIM), BF16),
        dma((2,)),
        dma((4,)),
        dma,
        dma((2,)),
    ]
    gather = [dma((2 * NZ - 1,)), dma((OWNERS,))]
    swap = lambda n: [dma((n - 1,)), dma((n,))]
    scratch += gather + gather + gather + swap(OWNERS)
    scratch += [dma, dma] + swap(NZ) + [dma, dma] + swap(NZ) + swap(NX) + swap(NY)
    scratch += pair(NX - 1, NY) + pair(NY - 1) + pair(NY - 1) + pair(NX - 1, NY)
    scratch += pair(NY - 1) + pair(NX - 1) + pair(NX - 1) + pair(NY - 1)

    hid, wg, cache_grad = call(
        pair_kernel,
        0,
        [
            shape((tokens, width), BF16),
            shape((share, DIM), F32),
            shape((PLEN * PASS_DEV, DIM), BF16),
        ],
        [ANY, VMEM, ANY, SMEM, SMEM, SMEM],
        [VMEM, VMEM, ANY],
        scratch,
        (
            hidden.reshape(tokens, width),
            weight,
            jnp.transpose(cache, (1, 0, 2)),
            lengths,
            passage_ids,
            owner_map,
        ),
    )
    hid, wg, cache_grad = pl.pallas_call(
        result_kernel,
        out_shape=[shape(x.shape, x.dtype) for x in (hid, wg, cache_grad)],
        in_specs=[ANY] * 3,
        out_specs=[ANY] * 3,
        scratch_shapes=[vmem(x.shape, x.dtype) for x in (hid, wg, cache_grad)] + [dma((2, 6))],
    )(hid, wg, cache_grad)
    cache_grad = jnp.transpose(cache_grad.reshape(PLEN, PASS_DEV, DIM), (1, 0, 2))
    return hid.reshape(Q_DEV, QL, width), wg, cache_grad


def solution(mesh):
    in_specs = (
        P(("dp", "passage"), None, None),
        P("passage", None),
        P("passage", None, None),
        P("passage"),
        P(("dp", "passage"), None),
        P(),
    )
    out_specs = (P(("dp", "passage"), None, None), P("passage", None), P("passage", None, None))
    return jax.shard_map(shards, mesh=mesh, in_specs=in_specs, out_specs=out_specs, check_vma=False)
```

```python
import functools
import math

import jax
import jax.numpy as jnp
from jax import lax
from jax.experimental import pallas as pl
from jax.experimental.pallas import tpu as pltpu
from jax.sharding import PartitionSpec as P

TAU = 0.1
EPS = 1e-06

NX, NY, NZ, NC = 4, 8, 8, 2
OWNERS = NZ * NC
Q_DEV, QL, CAND = 4, 32, 16
PASS_DEV, PLEN, ROWS = 16, 180, 192
DIM = 128
GROUPS = 60
UNROLL = 20
SLOTS = 256
CAP = 12
PAIRS = Q_DEV * CAND
NEG = -1e30

F32, BF16, I32 = jnp.float32, jnp.bfloat16, jnp.int32


def dot(a, b):
    return jnp.dot(a, b, preferred_element_type=F32)


def dot_nt(a, b):
    return lax.dot_general(a, b, (((1,), (1,)), ((), ())), preferred_element_type=F32)


def dot_tn(a, b):
    return lax.dot_general(a, b, (((0,), (0,)), ((), ())), preferred_element_type=F32)


def iota(shape, axis):
    return lax.broadcasted_iota(I32, shape, axis)


def ind(cond, dtype=F32):
    return jnp.where(cond, 1.0, 0.0).astype(dtype)


def pieces(x):
    a = x.astype(BF16)
    rest = x - a.astype(F32)
    b = rest.astype(BF16)
    return (a, b, (rest - b.astype(F32)).astype(BF16))


class Place:
    def __init__(self):
        self.me = lax.axis_index("passage")
        self.z, self.c = self.me >> 1, self.me & (NC - 1)
        self.sibling = self.z * NC + (1 - self.c)

    def ring(self, k):
        return ((self.z + k) & (NZ - 1)) * NC + self.c

    def ring_sibling(self, k):
        return ((self.z + k) & (NZ - 1)) * NC + (1 - self.c)


def remote(src, dst, send, recv, device):
    return pltpu.make_async_remote_copy(
        src_ref=src,
        dst_ref=dst,
        send_sem=send,
        recv_sem=recv,
        device_id=device,
        device_id_type=pl.DeviceIdType.MESH,
    )


NEAR = (1, 7, 2, 6, 3, 5, 4)


class Gather:
    def __init__(self, place, buf, send, recv):
        self.place, self.buf, self.send, self.recv = place, buf, send, recv
        self.sent, self.relayed = [], 0

    def copy(self, slot, n, peer):
        return remote(
            self.buf.at[slot], self.buf.at[slot], self.send.at[n], self.recv.at[slot],
            {"passage": peer},
        )

    def start(self):
        p = self.place
        for n, k in list(enumerate(NEAR))[::-1]:
            self.sent.append(self.copy(p.me, n, p.ring(k)))
            self.sent[-1].start()
        self.sent.append(self.copy(p.me, NZ - 1, p.sibling))
        self.sent[-1].start()

    def relay(self, upto):
        p = self.place
        for n in range(self.relayed, upto):
            forward = self.copy(p.ring(NEAR[n]), NZ + n, p.sibling)
            forward.wait_recv()
            forward.start()
            self.sent.append(forward)
        self.relayed = upto

    def finish(self):
        p = self.place
        self.relay(NZ - 1)
        self.copy(p.sibling, 0, p.sibling).wait_recv()
        for k in NEAR:
            self.copy(p.ring_sibling(k), 0, p.sibling).wait_recv()

    def drain(self):
        for copy in self.sent:
            copy.wait_send()


FAR = (4, 3, 5, 2, 6, 1, 7)
A_ROWS, B_ROWS = 80, 16
A_PIECE, B_PIECE = NY * A_ROWS, NX * B_ROWS
B_AT = NX * A_PIECE
FLAT = PASS_DEV * ROWS


def rows_at(start, count):
    return pl.ds(pl.multiple_of(start, 16), count)


class Swap:
    def __init__(self, n, at, device, send, recv):
        self.n, self.at, self.device, self.send, self.recv = n, at, device, send, recv

    def start(self, src_of, buf):
        self.buf, self.copies = buf, []
        far = sorted(range(1, self.n), key=lambda k: -min(k, self.n - k))
        for k in far:
            t = (self.at + k) & (self.n - 1)
            copy = remote(
                src_of(t), buf.at[self.at], self.send.at[k - 1], self.recv.at[self.at], self.device(t)
            )
            copy.start()
            self.copies.append(copy)

    def finish(self):
        for k in range(1, self.n):
            t = (self.at + k) & (self.n - 1)
            remote(
                self.buf.at[t], self.buf.at[t], self.send.at[0], self.recv.at[t], self.device(t)
            ).wait_recv()

    def drain(self):
        for copy in self.copies:
            copy.wait_send()


def pair_kernel(
    hidden_hbm, weight_ref, cache_hbm, len_ref, ids, owner_of,
    hid_ref, wg_ref, cache_out,
    hidden_ref, cache_ref, query_ref, full_ref, tiles, rows_buf, rows_vec, rows_tab,
    tab_vec, tab,
    cache_f, exps, logs, recips, scales,
    score_buf, grad_vec, grad_tab, cg_run, qg_group, qg_ref, cg_ref,
    ax_buf, ay_buf, by_buf, bx_buf, mid_a, mid_b, fin, q_sib, q_out, q_in, w_own, w_sib, w_out, w_in, w_x, w_y,
    in_sem, tab_sem, grad_sem, out_sem,
    w_send, w_recv, r_send, r_recv, q_send, q_recv, s_send, s_recv,
    qs_send, qs_recv, qz_send, qz_recv, ws_send, ws_recv, wz_send, wz_recv, wx_send, wx_recv, wy_send, wy_recv,
    a1_send, a1_recv, a2_send, a2_recv, a3_send, a3_recv, a4_send, a4_recv,
    b1_send, b1_recv, b2_send, b2_recv, b3_send, b3_recv, b4_send, b4_recv,
):
    place = Place()
    me, z, c = place.me, place.z, place.c
    dp = lax.axis_index("dp")
    ix, iy = dp >> 3, dp & (NY - 1)
    others = [(me + k) & (OWNERS - 1) for k in range(1, OWNERS)]
    to_x = lambda k: {"dp": ((ix + k) & (NX - 1)) * NY + iy}
    to_y = lambda k: {"dp": ix * NY + ((iy + k) & (NY - 1))}
    sibling = {"passage": place.sibling}
    similarity_scale = 1.0 / (TAU * math.sqrt(DIM))
    root_scale = 1.0 / math.sqrt(DIM)

    barrier = pltpu.get_barrier_semaphore()
    peers = [{"passage": d} for d in others]
    peers += [to_x(k) for k in range(1, NX)] + [to_y(k) for k in range(1, NY)]
    for device in peers:
        pl.semaphore_signal(barrier, inc=1, device_id=device, device_id_type=pl.DeviceIdType.MESH)
    hidden_in = pltpu.make_async_copy(hidden_hbm, hidden_ref, in_sem.at[0])
    cache_in = pltpu.make_async_copy(cache_hbm, cache_ref, in_sem.at[1])
    hidden_in.start()
    cache_in.start()

    def bounded(value, most):
        return jnp.minimum(jnp.maximum(value, 0), most)

    full_ref[me] = weight_ref[...]
    lane = iota((8, 128), 1)
    slot = iota((8, 128), 0) * 128 + lane
    mine = jnp.full((8, 128), -1, I32)
    listed = jnp.zeros((8, 128), I32)
    for n in range(PAIRS):
        row = owner_of[bounded(ids[n // CAND, n % CAND], OWNERS * PASS_DEV - 1)]
        same = (slot >> 4) == (row >> 4)
        mine = jnp.where(same & ((slot & 15) == listed), 256 * n + row, mine)
        listed = listed + jnp.where(same, 1, 0)
    rows_buf[me] = mine
    pl.semaphore_wait(barrier, len(peers))
    weights = Gather(place, full_ref, w_send, w_recv)
    weights.start()
    rows = Gather(place, rows_buf, r_send, r_recv)
    rows.start()

    cache_in.wait()
    cache_f[0 : PLEN * PASS_DEV, :] = cache_ref[...].reshape(PLEN * PASS_DEV, DIM).astype(F32)
    for r in range(PASS_DEV):
        tiles[r, ROWS - 16 : ROWS] = jnp.zeros((16, DIM), BF16)
        tiles[r, 0:PLEN] = cache_f[pl.ds(r, PLEN, stride=PASS_DEV), :].astype(BF16)
    logs[...] = jnp.zeros_like(logs)
    recips[...] = jnp.zeros_like(recips)

    weights.relay(NZ - 1)
    rows.finish()
    for d in range(OWNERS):
        rows_vec[d : d + 1, :] = rows_buf[d, pl.ds(me >> 3, 1), :]
    to_rows = pltpu.make_async_copy(rows_vec, rows_tab, tab_sem.at[0])
    to_rows.start()
    hidden_in.wait()
    weights.finish()
    raw = dot(hidden_ref[...], full_ref[...].reshape(-1, DIM))
    inverse = lax.rsqrt(jnp.mean(raw * raw, axis=-1, keepdims=True) + EPS)
    vectors = (raw * inverse).astype(BF16)
    query_ref[me] = vectors.reshape(Q_DEV, QL, DIM)
    queries = Gather(place, query_ref, q_send, q_recv)
    queries.start()

    to_rows.wait()
    first_row = PASS_DEV * me

    my_lane = 16 * (me & 7)

    def listed_pair(d, n):
        value = rows_tab[d, my_lane + n]
        row = jnp.where(value >= 0, (value & 255) - first_row, -1)
        return jnp.where(value >= 0, PAIRS * d + (value >> 8), -1), row

    deep = iota((PASS_DEV, 128), 0)

    def count_pairs(d, counts):
        for n in range(CAP):
            counts = counts + jnp.where(deep == listed_pair(d, n)[1], 1, 0)
        return counts

    counts = lax.fori_loop(0, OWNERS, count_pairs, jnp.zeros((PASS_DEV, 128), I32))
    group = slot & 63
    start = jnp.zeros((8, 128), I32)
    slot_row, slot_start, last = start, start, start - 1
    for r in range(PASS_DEV):
        number = jnp.broadcast_to(counts[r : r + 1, :], (8, 128))
        if r:
            slot_row = slot_row + jnp.where(group >= start, 1, 0)
            slot_start = jnp.where(group >= start, start, slot_start)
        start = start + ((number + 3) >> 2)
        last = jnp.where((lane == r) & (number > 0), start - 1, last)
    slot_rank = 4 * (group - slot_start) + (slot >> 6)

    def place_pairs(d, carry):
        seen, at_slot, at_entry = carry
        for n in range(CAP):
            pair, row = listed_pair(d, n)
            same = slot_row == row
            at_slot = jnp.where(same & (slot_rank == seen), pair, at_slot)
            seen = seen + jnp.where(same, 1, 0)
            at_entry = jnp.where((slot == 16 * d + n) & (pair >= 0), pair, at_entry)
        return seen, at_slot, at_entry

    none = jnp.full((8, 128), -1, I32)
    _, at_slot, at_entry = lax.fori_loop(
        0, OWNERS, place_pairs, (jnp.zeros((8, 128), I32), none, none - 1)
    )
    tab_vec[0] = at_slot
    tab_vec[1] = slot_row
    tab_vec[2] = at_entry
    tab_vec[3] = last
    to_tab = pltpu.make_async_copy(tab_vec.at[pl.ds(0, 4)], tab.at[pl.ds(0, 4)], tab_sem.at[1])
    to_tab.start()
    queries.finish()
    to_tab.wait()

    def row_of(g):
        return bounded(tab[1, 0, g], PASS_DEV - 1)

    def load_queries(g):
        parts = []
        for j in range(4):
            pair = tab[0, j // 2, 64 * (j % 2) + g]
            query = bounded(pair >> 4, OWNERS * Q_DEV - 1)
            parts.append(query_ref[query >> 2, query & (Q_DEV - 1)])
        return jnp.concatenate(parts, axis=0)

    live = iota((ROWS, 128), 0)

    def forward(i, _):
        for u in range(UNROLL):
            g = UNROLL * i + u
            row = row_of(g)
            sims = dot_nt(tiles[row], load_queries(g)) * similarity_scale
            sims = jnp.where(live < len_ref[row], sims, NEG)
            top = jnp.max(sims, axis=0, keepdims=True)
            e = jnp.exp(sims - top)
            total = jnp.sum(e, axis=0, keepdims=True)
            exps[g] = e
            logs[pl.ds(g, 1), :] = top + jnp.log(total)
            recips[pl.ds(g, 1), :] = 1.0 / total
        return 0

    lax.fori_loop(0, GROUPS // UNROLL, forward, 0)

    of_place = iota((SLOTS, 128), 1) // QL == iota((SLOTS, 128), 0) // 64
    spread = jnp.where(of_place, jnp.concatenate([logs[...]] * 4, axis=0), 0.0)
    one8 = jnp.ones((8, 128), BF16)
    score_row = TAU * sum(dot_nt(one8, part) for part in pieces(spread))
    pair = jnp.concatenate([at_slot[0:1], at_slot[1:2]], axis=1)
    is_cand = ind((iota((CAND, SLOTS), 0) == (pair & (CAND - 1))) & (pair >= 0))
    lane_of = ((pair >> 6) << 3) + ((pair >> 4) & (Q_DEV - 1))
    hits = ind((iota((128, SLOTS), 0) == lane_of) & (pair >= 0), BF16)
    mine = sum(
        dot_nt((is_cand * part[0:1].astype(F32)).astype(BF16), hits) for part in pieces(score_row)
    )
    score_buf[me] = mine[0:8] + pltpu.roll(mine[8:16], 4, 1)
    score_swap = Swap(OWNERS, me, lambda t: {"passage": t}, s_send, s_recv)
    score_swap.start(lambda t: score_buf.at[me], score_buf)

    def place_entries(i, spots):
        for u in range(16):
            pair = tab[0, i >> 3, 16 * (i & 7) + u]
            spots = jnp.where(at_entry == pair, 64 * (i & 3) + (i >> 2) + 4 * u, spots)
        return spots

    tab_vec[4] = lax.fori_loop(0, SLOTS // 16, place_entries, jnp.zeros((8, 128), I32))
    to_spots = pltpu.make_async_copy(tab_vec.at[4], tab.at[4], tab_sem.at[2])
    to_spots.start()

    def products(i, _):
        for u in range(UNROLL):
            g = UNROLL * i + u
            w = (exps[g] * recips[pl.ds(g, 1), :]).astype(BF16)
            qg_group[g] = dot_tn(w, tiles[row_of(g)]).reshape(4, QL, DIM)
        return 0

    lax.fori_loop(0, GROUPS // UNROLL, products, 0)

    score_swap.finish()
    scores = score_buf[0]
    for d in range(1, OWNERS):
        scores = scores + score_buf[d]
    low = lax.rem(lane, 8) < Q_DEV

    def both(x, op):
        return op(x, jnp.where(low, pltpu.roll(x, 124, 1), pltpu.roll(x, 4, 1)))

    top = both(jnp.broadcast_to(jnp.max(scores, axis=0, keepdims=True), (8, 128)), jnp.maximum)
    e = jnp.exp(scores - top)
    total = both(jnp.broadcast_to(jnp.sum(e, axis=0, keepdims=True), (8, 128)), jnp.add)
    grad = e / total - ind((iota((8, 128), 0) == 0) & low)
    grad = jnp.concatenate(
        [jnp.where(low, grad, 0.0), jnp.where(low, pltpu.roll(grad, 124, 1), 0.0)], axis=0
    )
    grad_row = is_cand * sum(dot(part, hits) for part in pieces(grad))
    grad_row = jnp.sum(grad_row, axis=0, keepdims=True)
    grad_vec[...] = jnp.broadcast_to(grad_row * root_scale, (8, SLOTS))
    grad_copy = pltpu.make_async_copy(grad_vec, grad_tab, grad_sem)
    grad_copy.start()
    same_group = ind(lax.rem(iota((64, SLOTS), 1), 64) == iota((64, SLOTS), 0))
    to_lanes = ind(of_place, BF16)
    by_lane = sum(dot(part, to_lanes) for part in pieces(same_group * grad_row))
    scales[...] = by_lane * recips[...] * root_scale
    to_spots.wait()
    grad_copy.wait()

    def sum_device(d, _):
        sums = [jnp.zeros((QL, DIM), F32) for _ in range(Q_DEV)]
        for n in range(CAP):
            sub, spot_lane = d >> 3, 16 * (d & 7) + n
            pair = tab[2, sub, spot_lane]
            at = bounded(tab[4, sub, spot_lane], 4 * GROUPS - 1)
            part = qg_group[at >> 2, at & 3]
            grad = grad_tab[0, 64 * (at & 3) + (at >> 2)]
            for q in range(Q_DEV):
                one = jnp.where((pair >= 0) & (((pair >> 4) & (Q_DEV - 1)) == q), grad, 0.0)
                sums[q] = sums[q] + part * one
        for q in range(Q_DEV):
            qg_ref[d >> 1, d & 1, q * QL : (q + 1) * QL, :] = sums[q].astype(BF16)
        return 0

    lax.fori_loop(0, OWNERS, sum_device, 0)
    q_pair = remote(qg_ref.at[:, 1 - c], q_sib, qs_send, qs_recv, sibling)
    q_pair.start()

    def cache_step(i, run):
        for u in range(UNROLL):
            g = UNROLL * i + u
            row = row_of(g)
            w = (exps[g] * scales[pl.ds(g, 1), :]).astype(BF16)
            again = (row == row_of(jnp.maximum(g - 1, 0))) & (g > 0)
            cg_run[g + 1] = jnp.where(again, cg_run[g], 0.0) + dot(w, load_queries(g))
        return run

    lax.fori_loop(0, 1, cache_step, 0)
    q_pair.wait_recv()
    for t in range(NZ):
        q_out[t] = (qg_ref[t, c].astype(F32) + q_sib[t].astype(F32)).astype(BF16)
    on_z = lambda t: {"passage": t * NC + c}
    q_swap = Swap(NZ, z, on_z, qz_send, qz_recv)
    q_swap.start(lambda t: q_out.at[t], q_in)
    lax.fori_loop(1, GROUPS // UNROLL, cache_step, 0)

    for r in range(PASS_DEV):
        last = tab[3, 0, r]
        value = jnp.where(last >= 0, cg_run[bounded(last, GROUPS - 1) + 1], 0.0)
        cache_f[pl.ds(r, ROWS, stride=PASS_DEV), :] = value
    cg_ref[...] = cache_f[...].astype(BF16)

    sent = []

    def push(src, dst, send, recv, device):
        copy = remote(src, dst, send, recv, device)
        copy.start()
        sent.append(copy)

    def await_recv(dst, send, recv):
        remote(dst, dst, send, recv, sibling).wait_recv()

    def y_at(k):
        return (iy + k) & (NY - 1)

    def x_at(k):
        return (ix + k) & (NX - 1)

    for k in FAR:
        src = cg_ref.at[rows_at(B_AT + y_at(k) * B_PIECE, B_PIECE), :]
        push(src, by_buf.at[k - 1], b1_send.at[k - 1], b1_recv.at[k - 1], to_y(k))
    for d in FAR + (0,):
        for k in (2, 1, 3):
            src = cg_ref.at[rows_at(x_at(k) * A_PIECE + y_at(d) * A_ROWS, A_ROWS), :]
            push(src, ax_buf.at[k - 1, d], a1_send.at[k - 1, d], a1_recv.at[k - 1, d], to_x(k))

    q_swap.finish()
    query_gradient = q_out[z].astype(F32)
    for k in range(1, NZ):
        query_gradient = query_gradient + q_in[(z + k) & (NZ - 1)].astype(F32)
    inverse = lax.rsqrt(jnp.mean(raw * raw, axis=-1, keepdims=True) + EPS)
    mean_term = jnp.mean(query_gradient * raw, axis=-1, keepdims=True)
    raw_grad = (
        inverse * query_gradient - raw * (inverse * inverse * inverse) * mean_term
    ).astype(BF16)
    weight_part = dot_tn(hidden_ref[...], raw_grad)
    w_own[...] = weight_part.astype(BF16).reshape(w_own.shape)
    w_pair = remote(w_own.at[:, 1 - c], w_sib, ws_send, ws_recv, sibling)
    w_pair.start()

    def a_first(d):
        total = cg_ref[rows_at(ix * A_PIECE + y_at(d) * A_ROWS, A_ROWS), :].astype(F32)
        for k in range(1, NX):
            await_recv(ax_buf.at[k - 1, d], a1_send.at[k - 1, d], a1_recv.at[k - 1, d])
            total = total + ax_buf[k - 1, d].astype(F32)
        mid_a[d] = total.astype(BF16)
        if d:
            push(mid_a.at[d], ay_buf.at[d - 1], a2_send.at[d - 1], a2_recv.at[d - 1], to_y(d))

    for d in FAR[:4]:
        a_first(d)
    w_pair.wait_recv()
    for t in range(NZ):
        w_out[t] = (w_own[t, c].astype(F32) + w_sib[t].astype(F32)).astype(BF16)
    w_swap = Swap(NZ, z, on_z, wz_send, wz_recv)
    w_swap.start(lambda t: w_out.at[t], w_in)
    for d in FAR[4:] + (0,):
        a_first(d)
    hid_ref[...] = dot_nt(raw_grad, full_ref[...].reshape(-1, DIM)).astype(BF16)

    total = cg_ref[rows_at(B_AT + iy * B_PIECE, B_PIECE), :].astype(F32)
    for k in range(1, NY):
        await_recv(by_buf.at[k - 1], b1_send.at[k - 1], b1_recv.at[k - 1])
        total = total + by_buf[k - 1].astype(F32)
    mid_b[...] = total.astype(BF16)
    for k in (2, 1, 3):
        src = mid_b.at[rows_at(x_at(k) * B_ROWS, B_ROWS), :]
        push(src, bx_buf.at[k - 1], b2_send.at[k - 1], b2_recv.at[k - 1], to_x(k))
    total = mid_a[0].astype(F32)
    for d in range(1, NY):
        await_recv(ay_buf.at[d - 1], a2_send.at[d - 1], a2_recv.at[d - 1])
        total = total + ay_buf[d - 1].astype(F32)
    a_span = lambda kx, ky: fin.at[rows_at(x_at(kx) * A_PIECE + y_at(ky) * A_ROWS, A_ROWS), :]
    fin[rows_at(ix * A_PIECE + iy * A_ROWS, A_ROWS), :] = total.astype(BF16)
    for d in FAR:
        push(a_span(0, 0), a_span(0, 0), a3_send.at[d - 1], a3_recv.at[d - 1], to_y(d))
    for k in (2, 1, 3):
        push(a_span(0, 0), a_span(0, 0), a4_send.at[k - 1, 0], a4_recv.at[k - 1, 0], to_x(k))

    total = mid_b[rows_at(ix * B_ROWS, B_ROWS), :].astype(F32)
    for k in range(1, NX):
        await_recv(bx_buf.at[k - 1], b2_send.at[k - 1], b2_recv.at[k - 1])
        total = total + bx_buf[k - 1].astype(F32)
    b_span = lambda kx, ky: fin.at[rows_at(B_AT + y_at(ky) * B_PIECE + x_at(kx) * B_ROWS, B_ROWS), :]
    fin[rows_at(B_AT + iy * B_PIECE + ix * B_ROWS, B_ROWS), :] = total.astype(BF16)
    for k in (2, 1, 3):
        push(b_span(0, 0), b_span(0, 0), b3_send.at[k - 1], b3_recv.at[k - 1], to_x(k))

    w_swap.finish()
    total = w_out[z].astype(F32)
    for k in range(1, NZ):
        total = total + w_in[(z + k) & (NZ - 1)].astype(F32)
    w_x[ix] = total.astype(BF16)
    x_swap = Swap(NX, ix, lambda t: {"dp": t * NY + iy}, wx_send, wx_recv)
    x_swap.start(lambda t: w_x.at[ix], w_x)

    for k in range(1, NX):
        await_recv(b_span(-k, 0), b3_send.at[k - 1], b3_recv.at[k - 1])
    b_line = lambda k: fin.at[rows_at(B_AT + y_at(k) * B_PIECE, B_PIECE), :]
    for d in FAR:
        push(b_line(0), b_line(0), b4_send.at[d - 1], b4_recv.at[d - 1], to_y(d))

    def a_forward(d):
        await_recv(a_span(0, -d), a3_send.at[d - 1], a3_recv.at[d - 1])
        for k in (2, 1, 3):
            push(a_span(0, -d), a_span(0, -d), a4_send.at[k - 1, d], a4_recv.at[k - 1, d], to_x(k))

    for d in NEAR[:4]:
        a_forward(d)
    x_swap.finish()
    total = w_x[0].astype(F32)
    for t in range(1, NX):
        total = total + w_x[t].astype(F32)
    w_y[iy] = total.astype(BF16)
    y_swap = Swap(NY, iy, lambda t: {"dp": ix * NY + t}, wy_send, wy_recv)
    y_swap.start(lambda t: w_y.at[iy], w_y)
    for d in NEAR[4:]:
        a_forward(d)

    for d in range(1, NY):
        await_recv(b_line(-d), b4_send.at[d - 1], b4_recv.at[d - 1])
    b_live = PLEN * PASS_DEV - B_AT
    b_out = pltpu.make_async_copy(
        fin.at[pl.ds(B_AT, b_live), :], cache_out.at[pl.ds(B_AT, b_live), :], out_sem.at[0]
    )
    b_out.start()
    for d in range(NY):
        for k in range(1, NX):
            await_recv(a_span(-k, -d), a4_send.at[k - 1, d], a4_recv.at[k - 1, d])
    a_out = pltpu.make_async_copy(
        fin.at[pl.ds(0, B_AT), :], cache_out.at[pl.ds(0, B_AT), :], out_sem.at[1]
    )
    a_out.start()
    y_swap.finish()
    total = w_y[0].astype(F32)
    for t in range(1, NY):
        total = total + w_y[t].astype(F32)
    wg_ref[...] = total

    q_pair.wait_send()
    w_pair.wait_send()
    for moved in (weights, rows, queries, score_swap, q_swap, w_swap, x_swap, y_swap):
        moved.drain()
    for copy in sent:
        copy.wait_send()
    b_out.wait()
    a_out.wait()


def result_kernel(hid, wg, cache, hid_out, wg_out, cache_out, hid_buf, wg_buf, cache_buf, sems):
    part = PLEN * PASS_DEV // 4
    moves = []
    for n in range(4):
        span = pl.ds(n * part, part)
        moves.append((cache.at[span, :], cache_buf.at[span, :], cache_out.at[span, :]))
    moves += [(hid, hid_buf, hid_out), (wg, wg_buf, wg_out)]
    reads, writes = [], []
    for n, (src, mid, _) in enumerate(moves):
        reads.append(pltpu.make_async_copy(src, mid, sems.at[0, n]))
        reads[-1].start()
    for n, (_, mid, dst) in enumerate(moves):
        reads[n].wait()
        writes.append(pltpu.make_async_copy(mid, dst, sems.at[1, n]))
        writes[-1].start()
    for copy in writes:
        copy.wait()


VMEM = pl.BlockSpec(memory_space=pltpu.VMEM)
SMEM = pl.BlockSpec(memory_space=pltpu.SMEM)
ANY = pl.BlockSpec(memory_space=pl.ANY)


def call(kernel, collective_id, out_shape, in_specs, out_specs, scratch, args):
    return pl.pallas_call(
        kernel,
        out_shape=out_shape,
        in_specs=in_specs,
        out_specs=out_specs,
        scratch_shapes=scratch,
        compiler_params=pltpu.CompilerParams(
            collective_id=collective_id, has_side_effects=True, vmem_limit_bytes=56 * 2**20
        ),
    )(*args)


def shards(hidden, weight, cache, lengths, passage_ids, owner_map):
    width = hidden.shape[-1]
    share = width // OWNERS
    tokens = Q_DEV * QL
    shape = jax.ShapeDtypeStruct
    dma = pltpu.SemaphoreType.DMA
    vmem = pltpu.VMEM

    def pair(*sizes):
        return [dma(sizes), dma(sizes)]

    scratch = [
        vmem((tokens, width), BF16),
        vmem((PLEN, PASS_DEV, DIM), BF16),
        vmem((OWNERS, Q_DEV, QL, DIM), BF16),
        vmem((OWNERS, share, DIM), BF16),
        vmem((PASS_DEV, ROWS, DIM), BF16),
        vmem((OWNERS, 8, 128), I32),
        vmem((OWNERS, 128), I32),
        pltpu.SMEM((OWNERS, 128), I32),
        vmem((5, 8, 128), I32),
        pltpu.SMEM((5, 8, 128), I32),
        vmem((FLAT, DIM), F32),
        vmem((GROUPS, ROWS, 128), F32),
        vmem((64, 128), F32),
        vmem((64, 128), F32),
        vmem((64, 128), F32),
        vmem((OWNERS, 8, 128), F32),
        vmem((8, SLOTS), F32),
        pltpu.SMEM((8, SLOTS), F32),
        vmem((GROUPS + 1, ROWS, DIM), F32),
        vmem((GROUPS, 4, QL, DIM), F32),
        vmem((NZ, NC, tokens, DIM), BF16),
        vmem((FLAT, DIM), BF16),
        vmem((NX - 1, NY, A_ROWS, DIM), BF16),
        vmem((NY - 1, A_ROWS, DIM), BF16),
        vmem((NY - 1, B_PIECE, DIM), BF16),
        vmem((NX - 1, B_ROWS, DIM), BF16),
        vmem((NY, A_ROWS, DIM), BF16),
        vmem((B_PIECE, DIM), BF16),
        vmem((FLAT, DIM), BF16),
        vmem((NZ, tokens, DIM), BF16),
        vmem((NZ, tokens, DIM), BF16),
        vmem((NZ, tokens, DIM), BF16),
        vmem((NZ, NC, share, DIM), BF16),
        vmem((NZ, share, DIM), BF16),
        vmem((NZ, share, DIM), BF16),
        vmem((NZ, share, DIM), BF16),
        vmem((NX, share, DIM), BF16),
        vmem((NY, share, DIM), BF16),
        dma((2,)),
        dma((4,)),
        dma,
        dma((2,)),
    ]
    gather = [dma((2 * NZ - 1,)), dma((OWNERS,))]
    swap = lambda n: [dma((n - 1,)), dma((n,))]
    scratch += gather + gather + gather + swap(OWNERS)
    scratch += [dma, dma] + swap(NZ) + [dma, dma] + swap(NZ) + swap(NX) + swap(NY)
    scratch += pair(NX - 1, NY) + pair(NY - 1) + pair(NY - 1) + pair(NX - 1, NY)
    scratch += pair(NY - 1) + pair(NX - 1) + pair(NX - 1) + pair(NY - 1)

    hid, wg, cache_grad = call(
        pair_kernel,
        0,
        [
            shape((tokens, width), BF16),
            shape((share, DIM), F32),
            shape((PLEN * PASS_DEV, DIM), BF16),
        ],
        [ANY, VMEM, ANY, SMEM, SMEM, SMEM],
        [VMEM, VMEM, ANY],
        scratch,
        (
            hidden.reshape(tokens, width),
            weight,
            jnp.transpose(cache, (1, 0, 2)),
            lengths,
            passage_ids,
            owner_map,
        ),
    )
    hid, wg, cache_grad = pl.pallas_call(
        result_kernel,
        out_shape=[shape(x.shape, x.dtype) for x in (hid, wg, cache_grad)],
        in_specs=[ANY] * 3,
        out_specs=[ANY] * 3,
        scratch_shapes=[vmem(x.shape, x.dtype) for x in (hid, wg, cache_grad)] + [dma((2, 6))],
    )(hid, wg, cache_grad)
    cache_grad = jnp.transpose(cache_grad.reshape(PLEN, PASS_DEV, DIM), (1, 0, 2))
    return hid.reshape(Q_DEV, QL, width), wg, cache_grad


def solution(mesh):
    in_specs = (
        P(("dp", "passage"), None, None),
        P("passage", None),
        P("passage", None, None),
        P("passage"),
        P(("dp", "passage"), None),
        P(),
    )
    out_specs = (P(("dp", "passage"), None, None), P("passage", None), P("passage", None, None))
    return jax.shard_map(shards, mesh=mesh, in_specs=in_specs, out_specs=out_specs, check_vma=False)
```

```python
import functools
import math

import jax
import jax.numpy as jnp
from jax import lax
from jax.experimental import pallas as pl
from jax.experimental.pallas import tpu as pltpu
from jax.sharding import PartitionSpec as P

TAU = 0.1
EPS = 1e-06

NX, NY, NZ, NC = 4, 8, 8, 2
OWNERS = NZ * NC
Q_DEV, QL, CAND = 4, 32, 16
PASS_DEV, PLEN, ROWS = 16, 180, 192
DIM = 128
GROUPS = 60
UNROLL = 30
SLOTS = 256
CAP = 12
PAIRS = Q_DEV * CAND
NEG = -1e30

F32, BF16, I32 = jnp.float32, jnp.bfloat16, jnp.int32


def dot(a, b):
    return jnp.dot(a, b, preferred_element_type=F32)


def dot_nt(a, b):
    return lax.dot_general(a, b, (((1,), (1,)), ((), ())), preferred_element_type=F32)


def dot_tn(a, b):
    return lax.dot_general(a, b, (((0,), (0,)), ((), ())), preferred_element_type=F32)


def iota(shape, axis):
    return lax.broadcasted_iota(I32, shape, axis)


def ind(cond, dtype=F32):
    return jnp.where(cond, 1.0, 0.0).astype(dtype)


def pieces(x):
    a = x.astype(BF16)
    rest = x - a.astype(F32)
    b = rest.astype(BF16)
    return (a, b, (rest - b.astype(F32)).astype(BF16))


class Place:
    def __init__(self):
        self.me = lax.axis_index("passage")
        self.z, self.c = self.me >> 1, self.me & (NC - 1)
        self.sibling = self.z * NC + (1 - self.c)

    def ring(self, k):
        return ((self.z + k) & (NZ - 1)) * NC + self.c

    def ring_sibling(self, k):
        return ((self.z + k) & (NZ - 1)) * NC + (1 - self.c)


def remote(src, dst, send, recv, device):
    return pltpu.make_async_remote_copy(
        src_ref=src,
        dst_ref=dst,
        send_sem=send,
        recv_sem=recv,
        device_id=device,
        device_id_type=pl.DeviceIdType.MESH,
    )


NEAR = (1, 7, 2, 6, 3, 5, 4)


class Gather:
    def __init__(self, place, buf, send, recv):
        self.place, self.buf, self.send, self.recv = place, buf, send, recv
        self.sent, self.relayed = [], 0

    def copy(self, slot, n, peer):
        return remote(
            self.buf.at[slot], self.buf.at[slot], self.send.at[n], self.recv.at[slot],
            {"passage": peer},
        )

    def start(self):
        p = self.place
        for n, k in list(enumerate(NEAR))[::-1]:
            self.sent.append(self.copy(p.me, n, p.ring(k)))
            self.sent[-1].start()
        self.sent.append(self.copy(p.me, NZ - 1, p.sibling))
        self.sent[-1].start()

    def relay(self, upto):
        p = self.place
        for n in range(self.relayed, upto):
            forward = self.copy(p.ring(NEAR[n]), NZ + n, p.sibling)
            forward.wait_recv()
            forward.start()
            self.sent.append(forward)
        self.relayed = upto

    def finish(self):
        p = self.place
        self.relay(NZ - 1)
        self.copy(p.sibling, 0, p.sibling).wait_recv()
        for k in NEAR:
            self.copy(p.ring_sibling(k), 0, p.sibling).wait_recv()

    def drain(self):
        for copy in self.sent:
            copy.wait_send()


FAR = (4, 3, 5, 2, 6, 1, 7)
A_ROWS, B_ROWS = 80, 16
A_PIECE, B_PIECE = NY * A_ROWS, NX * B_ROWS
B_AT = NX * A_PIECE
FLAT = PASS_DEV * ROWS


def rows_at(start, count):
    return pl.ds(pl.multiple_of(start, 16), count)


class Swap:
    def __init__(self, n, at, device, send, recv):
        self.n, self.at, self.device, self.send, self.recv = n, at, device, send, recv

    def start(self, src_of, buf):
        self.buf, self.copies = buf, []
        far = sorted(range(1, self.n), key=lambda k: -min(k, self.n - k))
        for k in far:
            t = (self.at + k) & (self.n - 1)
            copy = remote(
                src_of(t), buf.at[self.at], self.send.at[k - 1], self.recv.at[self.at], self.device(t)
            )
            copy.start()
            self.copies.append(copy)

    def finish(self):
        for k in range(1, self.n):
            t = (self.at + k) & (self.n - 1)
            remote(
                self.buf.at[t], self.buf.at[t], self.send.at[0], self.recv.at[t], self.device(t)
            ).wait_recv()

    def drain(self):
        for copy in self.copies:
            copy.wait_send()


def pair_kernel(
    hidden_hbm, weight_ref, cache_hbm, len_ref, ids, owner_of,
    hid_ref, wg_ref, cache_out,
    hidden_ref, cache_ref, query_ref, full_ref, tiles, rows_buf, rows_vec, rows_tab,
    tab_vec, tab,
    cache_f, exps, probs, logs, recips,
    score_buf, grad_vec, grad_tab, cg_run, qg_group, qg_ref, cg_ref,
    ax_buf, ay_buf, by_buf, bx_buf, mid_a, mid_b, fin, q_sib, q_out, q_in, w_own, w_sib, w_out, w_in, w_x, w_y,
    in_sem, tab_sem, grad_sem, out_sem,
    w_send, w_recv, r_send, r_recv, q_send, q_recv, s_send, s_recv,
    qs_send, qs_recv, qz_send, qz_recv, ws_send, ws_recv, wz_send, wz_recv, wx_send, wx_recv, wy_send, wy_recv,
    a1_send, a1_recv, a2_send, a2_recv, a3_send, a3_recv, a4_send, a4_recv,
    b1_send, b1_recv, b2_send, b2_recv, b3_send, b3_recv, b4_send, b4_recv,
):
    place = Place()
    me, z, c = place.me, place.z, place.c
    dp = lax.axis_index("dp")
    ix, iy = dp >> 3, dp & (NY - 1)
    others = [(me + k) & (OWNERS - 1) for k in range(1, OWNERS)]
    to_x = lambda k: {"dp": ((ix + k) & (NX - 1)) * NY + iy}
    to_y = lambda k: {"dp": ix * NY + ((iy + k) & (NY - 1))}
    sibling = {"passage": place.sibling}
    similarity_scale = 1.0 / (TAU * math.sqrt(DIM))
    root_scale = 1.0 / math.sqrt(DIM)

    barrier = pltpu.get_barrier_semaphore()
    peers = [{"passage": d} for d in others]
    peers += [to_x(k) for k in range(1, NX)] + [to_y(k) for k in range(1, NY)]
    for device in peers:
        pl.semaphore_signal(barrier, inc=1, device_id=device, device_id_type=pl.DeviceIdType.MESH)
    hidden_in = pltpu.make_async_copy(hidden_hbm, hidden_ref, in_sem.at[0])
    cache_in = pltpu.make_async_copy(cache_hbm, cache_ref, in_sem.at[1])
    hidden_in.start()
    cache_in.start()

    def bounded(value, most):
        return jnp.minimum(jnp.maximum(value, 0), most)

    full_ref[me] = weight_ref[...]
    lane = iota((8, 128), 1)
    slot = iota((8, 128), 0) * 128 + lane
    mine = jnp.full((8, 128), -1, I32)
    listed = jnp.zeros((8, 128), I32)
    for n in range(PAIRS):
        row = owner_of[bounded(ids[n // CAND, n % CAND], OWNERS * PASS_DEV - 1)]
        same = (slot >> 4) == (row >> 4)
        mine = jnp.where(same & ((slot & 15) == listed), 256 * n + row, mine)
        listed = listed + jnp.where(same, 1, 0)
    rows_buf[me] = mine
    pl.semaphore_wait(barrier, len(peers))
    weights = Gather(place, full_ref, w_send, w_recv)
    weights.start()
    rows = Gather(place, rows_buf, r_send, r_recv)
    rows.start()

    cache_in.wait()
    cache_f[0 : PLEN * PASS_DEV, :] = cache_ref[...].reshape(PLEN * PASS_DEV, DIM).astype(F32)
    for r in range(PASS_DEV):
        tiles[r, ROWS - 16 : ROWS] = jnp.zeros((16, DIM), BF16)
        tiles[r, 0:PLEN] = cache_f[pl.ds(r, PLEN, stride=PASS_DEV), :].astype(BF16)
    logs[...] = jnp.zeros_like(logs)
    recips[...] = jnp.zeros_like(recips)

    weights.relay(NZ - 1)
    rows.finish()
    for d in range(OWNERS):
        rows_vec[d : d + 1, :] = rows_buf[d, pl.ds(me >> 3, 1), :]
    to_rows = pltpu.make_async_copy(rows_vec, rows_tab, tab_sem.at[0])
    to_rows.start()
    hidden_in.wait()
    weights.finish()
    raw = dot(hidden_ref[...], full_ref[...].reshape(-1, DIM))
    inverse = lax.rsqrt(jnp.mean(raw * raw, axis=-1, keepdims=True) + EPS)
    vectors = (raw * inverse).astype(BF16)
    query_ref[me] = vectors.reshape(Q_DEV, QL, DIM)
    queries = Gather(place, query_ref, q_send, q_recv)
    queries.start()

    to_rows.wait()
    first_row = PASS_DEV * me

    my_lane = 16 * (me & 7)

    def listed_pair(d, n):
        value = rows_tab[d, my_lane + n]
        row = jnp.where(value >= 0, (value & 255) - first_row, -1)
        return jnp.where(value >= 0, PAIRS * d + (value >> 8), -1), row

    deep = iota((PASS_DEV, 128), 0)

    def count_pairs(d, counts):
        for n in range(CAP):
            counts = counts + jnp.where(deep == listed_pair(d, n)[1], 1, 0)
        return counts

    counts = lax.fori_loop(0, OWNERS, count_pairs, jnp.zeros((PASS_DEV, 128), I32))
    group = slot & 63
    start = jnp.zeros((8, 128), I32)
    slot_row, slot_start, last = start, start, start - 1
    for r in range(PASS_DEV):
        number = jnp.broadcast_to(counts[r : r + 1, :], (8, 128))
        if r:
            slot_row = slot_row + jnp.where(group >= start, 1, 0)
            slot_start = jnp.where(group >= start, start, slot_start)
        start = start + ((number + 3) >> 2)
        last = jnp.where((lane == r) & (number > 0), start - 1, last)
    slot_rank = 4 * (group - slot_start) + (slot >> 6)

    def place_pairs(d, carry):
        seen, at_slot, at_entry = carry
        for n in range(CAP):
            pair, row = listed_pair(d, n)
            same = slot_row == row
            at_slot = jnp.where(same & (slot_rank == seen), pair, at_slot)
            seen = seen + jnp.where(same, 1, 0)
            at_entry = jnp.where((slot == 16 * d + n) & (pair >= 0), pair, at_entry)
        return seen, at_slot, at_entry

    none = jnp.full((8, 128), -1, I32)
    _, at_slot, at_entry = lax.fori_loop(
        0, OWNERS, place_pairs, (jnp.zeros((8, 128), I32), none, none - 1)
    )
    tab_vec[0] = at_slot
    tab_vec[1] = slot_row
    tab_vec[2] = at_entry
    tab_vec[3] = last
    to_tab = pltpu.make_async_copy(tab_vec.at[pl.ds(0, 4)], tab.at[pl.ds(0, 4)], tab_sem.at[1])
    to_tab.start()
    queries.finish()
    to_tab.wait()

    def row_of(g):
        return bounded(tab[1, 0, g], PASS_DEV - 1)

    def load_queries(g, scaled=False):
        parts = []
        for j in range(4):
            pair = tab[0, j // 2, 64 * (j % 2) + g]
            query = bounded(pair >> 4, OWNERS * Q_DEV - 1)
            part = query_ref[query >> 2, query & (Q_DEV - 1)]
            if scaled:
                part = (part.astype(F32) * grad_tab[0, 64 * j + g]).astype(BF16)
            parts.append(part)
        return jnp.concatenate(parts, axis=0)

    live = iota((ROWS, 128), 0)

    def forward(i, _):
        for u in range(UNROLL):
            g = UNROLL * i + u
            row = row_of(g)
            sims = dot_nt(tiles[row], load_queries(g)) * similarity_scale
            sims = jnp.where(live < len_ref[row], sims, NEG)
            top = jnp.max(sims, axis=0, keepdims=True)
            e = jnp.exp(sims - top)
            total = jnp.sum(e, axis=0, keepdims=True)
            exps[g] = e
            logs[pl.ds(g, 1), :] = top + jnp.log(total)
            recips[pl.ds(g, 1), :] = 1.0 / total
        return 0

    lax.fori_loop(0, GROUPS // UNROLL, forward, 0)

    of_place = iota((SLOTS, 128), 1) // QL == iota((SLOTS, 128), 0) // 64
    spread = jnp.where(of_place, jnp.concatenate([logs[...]] * 4, axis=0), 0.0)
    one8 = jnp.ones((8, 128), BF16)
    score_row = TAU * sum(dot_nt(one8, part) for part in pieces(spread))
    pair = jnp.concatenate([at_slot[0:1], at_slot[1:2]], axis=1)
    is_cand = ind((iota((CAND, SLOTS), 0) == (pair & (CAND - 1))) & (pair >= 0))
    lane_of = ((pair >> 6) << 3) + ((pair >> 4) & (Q_DEV - 1))
    hits = ind((iota((128, SLOTS), 0) == lane_of) & (pair >= 0), BF16)
    mine = sum(
        dot_nt((is_cand * part[0:1].astype(F32)).astype(BF16), hits) for part in pieces(score_row)
    )
    score_buf[me] = mine[0:8] + pltpu.roll(mine[8:16], 4, 1)
    score_swap = Swap(OWNERS, me, lambda t: {"passage": t}, s_send, s_recv)
    score_swap.start(lambda t: score_buf.at[me], score_buf)

    def place_entries(i, spots):
        for u in range(16):
            pair = tab[0, i >> 3, 16 * (i & 7) + u]
            spots = jnp.where(at_entry == pair, 64 * (i & 3) + (i >> 2) + 4 * u, spots)
        return spots

    tab_vec[4] = lax.fori_loop(0, SLOTS // 16, place_entries, jnp.zeros((8, 128), I32))
    to_spots = pltpu.make_async_copy(tab_vec.at[4], tab.at[4], tab_sem.at[2])
    to_spots.start()

    def products(i, _):
        for u in range(UNROLL):
            g = UNROLL * i + u
            w = (exps[g] * recips[pl.ds(g, 1), :]).astype(BF16)
            probs[g] = w
            qg_group[g] = dot_tn(w, tiles[row_of(g)]).reshape(4, QL, DIM)
        return 0

    lax.fori_loop(0, GROUPS // UNROLL, products, 0)

    score_swap.finish()
    scores = score_buf[0]
    for d in range(1, OWNERS):
        scores = scores + score_buf[d]
    low = lax.rem(lane, 8) < Q_DEV

    def both(x, op):
        return op(x, jnp.where(low, pltpu.roll(x, 124, 1), pltpu.roll(x, 4, 1)))

    top = both(jnp.broadcast_to(jnp.max(scores, axis=0, keepdims=True), (8, 128)), jnp.maximum)
    e = jnp.exp(scores - top)
    total = both(jnp.broadcast_to(jnp.sum(e, axis=0, keepdims=True), (8, 128)), jnp.add)
    grad = e / total - ind((iota((8, 128), 0) == 0) & low)
    grad = jnp.concatenate(
        [jnp.where(low, grad, 0.0), jnp.where(low, pltpu.roll(grad, 124, 1), 0.0)], axis=0
    )
    grad_row = is_cand * sum(dot(part, hits) for part in pieces(grad))
    grad_row = jnp.sum(grad_row, axis=0, keepdims=True)
    grad_vec[...] = jnp.broadcast_to(grad_row * root_scale, (8, SLOTS))
    grad_copy = pltpu.make_async_copy(grad_vec, grad_tab, grad_sem)
    grad_copy.start()
    to_spots.wait()
    grad_copy.wait()

    def sum_device(d, _):
        sums = [jnp.zeros((QL, DIM), F32) for _ in range(Q_DEV)]
        for n in range(CAP):
            sub, spot_lane = d >> 3, 16 * (d & 7) + n
            pair = tab[2, sub, spot_lane]
            at = bounded(tab[4, sub, spot_lane], 4 * GROUPS - 1)
            part = qg_group[at >> 2, at & 3]
            grad = grad_tab[0, 64 * (at & 3) + (at >> 2)]
            for q in range(Q_DEV):
                one = jnp.where((pair >= 0) & (((pair >> 4) & (Q_DEV - 1)) == q), grad, 0.0)
                sums[q] = sums[q] + part * one
        for q in range(Q_DEV):
            qg_ref[d >> 1, d & 1, q * QL : (q + 1) * QL, :] = sums[q].astype(BF16)
        return 0

    lax.fori_loop(0, OWNERS, sum_device, 0)
    q_pair = remote(qg_ref.at[:, 1 - c], q_sib, qs_send, qs_recv, sibling)
    q_pair.start()

    def cache_step(i, run):
        for u in range(UNROLL):
            g = UNROLL * i + u
            row = row_of(g)
            again = (row == row_of(jnp.maximum(g - 1, 0))) & (g > 0)
            cg_run[g + 1] = jnp.where(again, cg_run[g], 0.0) + dot(probs[g], load_queries(g, True))
        return run

    lax.fori_loop(0, 1, cache_step, 0)
    q_pair.wait_recv()
    for t in range(NZ):
        q_out[t] = (qg_ref[t, c].astype(F32) + q_sib[t].astype(F32)).astype(BF16)
    on_z = lambda t: {"passage": t * NC + c}
    q_swap = Swap(NZ, z, on_z, qz_send, qz_recv)
    q_swap.start(lambda t: q_out.at[t], q_in)
    lax.fori_loop(1, GROUPS // UNROLL, cache_step, 0)

    for r in range(PASS_DEV):
        last = tab[3, 0, r]
        value = jnp.where(last >= 0, cg_run[bounded(last, GROUPS - 1) + 1], 0.0)
        cache_f[pl.ds(r, ROWS, stride=PASS_DEV), :] = value
    cg_ref[B_AT:FLAT, :] = cache_f[B_AT:FLAT, :].astype(BF16)

    sent = []

    def push(src, dst, send, recv, device):
        copy = remote(src, dst, send, recv, device)
        copy.start()
        sent.append(copy)

    def await_recv(dst, send, recv):
        remote(dst, dst, send, recv, sibling).wait_recv()

    def y_at(k):
        return (iy + k) & (NY - 1)

    def x_at(k):
        return (ix + k) & (NX - 1)

    for k in FAR:
        src = cg_ref.at[rows_at(B_AT + y_at(k) * B_PIECE, B_PIECE), :]
        push(src, by_buf.at[k - 1], b1_send.at[k - 1], b1_recv.at[k - 1], to_y(k))
    for d in FAR + (0,):
        for k in (2, 1, 3):
            span = rows_at(x_at(k) * A_PIECE + y_at(d) * A_ROWS, A_ROWS)
            cg_ref[span, :] = cache_f[span, :].astype(BF16)
            src = cg_ref.at[span, :]
            push(src, ax_buf.at[k - 1, d], a1_send.at[k - 1, d], a1_recv.at[k - 1, d], to_x(k))

    q_swap.finish()
    query_gradient = q_out[z].astype(F32)
    for k in range(1, NZ):
        query_gradient = query_gradient + q_in[(z + k) & (NZ - 1)].astype(F32)
    inverse = lax.rsqrt(jnp.mean(raw * raw, axis=-1, keepdims=True) + EPS)
    mean_term = jnp.mean(query_gradient * raw, axis=-1, keepdims=True)
    raw_grad = (
        inverse * query_gradient - raw * (inverse * inverse * inverse) * mean_term
    ).astype(BF16)
    weight_part = dot_tn(hidden_ref[...], raw_grad)
    w_own[...] = weight_part.astype(BF16).reshape(w_own.shape)
    w_pair = remote(w_own.at[:, 1 - c], w_sib, ws_send, ws_recv, sibling)
    w_pair.start()

    def a_first(d):
        total = cache_f[rows_at(ix * A_PIECE + y_at(d) * A_ROWS, A_ROWS), :]
        for k in range(1, NX):
            await_recv(ax_buf.at[k - 1, d], a1_send.at[k - 1, d], a1_recv.at[k - 1, d])
            total = total + ax_buf[k - 1, d].astype(F32)
        mid_a[d] = total.astype(BF16)
        if d:
            push(mid_a.at[d], ay_buf.at[d - 1], a2_send.at[d - 1], a2_recv.at[d - 1], to_y(d))

    for d in FAR[:4]:
        a_first(d)
    w_pair.wait_recv()
    for t in range(NZ):
        w_out[t] = (w_own[t, c].astype(F32) + w_sib[t].astype(F32)).astype(BF16)
    w_swap = Swap(NZ, z, on_z, wz_send, wz_recv)
    w_swap.start(lambda t: w_out.at[t], w_in)
    for d in FAR[4:] + (0,):
        a_first(d)
    hid_ref[...] = dot_nt(raw_grad, full_ref[...].reshape(-1, DIM)).astype(BF16)

    total = cg_ref[rows_at(B_AT + iy * B_PIECE, B_PIECE), :].astype(F32)
    for k in range(1, NY):
        await_recv(by_buf.at[k - 1], b1_send.at[k - 1], b1_recv.at[k - 1])
        total = total + by_buf[k - 1].astype(F32)
    mid_b[...] = total.astype(BF16)
    for k in (2, 1, 3):
        src = mid_b.at[rows_at(x_at(k) * B_ROWS, B_ROWS), :]
        push(src, bx_buf.at[k - 1], b2_send.at[k - 1], b2_recv.at[k - 1], to_x(k))
    total = mid_a[0].astype(F32)
    for d in range(1, NY):
        await_recv(ay_buf.at[d - 1], a2_send.at[d - 1], a2_recv.at[d - 1])
        total = total + ay_buf[d - 1].astype(F32)
    a_span = lambda kx, ky: fin.at[rows_at(x_at(kx) * A_PIECE + y_at(ky) * A_ROWS, A_ROWS), :]
    fin[rows_at(ix * A_PIECE + iy * A_ROWS, A_ROWS), :] = total.astype(BF16)
    for d in FAR:
        push(a_span(0, 0), a_span(0, 0), a3_send.at[d - 1], a3_recv.at[d - 1], to_y(d))
    for k in (2, 1, 3):
        push(a_span(0, 0), a_span(0, 0), a4_send.at[k - 1, 0], a4_recv.at[k - 1, 0], to_x(k))

    total = mid_b[rows_at(ix * B_ROWS, B_ROWS), :].astype(F32)
    for k in range(1, NX):
        await_recv(bx_buf.at[k - 1], b2_send.at[k - 1], b2_recv.at[k - 1])
        total = total + bx_buf[k - 1].astype(F32)
    b_span = lambda kx, ky: fin.at[rows_at(B_AT + y_at(ky) * B_PIECE + x_at(kx) * B_ROWS, B_ROWS), :]
    fin[rows_at(B_AT + iy * B_PIECE + ix * B_ROWS, B_ROWS), :] = total.astype(BF16)
    for k in (2, 1, 3):
        push(b_span(0, 0), b_span(0, 0), b3_send.at[k - 1], b3_recv.at[k - 1], to_x(k))

    w_swap.finish()
    total = w_out[z].astype(F32)
    for k in range(1, NZ):
        total = total + w_in[(z + k) & (NZ - 1)].astype(F32)
    w_x[ix] = total.astype(BF16)
    x_swap = Swap(NX, ix, lambda t: {"dp": t * NY + iy}, wx_send, wx_recv)
    x_swap.start(lambda t: w_x.at[ix], w_x)

    for k in range(1, NX):
        await_recv(b_span(-k, 0), b3_send.at[k - 1], b3_recv.at[k - 1])
    b_line = lambda k: fin.at[rows_at(B_AT + y_at(k) * B_PIECE, B_PIECE), :]
    for d in FAR:
        push(b_line(0), b_line(0), b4_send.at[d - 1], b4_recv.at[d - 1], to_y(d))

    def a_forward(d):
        await_recv(a_span(0, -d), a3_send.at[d - 1], a3_recv.at[d - 1])
        for k in (2, 1, 3):
            push(a_span(0, -d), a_span(0, -d), a4_send.at[k - 1, d], a4_recv.at[k - 1, d], to_x(k))

    for d in NEAR[:4]:
        a_forward(d)
    x_swap.finish()
    total = w_x[0].astype(F32)
    for t in range(1, NX):
        total = total + w_x[t].astype(F32)
    w_y[iy] = total.astype(BF16)
    y_swap = Swap(NY, iy, lambda t: {"dp": ix * NY + t}, wy_send, wy_recv)
    y_swap.start(lambda t: w_y.at[iy], w_y)
    for d in NEAR[4:]:
        a_forward(d)

    for d in range(1, NY):
        await_recv(b_line(-d), b4_send.at[d - 1], b4_recv.at[d - 1])
    b_live = PLEN * PASS_DEV - B_AT
    b_out = pltpu.make_async_copy(
        fin.at[pl.ds(B_AT, b_live), :], cache_out.at[pl.ds(B_AT, b_live), :], out_sem.at[0]
    )
    b_out.start()
    for d in range(NY):
        for k in range(1, NX):
            await_recv(a_span(-k, -d), a4_send.at[k - 1, d], a4_recv.at[k - 1, d])
    a_out = pltpu.make_async_copy(
        fin.at[pl.ds(0, B_AT), :], cache_out.at[pl.ds(0, B_AT), :], out_sem.at[1]
    )
    a_out.start()
    y_swap.finish()
    total = w_y[0].astype(F32)
    for t in range(1, NY):
        total = total + w_y[t].astype(F32)
    wg_ref[...] = total

    q_pair.wait_send()
    w_pair.wait_send()
    for moved in (weights, rows, queries, score_swap, q_swap, w_swap, x_swap, y_swap):
        moved.drain()
    for copy in sent:
        copy.wait_send()
    b_out.wait()
    a_out.wait()


def result_kernel(hid, wg, cache, hid_out, wg_out, cache_out, hid_buf, wg_buf, cache_buf, sems):
    part = PLEN * PASS_DEV // 4
    moves = []
    for n in range(4):
        span = pl.ds(n * part, part)
        moves.append((cache.at[span, :], cache_buf.at[span, :], cache_out.at[span, :]))
    moves += [(hid, hid_buf, hid_out), (wg, wg_buf, wg_out)]
    reads, writes = [], []
    for n, (src, mid, _) in enumerate(moves):
        reads.append(pltpu.make_async_copy(src, mid, sems.at[0, n]))
        reads[-1].start()
    for n, (_, mid, dst) in enumerate(moves):
        reads[n].wait()
        writes.append(pltpu.make_async_copy(mid, dst, sems.at[1, n]))
        writes[-1].start()
    for copy in writes:
        copy.wait()


VMEM = pl.BlockSpec(memory_space=pltpu.VMEM)
SMEM = pl.BlockSpec(memory_space=pltpu.SMEM)
ANY = pl.BlockSpec(memory_space=pl.ANY)


def call(kernel, collective_id, out_shape, in_specs, out_specs, scratch, args):
    return pl.pallas_call(
        kernel,
        out_shape=out_shape,
        in_specs=in_specs,
        out_specs=out_specs,
        scratch_shapes=scratch,
        compiler_params=pltpu.CompilerParams(
            collective_id=collective_id, has_side_effects=True, vmem_limit_bytes=56 * 2**20
        ),
    )(*args)


def shards(hidden, weight, cache, lengths, passage_ids, owner_map):
    width = hidden.shape[-1]
    share = width // OWNERS
    tokens = Q_DEV * QL
    shape = jax.ShapeDtypeStruct
    dma = pltpu.SemaphoreType.DMA
    vmem = pltpu.VMEM

    def pair(*sizes):
        return [dma(sizes), dma(sizes)]

    scratch = [
        vmem((tokens, width), BF16),
        vmem((PLEN, PASS_DEV, DIM), BF16),
        vmem((OWNERS, Q_DEV, QL, DIM), BF16),
        vmem((OWNERS, share, DIM), BF16),
        vmem((PASS_DEV, ROWS, DIM), BF16),
        vmem((OWNERS, 8, 128), I32),
        vmem((OWNERS, 128), I32),
        pltpu.SMEM((OWNERS, 128), I32),
        vmem((5, 8, 128), I32),
        pltpu.SMEM((5, 8, 128), I32),
        vmem((FLAT, DIM), F32),
        vmem((GROUPS, ROWS, 128), F32),
        vmem((GROUPS, ROWS, 128), BF16),
        vmem((64, 128), F32),
        vmem((64, 128), F32),
        vmem((OWNERS, 8, 128), F32),
        vmem((8, SLOTS), F32),
        pltpu.SMEM((8, SLOTS), F32),
        vmem((GROUPS + 1, ROWS, DIM), F32),
        vmem((GROUPS, 4, QL, DIM), F32),
        vmem((NZ, NC, tokens, DIM), BF16),
        vmem((FLAT, DIM), BF16),
        vmem((NX - 1, NY, A_ROWS, DIM), BF16),
        vmem((NY - 1, A_ROWS, DIM), BF16),
        vmem((NY - 1, B_PIECE, DIM), BF16),
        vmem((NX - 1, B_ROWS, DIM), BF16),
        vmem((NY, A_ROWS, DIM), BF16),
        vmem((B_PIECE, DIM), BF16),
        vmem((FLAT, DIM), BF16),
        vmem((NZ, tokens, DIM), BF16),
        vmem((NZ, tokens, DIM), BF16),
        vmem((NZ, tokens, DIM), BF16),
        vmem((NZ, NC, share, DIM), BF16),
        vmem((NZ, share, DIM), BF16),
        vmem((NZ, share, DIM), BF16),
        vmem((NZ, share, DIM), BF16),
        vmem((NX, share, DIM), BF16),
        vmem((NY, share, DIM), BF16),
        dma((2,)),
        dma((4,)),
        dma,
        dma((2,)),
    ]
    gather = [dma((2 * NZ - 1,)), dma((OWNERS,))]
    swap = lambda n: [dma((n - 1,)), dma((n,))]
    scratch += gather + gather + gather + swap(OWNERS)
    scratch += [dma, dma] + swap(NZ) + [dma, dma] + swap(NZ) + swap(NX) + swap(NY)
    scratch += pair(NX - 1, NY) + pair(NY - 1) + pair(NY - 1) + pair(NX - 1, NY)
    scratch += pair(NY - 1) + pair(NX - 1) + pair(NX - 1) + pair(NY - 1)

    hid, wg, cache_grad = call(
        pair_kernel,
        0,
        [
            shape((tokens, width), BF16),
            shape((share, DIM), F32),
            shape((PLEN * PASS_DEV, DIM), BF16),
        ],
        [ANY, VMEM, ANY, SMEM, SMEM, SMEM],
        [VMEM, VMEM, ANY],
        scratch,
        (
            hidden.reshape(tokens, width),
            weight,
            jnp.transpose(cache, (1, 0, 2)),
            lengths,
            passage_ids,
            owner_map,
        ),
    )
    hid, wg, cache_grad = pl.pallas_call(
        result_kernel,
        out_shape=[shape(x.shape, x.dtype) for x in (hid, wg, cache_grad)],
        in_specs=[ANY] * 3,
        out_specs=[ANY] * 3,
        scratch_shapes=[vmem(x.shape, x.dtype) for x in (hid, wg, cache_grad)] + [dma((2, 6))],
    )(hid, wg, cache_grad)
    cache_grad = jnp.transpose(cache_grad.reshape(PLEN, PASS_DEV, DIM), (1, 0, 2))
    return hid.reshape(Q_DEV, QL, width), wg, cache_grad


def solution(mesh):
    in_specs = (
        P(("dp", "passage"), None, None),
        P("passage", None),
        P("passage", None, None),
        P("passage"),
        P(("dp", "passage"), None),
        P(),
    )
    out_specs = (P(("dp", "passage"), None, None), P("passage", None), P("passage", None, None))
    return jax.shard_map(shards, mesh=mesh, in_specs=in_specs, out_specs=out_specs, check_vma=False)
```
